32 devices in a mesh: dp: 16 (over z, x, core), expert: 2 (over y).
Axes of the slice: x: 2, y: 2, z: 4, core: 2. Of those that a mesh axis runs over, the one named last changes fastest.
Arguments:
- grad_out: bfloat16 [8192, 1024], P(('dp', 'expert')), may hold values from -1 to 1
- routes: int32 [8192, 6], P(('dp', 'expert')), may hold values from 0 to 63, all different within a row; in each aligned block of 256 rows (0 to 255, 256 to 511, ...) at most 48 rows name the same one
- route_weight: float32 [8192, 6], P(('dp', 'expert')), may hold values from 0.05 to 0.35
- example_ids: int32 [16, 512], P('dp', 'expert'), may hold values from 0 to 7, never falling along the last dimension, each value on 1 to 128 neighbouring positions
- example_weight: float32 [16, 8], P('dp'), may hold values from 0.5 to 50
- hidden: bfloat16 [16, 2, 2, 48, 704], P('dp', 'expert'), may hold values from -6 to 6
Outputs:
- expert_grads: float32 [704, 2, 1024], P('dp', 'expert')
The draws below stay inside these ranges and needn't reach their ends.
Inputs may be any that keep to these rules, and one draw needn't show every extreme that they name: `routes`: each row names 6 different experts; in the rows of one device no expert is named more than 48 times, a bound that some block reaches. `example_ids`: along a data group's tokens the numbers never fall; each of the 8 examples has from 1 to a quarter of 512 tokens, one exactly that many.
All inputs are finite; a program needn't handle non-finite values.
Results may differ from the reference program's by a relative error of at most 0.0011.
Values may be sent and summed in bfloat16 or wider, within the bound.
No kernel may reach another device: no remote copies, remote signals or barrier semaphores. Data moves between devices by JAX's collectives and lax.ppermute only.
A program may use at most 64 MiB of HBM per device.

```python
import math
import jax
import jax.numpy as jnp
import numpy as np
from jax import lax

EXPERTS = 64
TOP = 6
FF_WIN = 704
D_WIN = 1024
EXAMPLES = 8
TOK_DEV = 256
SOURCES = 2
EXP_FLIGHT = 2
GROUPS = 16
GROUP_TOK = 512
TOKENS = 8192
CAP = 48
N_DP = 16


def draw_grad_out(key, part):
    own_key, common_key = jax.random.split(jax.random.fold_in(key, 101), 2)
    own = jax.random.normal(own_key, (GROUPS, GROUP_TOK, D_WIN), jnp.float32)
    common = 0.7 * jax.random.normal(common_key, (GROUPS, 1, D_WIN), jnp.float32)
    values = own + common
    values = jnp.clip(values / math.sqrt(TOK_DEV), -1.0, 1.0)
    return values.reshape(TOKENS, D_WIN).astype(jnp.bfloat16)


def draw_hidden(key, part):
    own_key, common_key = jax.random.split(jax.random.fold_in(key, 202), 2)
    own = jax.random.normal(own_key, (GROUPS, EXP_FLIGHT, SOURCES, CAP, FF_WIN), jnp.float32)
    common = 0.7 * jax.random.normal(common_key, (GROUPS, EXP_FLIGHT, 1, 1, FF_WIN), jnp.float32)
    values = own + common
    return jnp.clip(values, -6.0, 6.0).astype(jnp.bfloat16)


def block_levels(key, extent, shards, least, top_value):
    factor_of = 1.0
    for axis_at, blocks in shards:
        heights = jax.random.uniform(jax.random.fold_in(jax.random.fold_in(key, 6), axis_at), (blocks,), jnp.float32, least / len(shards), top_value / len(shards))
        factor_of = factor_of * jnp.repeat(jnp.exp(heights), extent[axis_at] // blocks).reshape((-1,) + (1,) * (len(extent) - 1 - axis_at))
    return factor_of


def split_up(amount, total, most, skew):
    loads = [(1 << 20) // math.isqrt(grade ** skew) + 1 for grade in range(2, amount + 1)]
    spare, holding = total - most - (amount - 1), [1] * (amount - 1)
    while spare > 0:
        movable = [i for i in range(amount - 1) if holding[i] < most]
        pool, budget = sum([loads[i] for i in movable]), spare
        for i in movable:
            extra = min(most - holding[i], max(1, budget * loads[i] // pool), spare)
            holding[i] = holding[i] + extra
            spare = spare - extra
    return np.array([most] + holding)


def ragged_sizes(key, count, total, most, slope):
    if count == 2:
        one = jax.random.randint(key, (), max(1, total - most), min(most, total - 1) + 1)
        return jnp.stack([one, total - one])
    sizes = jnp.asarray(split_up(count, total, most, slope), jnp.int32)
    twos = (count - 1) // 2
    giver, sink = sizes[1:1 + 2 * twos:2], sizes[2:2 + 2 * twos:2]
    room = jnp.minimum(giver - 1, most - sink)
    passed = jax.random.randint(jax.random.fold_in(key, 1), (twos,), 0, 1 << 20) % (room + 1)
    sizes = sizes.at[1:1 + 2 * twos:2].set(giver - passed).at[2:2 + 2 * twos:2].set(sink + passed)
    return sizes[jax.random.permutation(jax.random.fold_in(key, 2), count)]


def deal_out(key, own, number, rows, count, top, reach, skew):
    order = jax.random.permutation(key, count)
    packed, usual = load_shares(count, rows * top, reach, skew, True), load_shares(count, rows * top, reach, skew, False)
    places = jnp.arange(count)

    def named(lengths, turn):
        used = int((lengths > 0).sum())
        fixed = max(1, used // 4)
        shifted = fixed + (places - fixed + turn * (used - fixed)) % max(1, count - fixed)
        return jnp.zeros((count,), jnp.int32).at[order[jnp.where(places < fixed, places, shifted)]].set(jnp.asarray(lengths, jnp.int32))

    lengths = jnp.where(number % 4 == 0, named(packed, number // 4), named(usual, number - number // 4 - 1))
    mixed = jax.random.permutation(jax.random.fold_in(own, 3), count)
    source_of, sink = mixed[0:count // 2 * 2:2], mixed[1:count // 2 * 2:2]
    margin = jnp.minimum(lengths[source_of] - 1, reach - lengths[sink]) // 2
    margin = jnp.where((source_of == order[0]) | (sink == order[0]) | (lengths[sink] == 0), 0, jnp.maximum(margin, 0))
    shifted = jax.random.randint(jax.random.fold_in(own, 4), (count // 2,), 0, 1 << 20) % (margin + 1)
    lengths = lengths.at[source_of].add(-shifted).at[sink].add(shifted)
    labels = jnp.searchsorted(jnp.cumsum(lengths), jnp.arange(rows * top), side="right").astype(jnp.int32)
    listing = labels.reshape(top, rows).T
    listing = listing[jax.random.permutation(jax.random.fold_in(own, 1), rows)]
    turn = jax.random.randint(jax.random.fold_in(own, 2), (rows, 1), 0, top)
    return jnp.take_along_axis(listing, (jnp.arange(top)[None, :] + turn) % top, axis=1)


def load_shares(number_of, total, limit, lean, full):
    portions = [(1 << 20) // math.isqrt(rank ** lean) + 1 for rank in range(1, number_of + 1)]
    largest = limit if full else min(limit, max(-(-total // number_of), total * portions[0] // sum(portions)))
    least = 1 if total - largest >= number_of - 1 else 0
    counts, rest = [largest] + [least] * (number_of - 1), total - largest - least * (number_of - 1)
    while rest > 0:
        free = [i for i in range(1, number_of) if counts[i] < largest] or [i for i in range(1, number_of) if counts[i] < limit]
        pool, left = sum([portions[i] for i in free]), rest
        for i in free:
            addition = min(limit - counts[i], max(1, left * portions[i] // pool), rest)
            counts[i] = counts[i] + addition
            rest = rest - addition
    return np.array(counts)


def setup_inputs(seed: int = 0) -> dict:
    key_of = jax.random.split(jax.random.key(seed), 7)
    grad_out = draw_grad_out(jax.random.fold_in(key_of[6], 71), 0)
    routes_keys = jax.random.split(jax.random.fold_in(key_of[1], 1), TOKENS // TOK_DEV)
    routes_turns = jax.random.permutation(jax.random.fold_in(key_of[1], 3), TOKENS // TOK_DEV)
    routes = jax.vmap(lambda own, number: deal_out(jax.random.fold_in(key_of[1], 2), own, number, TOK_DEV, EXPERTS, TOP, CAP, 2))(routes_keys, routes_turns).reshape((TOKENS, TOP))
    route_weight = jnp.clip(0.05 + 0.29999999 * jax.random.uniform(key_of[2], (TOKENS, TOP), jnp.float32) ** block_levels(key_of[2], (TOKENS, TOP), ((0, 32),), -0.2, 0.2), 0.05, 0.35)
    example_ids = jax.vmap(lambda own: jnp.searchsorted(jnp.cumsum(ragged_sizes(own, EXAMPLES, GROUP_TOK, GROUP_TOK // 4, 0)), jnp.arange(GROUP_TOK), side="right"))(jax.random.split(key_of[3], GROUPS)).reshape((GROUPS, GROUP_TOK)).astype(jnp.int32)
    example_weight = jnp.clip(jnp.exp(math.log(50.0) - 4.6051702 * jax.random.uniform(key_of[4], (GROUPS, EXAMPLES), jnp.float32) ** block_levels(key_of[4], (GROUPS, EXAMPLES), ((0, 16),), -0.2, 0.2)), 0.5, 50.0)
    hidden = draw_hidden(jax.random.fold_in(key_of[6], 71), 0)
    return dict(grad_out=grad_out, routes=routes, route_weight=route_weight, example_ids=example_ids, example_weight=example_weight, hidden=hidden)


def slot_layout(block_routes, expert_list, capacity):
    matches = (block_routes[..., None] == expert_list).astype(jnp.float32)
    routed = lax.optimization_barrier(jnp.sum(matches, axis=-2))
    ranking = jnp.cumsum(routed, axis=-2) - routed
    slot_index = jnp.arange(capacity).astype(jnp.float32)
    placed = routed[..., None] * (ranking[..., None] == slot_index).astype(jnp.float32)
    return (matches, placed)

def reference(grad_out, routes, route_weight, example_ids, example_weight, hidden):
    highest = lax.Precision.HIGHEST
    in_flight = jnp.arange(EXP_FLIGHT).astype(jnp.int32)
    example_index = jnp.arange(EXAMPLES).astype(jnp.int32)
    cot_groups = grad_out.reshape(N_DP, SOURCES, TOK_DEV, D_WIN)
    route_groups = routes.reshape(N_DP, SOURCES, TOK_DEV, TOP)
    weight_groups = route_weight.reshape(N_DP, SOURCES, TOK_DEV, TOP)
    id_groups = example_ids.reshape(N_DP, SOURCES, TOK_DEV)

    def per_group(running, group_data):
        cot_rows, route_rows, weight_rows, id_rows, loss_weights, acts_group = group_data
        matches, placed = slot_layout(route_rows, in_flight, CAP)
        membership = (id_rows[..., None] == example_index).astype(jnp.float32)
        token_weight = lax.optimization_barrier(jnp.sum(membership * loss_weights, axis=-1))
        token_scale = lax.optimization_barrier(jnp.sum(matches * weight_rows[..., None], axis=-2)) * token_weight[..., None]
        slot_rows = jnp.einsum('stec,std->escd', placed, cot_rows.astype(jnp.float32), precision=highest)
        slot_scale = jnp.transpose(lax.optimization_barrier(jnp.sum(placed * token_scale[..., None], axis=1)), (1, 0, 2))
        slot_cot = (slot_rows * slot_scale[..., None]).astype(jnp.bfloat16)
        cot_flat = slot_cot.reshape(EXP_FLIGHT, SOURCES * CAP, D_WIN).astype(jnp.float32)
        member = jnp.einsum('stec,stx->escx', placed, membership, precision=highest).reshape(EXP_FLIGHT, SOURCES * CAP, EXAMPLES)
        acts_flat = acts_group.reshape(EXP_FLIGHT, SOURCES * CAP, FF_WIN).astype(jnp.float32)
        gram_left = jnp.einsum('eif,ekf->eik', acts_flat, acts_flat, precision=highest)
        gram_right = jnp.einsum('eid,ekd->eik', cot_flat, cot_flat, precision=highest)
        spread = jnp.einsum('eik,ekx->eix', gram_left * gram_right, member, precision=highest)
        squares = lax.optimization_barrier(jnp.sum(spread * member, axis=(0, 1)))
        clip_factor = 1.0 / jnp.maximum(jnp.sqrt(squares / (FF_WIN * D_WIN)), 1.0)
        slot_weight = lax.optimization_barrier(jnp.sum(member * clip_factor, axis=-1)) / EXAMPLES
        scaled = (slot_weight[..., None] * cot_flat).astype(jnp.bfloat16).astype(jnp.float32)
        group_grads = jnp.einsum('eif,eid->fed', acts_flat, scaled, precision=highest)
        return (running + group_grads, None)
    summed_grads, unused_out = lax.scan(per_group, jnp.zeros((FF_WIN, EXP_FLIGHT, D_WIN), jnp.float32), (cot_groups, route_groups, weight_groups, id_groups, example_weight, hidden))
    return summed_grads
```

```python
import jax
import jax.numpy as jnp
from jax import lax
from jax.sharding import PartitionSpec as P

EXAMPLES = 8


def shards(grad_out, routes, route_weight, example_ids, example_weight, hidden):
    sources = lax.axis_size("expert")
    me = lax.axis_index("expert")
    n_dp = lax.axis_size("dp")
    rank = lax.axis_index("dp")
    far = 4
    near = n_dp // far
    tokens = grad_out.shape[0]
    width = grad_out.shape[1]
    cap = hidden.shape[3]
    ff = hidden.shape[4]
    rows = ff // n_dp
    pad_rows = -(-rows // 16) * 16
    ids = example_ids.reshape(tokens)
    example_index = jnp.arange(EXAMPLES, dtype=jnp.int32)
    experts = jnp.arange(sources, dtype=jnp.int32)

    routes_t = routes.T
    hits = (routes_t[None] == experts[:, None, None]).astype(jnp.float32)
    routed = jnp.sum(hits, axis=1)
    token_weight = jnp.sum(
        jnp.where(ids[None, :] == example_index[:, None], example_weight[0][:, None], 0.0), axis=0
    )
    scale = jnp.sum(hits * route_weight.T[None], axis=1) * token_weight[None]
    order = jnp.arange(tokens)
    before = (order[:, None] < order[None, :]).astype(jnp.bfloat16)
    ranking = jnp.dot(routed.astype(jnp.bfloat16), before, preferred_element_type=jnp.float32)
    slot = jnp.arange(cap).astype(jnp.float32)
    placed = jnp.where(ranking[:, None, :] == slot[None, :, None], routed[:, None, :], 0.0)
    slot_scale = jnp.sum(placed * scale[:, None, :], axis=2)
    slot_code = jnp.sum(placed * (ids + 1).astype(jnp.float32)[None, None, :], axis=2)
    slot_rows = jnp.einsum(
        "ect,td->ecd", placed.astype(jnp.bfloat16), grad_out, preferred_element_type=jnp.float32
    )
    outgoing = (slot_rows * slot_scale[:, :, None]).astype(jnp.bfloat16)

    own_rows = lax.dynamic_index_in_dim(outgoing, me, 0, keepdims=False)
    own_code = lax.dynamic_index_in_dim(slot_code, me, 0, keepdims=False)
    rest_rows, codes = [], [own_code]
    acts = [lax.dynamic_index_in_dim(hidden[0, 0], me, 0, keepdims=False)]
    for k in range(1, sources):
        there = (me - k + sources) % sources
        pairs = [(s, (s - k) % sources) for s in range(sources)]
        send = lax.dynamic_index_in_dim(outgoing, there, 0, keepdims=False)
        send_code = lax.dynamic_index_in_dim(slot_code, there, 0, keepdims=False)
        rest_rows.append(lax.ppermute(send, "expert", pairs))
        codes.append(lax.ppermute(send_code, "expert", pairs))
        acts.append(lax.dynamic_index_in_dim(hidden[0, 0], (me + k) % sources, 0, keepdims=False))
    rest = jnp.concatenate(rest_rows, axis=0)
    code = jnp.concatenate(codes, axis=0)
    acts = jnp.concatenate(acts, axis=0)

    mine = rank // near

    def over_far(array, k):
        pairs = [
            (a * near + b, ((a + k) % far) * near + b) for a in range(far) for b in range(near)
        ]
        return lax.ppermute(array, "dp", pairs)

    cuts = acts.reshape(sources * cap, far, near, rows).transpose(1, 2, 3, 0)
    cuts = jnp.pad(cuts, ((0, 0), (0, 0), (0, pad_rows - rows), (0, 0)))
    cuts = cuts.reshape(far, near * pad_rows, sources * cap)
    own_far, rest_far, cut_far = [own_rows], [rest], []
    for k in range(far):
        cut = lax.dynamic_index_in_dim(cuts, (mine + k) % far, 0, keepdims=False)
        cut_far.append(cut if k == 0 else over_far(cut, k))
    for k in range(1, far):
        own_far.append(over_far(own_rows, k))
    for k in range(1, far):
        rest_far.append(over_far(rest, k))

    cot = jnp.concatenate([own_rows, rest], axis=0)
    left = lax.dot_general(
        acts, acts, (((1,), (1,)), ((), ())), preferred_element_type=jnp.float32
    )
    right = lax.dot_general(cot, cot, (((1,), (1,)), ((), ())), preferred_element_type=jnp.float32)
    alike = code[:, None] == code[None, :]
    per_slot = jnp.sum(jnp.where(alike, left * right, 0.0), axis=1)
    member = (code[:, None] == (example_index + 1).astype(jnp.float32)[None]).astype(jnp.float32)
    squares = jnp.sum(per_slot[:, None] * member, axis=0)
    total = squares
    for k in range(1, sources):
        total = total + lax.ppermute(
            squares, "expert", [(s, (s - k) % sources) for s in range(sources)]
        )
    clip = 1.0 / jnp.maximum(jnp.sqrt(total / (ff * width)), 1.0)
    weight = jnp.sum(member * clip[None], axis=1) / EXAMPLES
    weights = [weight] + [over_far(weight, k) for k in range(1, far)]

    part = jnp.zeros((near * pad_rows, width), jnp.float32)
    for k in range(far):
        rows_k = jnp.concatenate([own_far[k], rest_far[k]], axis=0)
        scaled = (weights[k][:, None] * rows_k.astype(jnp.float32)).astype(jnp.bfloat16)
        part = part + jnp.dot(cut_far[k], scaled, preferred_element_type=jnp.float32)
    here = rank % near
    part = part.reshape(near, pad_rows, width)[:, :rows]
    left_over, bit = near, 1
    while left_over > 1:
        low = (here // bit) % 2
        part = part.reshape(left_over // 2, 2, rows, width)
        keep = lax.dynamic_index_in_dim(part, low, 1, keepdims=False)
        give = lax.dynamic_index_in_dim(part, 1 - low, 1, keepdims=False)
        pairs = [(i, i ^ bit) for i in range(n_dp)]
        part = keep + lax.ppermute(give, "dp", pairs)
        left_over, bit = left_over // 2, bit * 2
    return part.reshape(rows, 1, width)


def solution(mesh):
    placed = (
        P(("dp", "expert"), None),
        P(("dp", "expert"), None),
        P(("dp", "expert"), None),
        P("dp", "expert"),
        P("dp", None),
        P("dp", "expert", None, None, None),
    )
    return jax.shard_map(
        shards, mesh=mesh, in_specs=placed, out_specs=P("dp", "expert", None), check_vma=False
    )
```

```python
import jax
import jax.numpy as jnp
from jax import lax
from jax.experimental import pallas as pl
from jax.experimental.pallas import tpu as pltpu
from jax.sharding import PartitionSpec as P

EXAMPLES = 8
FAR = 4
LANES = 128
BF16 = jnp.bfloat16
F32 = jnp.float32


def iota(shape, axis):
    return lax.broadcasted_iota(jnp.int32, shape, axis)


def reversed_bits(p, count):
    return int(format(p, "b").zfill(count)[::-1], 2) if count else 0


def build(sources, cap, routes, weights, ids, loss, grad, own, own_code, *gives):
    me = lax.axis_index("expert")
    tokens, width = grad.shape
    token_ids = ids[...]
    token_weight = jnp.zeros((1, tokens), F32)
    for x in range(EXAMPLES):
        token_weight = jnp.where(token_ids == x, loss[0, x], token_weight)
    token_code = (token_ids + 1).astype(F32)
    hits, scales = [], []
    for k in range(sources):
        match = routes[...] == lax.rem(me + (sources - k), sources)
        hits.append(jnp.sum(jnp.where(match, 1.0, 0.0), axis=0, keepdims=True))
        scales.append(
            jnp.sum(jnp.where(match, weights[...], 0.0), axis=0, keepdims=True) * token_weight
        )
    pad = -(-sources // 8) * 8 - sources
    routed = jnp.concatenate(hits + [jnp.zeros((1, tokens), F32)] * pad, axis=0)
    before = (iota((tokens, tokens), 0) < iota((tokens, tokens), 1)).astype(F32).astype(BF16)
    ranking = jnp.dot(routed.astype(BF16), before, preferred_element_type=F32)
    slot = iota((cap, tokens), 0).astype(F32)
    for k in range(sources):
        placed = jnp.where(ranking[k : k + 1] == slot, hits[k], 0.0)
        slot_scale = jnp.sum(placed * scales[k], axis=1, keepdims=True)
        code = jnp.sum(placed * token_code, axis=1, keepdims=True)
        rows = jnp.dot(placed.astype(BF16), grad[...], preferred_element_type=F32)
        rows = (rows * slot_scale).astype(BF16)
        if k == 0:
            own[...] = rows
            own_code[...] = jnp.broadcast_to(code, (cap, LANES))
        else:
            gives[k - 1][:, :width] = rows
            gives[k - 1][:, width:] = jnp.broadcast_to(code, (cap, LANES)).astype(BF16)


def cut(sources, n_dp, pad, hidden, *outs):
    me, rank = lax.axis_index("expert"), lax.axis_index("dp")
    near = n_dp // FAR
    bits = near.bit_length() - 1
    ff = hidden.shape[2]
    rows = ff // n_dp
    mine, here = rank // near, lax.rem(rank, near)
    column = iota((1, near * pad), 1)
    wanted = jnp.full((1, near * pad), -ff, jnp.int32)
    for p in range(near):
        inside = (column >= p * pad) & (column < p * pad + rows)
        wanted = jnp.where(
            inside, (here ^ reversed_bits(p, bits)) * rows + column - p * pad, wanted
        )
    unit = iota((ff, near * pad), 0)
    acts = [hidden[lax.rem(me + j, sources)] for j in range(sources)]
    acts = jnp.concatenate(acts, axis=0)
    cap = hidden.shape[1]
    for k in range(FAR):
        pick = jnp.where(unit == wanted + (mine ^ k) * (near * rows), 1.0, 0.0).astype(BF16)
        units = jnp.dot(acts, pick, preferred_element_type=F32).astype(BF16)
        for j in range(sources):
            outs[k][:, j * near * pad : (j + 1) * near * pad] = units[j * cap : (j + 1) * cap]


def norms(sources, hidden, own, own_code, *refs):
    takes, squares = refs[: sources - 1], refs[sources - 1]
    me = lax.axis_index("expert")
    width = own.shape[1]
    acts = jnp.concatenate([hidden[lax.rem(me + j, sources)] for j in range(sources)], axis=0)
    cot = jnp.concatenate([own[...]] + [t[:, :width] for t in takes], axis=0)
    member = membership(own_code, takes, width)
    last = (((1,), (1,)), ((), ()))
    left = lax.dot_general(acts, acts, last, preferred_element_type=F32)
    right = lax.dot_general(cot, cot, last, preferred_element_type=F32)
    one_hot = member.astype(BF16)
    alike = lax.dot_general(one_hot, one_hot, last, preferred_element_type=F32)
    per_slot = jnp.sum(left * right * alike, axis=1, keepdims=True)
    squares[...] = jnp.sum(per_slot * member, axis=0, keepdims=True)


def membership(own_code, takes, width):
    code = jnp.concatenate(
        [own_code[...]] + [t[:, width:].astype(F32) for t in takes], axis=0
    )
    lane = iota(code.shape, 1).astype(F32)
    return jnp.where((code == lane) & (code > 0.0), 1.0, 0.0)


def scale(sources, ff, own_code, *refs):
    takes = refs[: sources - 1]
    squares = refs[sources - 1 : 2 * sources - 1]
    rest = refs[2 * sources - 1]
    cap = own_code.shape[0]
    width = takes[0].shape[1] - LANES
    total = squares[0][...]
    for s in squares[1:]:
        total = total + s[...]
    clip = 1.0 / jnp.maximum(jnp.sqrt(total / (ff * width)), 1.0)
    member = membership(own_code, takes, width)
    weight = jnp.sum(member * clip, axis=1, keepdims=True) / EXAMPLES
    for k in range(1, sources):
        part = slice((k - 1) * cap, k * cap)
        slot_weight = weight[k * cap : (k + 1) * cap]
        rest[part, :width] = (slot_weight * takes[k - 1][:, :width].astype(F32)).astype(BF16)
        if k > 1:
            rest[part, width:] = jnp.zeros((cap, LANES), BF16)
    weight = jnp.broadcast_to(weight[:cap], (cap, LANES))
    high = weight.astype(BF16).astype(F32)
    middle = (weight - high).astype(BF16).astype(F32)
    low = weight - high - middle
    lane = iota((cap, LANES), 1)
    three = jnp.where(lane == 0, high, jnp.where(lane == 1, middle, low))
    rest[:cap, width:] = three.astype(BF16)


def product(sources, rows, pad, *refs):
    owns, rests, cuts = refs[:FAR], refs[FAR : 2 * FAR], refs[2 * FAR : 3 * FAR]
    keep, give = refs[3 * FAR : 3 * FAR + 2]
    cots, units = refs[3 * FAR + 2 :]
    cap, width = owns[0].shape
    slots = sources * cap
    for k in range(FAR):
        three = rests[k][:cap, width:].astype(F32)
        weight = three[:, 0:1] + three[:, 1:2] + three[:, 2:3]
        cots[k * slots : k * slots + cap] = (weight * owns[k][...].astype(F32)).astype(BF16)
        cots[k * slots + cap : (k + 1) * slots] = rests[k][:, :width]
        across = units.shape[1]
        for j in range(sources):
            units[k * slots + j * cap : k * slots + (j + 1) * cap] = cuts[k][
                :, j * across : (j + 1) * across
            ]
    half = keep.shape[0]
    pieces = width // LANES
    part = lax.dot_general(
        units[...], cots[...], (((0,), (0,)), ((), ())), preferred_element_type=F32
    )
    for p in range(2 * half):
        out = keep if p < half else give
        for j in range(pieces):
            out[p % half, pl.ds(j, rows, stride=pieces), :] = part[
                p * pad : p * pad + rows, j * LANES : (j + 1) * LANES
            ]


def call(body, outs, args, scalars=(), scratch=(), flops=0):
    vmem = pl.BlockSpec(memory_space=pltpu.VMEM)
    smem = pl.BlockSpec(memory_space=pltpu.SMEM)
    moved = sum(a.size * a.dtype.itemsize for a in args) + sum(
        o.size * o.dtype.itemsize for o in outs
    )
    return pl.pallas_call(
        body,
        out_shape=tuple(outs),
        in_specs=[smem if i in scalars else vmem for i in range(len(args))],
        out_specs=tuple([vmem] * len(outs)),
        scratch_shapes=list(scratch),
        compiler_params=pltpu.CompilerParams(vmem_limit_bytes=32 * 1024 * 1024),
        cost_estimate=pl.CostEstimate(flops=flops, bytes_accessed=moved, transcendentals=0),
    )(*args)


def shards(grad_out, routes, route_weight, example_ids, example_weight, hidden):
    sources = lax.axis_size("expert")
    n_dp = lax.axis_size("dp")
    near = n_dp // FAR
    tokens, width = grad_out.shape
    cap, ff = hidden.shape[3], hidden.shape[4]
    rows = ff // n_dp
    pad = -(-rows // 16) * 16
    while near * pad * sources % LANES:
        pad += 16
    slots = sources * cap
    acts = hidden.reshape(sources, cap, ff)
    shape = jax.ShapeDtypeStruct

    def over_experts(array, k):
        return lax.ppermute(
            array, "expert", [(s, (s - k) % sources) for s in range(sources)]
        )

    def over_far(array, k):
        return lax.ppermute(array, "dp", [(i, i ^ (k * near)) for i in range(n_dp)])

    own, own_code, *gives = call(
        lambda *refs: build(sources, cap, *refs),
        [shape((cap, width), BF16), shape((cap, LANES), F32)]
        + [shape((cap, width + LANES), BF16)] * (sources - 1),
        (routes.T, route_weight.T, example_ids, example_weight, grad_out),
        scalars=(3,),
        flops=2 * slots * tokens * width,
    )
    takes = [over_experts(g, k + 1) for k, g in enumerate(gives)]
    owns = [own, over_far(own, 1), over_far(own, 2)]

    cuts = call(
        lambda *refs: cut(sources, n_dp, pad, *refs),
        [shape((cap, sources * near * pad), BF16)] * FAR,
        (acts,),
        flops=2 * slots * ff * near * pad * FAR,
    )
    cuts = [cuts[0]] + [over_far(cuts[k], k) for k in range(1, FAR)]
    owns.append(over_far(owns[2], 1))

    (squares,) = call(
        lambda *refs: norms(sources, *refs),
        [shape((1, LANES), F32)],
        (acts, own, own_code, *takes),
        flops=2 * slots * slots * (ff + width),
    )
    all_squares = [squares] + [over_experts(squares, k) for k in range(1, sources)]
    (rest,) = call(
        lambda *refs: scale(sources, ff, *refs),
        [shape((slots - cap, width + LANES), BF16)],
        (own_code, *takes, *all_squares),
        flops=slots * width,
    )
    rests = [rest, over_far(rest, 1), None, over_far(rest, 3)]
    rests[2] = over_far(rests[3], 1)

    keep, give = call(
        lambda *refs: product(sources, rows, pad, *refs),
        [shape((near // 2, rows * (width // LANES), LANES), F32)] * 2,
        (*owns, *rests, *cuts),
        scratch=(
            pltpu.VMEM((FAR * slots, width), BF16),
            pltpu.VMEM((FAR * slots, near * pad), BF16),
        ),
        flops=2 * FAR * slots * near * pad * width,
    )
    bit = 1
    while True:
        part = keep + lax.ppermute(give, "dp", [(i, i ^ bit) for i in range(n_dp)])
        half = part.shape[0] // 2
        if half == 0:
            break
        keep, give, bit = part[:half], part[half:], bit * 2
    return part.reshape(rows, 1, width)


def solution(mesh):
    placed = (
        P(("dp", "expert"), None),
        P(("dp", "expert"), None),
        P(("dp", "expert"), None),
        P("dp", "expert"),
        P("dp", None),
        P("dp", "expert", None, None, None),
    )
    return jax.shard_map(
        shards, mesh=mesh, in_specs=placed, out_specs=P("dp", "expert", None), check_vma=False
    )
```

```python
import jax
import jax.numpy as jnp
from jax import lax
from jax.experimental import pallas as pl
from jax.experimental.pallas import tpu as pltpu
from jax.sharding import PartitionSpec as P

EXAMPLES = 8
FAR = 4
LANES = 128
BF16 = jnp.bfloat16
F32 = jnp.float32


def iota(shape, axis):
    return lax.broadcasted_iota(jnp.int32, shape, axis)


def reversed_bits(p, count):
    return int(format(p, "b").zfill(count)[::-1], 2) if count else 0


def build(sources, cap, routes_at, weights_at, ids_at, loss_at, grad_at, own, own_code, *refs):
    gives = refs[: sources - 1]
    routes, weights, ids, loss, grad, sems = refs[sources - 1 :]
    fetches = [
        pltpu.make_async_copy(source, target, sems.at[i])
        for i, (source, target) in enumerate(
            [
                (routes_at, routes),
                (ids_at, ids),
                (loss_at, loss),
                (weights_at, weights),
                (grad_at, grad),
            ]
        )
    ]
    for fetch in fetches:
        fetch.start()
    me = lax.axis_index("expert")
    tokens, width = grad.shape
    before = (iota((tokens, tokens), 0) < iota((tokens, tokens), 1)).astype(F32).astype(BF16)
    slot = iota((cap, tokens), 0).astype(F32)
    fetches[0].wait()
    matches = [routes[...] == lax.rem(me + (sources - k), sources) for k in range(sources)]
    hits = [jnp.sum(jnp.where(m, 1.0, 0.0), axis=0, keepdims=True) for m in matches]
    pad = -(-sources // 8) * 8 - sources
    routed = jnp.concatenate(hits + [jnp.zeros((1, tokens), F32)] * pad, axis=0)
    ranking = jnp.dot(routed.astype(BF16), before, preferred_element_type=F32)
    for fetch in fetches[1:4]:
        fetch.wait()
    token_ids = ids[...]
    token_weight = jnp.zeros((1, tokens), F32)
    for x in range(EXAMPLES):
        token_weight = jnp.where(token_ids == x, loss[0, x], token_weight)
    token_code = (token_ids + 1).astype(F32)
    ready = []
    for k in range(sources):
        scale = jnp.sum(jnp.where(matches[k], weights[...], 0.0), axis=0, keepdims=True)
        scale = scale * token_weight
        placed = jnp.where(ranking[k : k + 1] == slot, hits[k], 0.0)
        slot_scale = jnp.sum(placed * scale, axis=1, keepdims=True)
        code = jnp.sum(placed * token_code, axis=1, keepdims=True)
        ready.append((placed.astype(BF16), slot_scale, code))
    fetches[4].wait()
    for k in range(sources):
        placed, slot_scale, code = ready[k]
        rows = jnp.dot(placed, grad[...], preferred_element_type=F32)
        rows = (rows * slot_scale).astype(BF16)
        if k == 0:
            own[...] = rows
            own_code[...] = jnp.broadcast_to(code, (cap, LANES))
        else:
            gives[k - 1][:, :width] = rows
            gives[k - 1][:, width:] = jnp.broadcast_to(code, (cap, LANES)).astype(BF16)


def cut(sources, n_dp, pad, hidden, *outs):
    me, rank = lax.axis_index("expert"), lax.axis_index("dp")
    near = n_dp // FAR
    bits = near.bit_length() - 1
    ff = hidden.shape[2]
    rows = ff // n_dp
    mine, here = rank // near, lax.rem(rank, near)
    column = iota((1, near * pad), 1)
    wanted = jnp.full((1, near * pad), -ff, jnp.int32)
    for p in range(near):
        inside = (column >= p * pad) & (column < p * pad + rows)
        wanted = jnp.where(
            inside, (here ^ reversed_bits(p, bits)) * rows + column - p * pad, wanted
        )
    unit = iota((ff, near * pad), 0)
    acts = [hidden[lax.rem(me + j, sources)] for j in range(sources)]
    acts = jnp.concatenate(acts, axis=0)
    for k in range(FAR):
        pick = jnp.where(unit == wanted + (mine ^ k) * (near * rows), 1.0, 0.0).astype(BF16)
        outs[k][...] = jnp.dot(acts, pick, preferred_element_type=F32).astype(BF16)


def meet(sources, hidden, own, own_code, turned, *refs):
    takes, cuts = refs[: sources - 1], refs[sources - 1 : sources - 1 + FAR]
    squares, outs = refs[-FAR - 1], refs[-FAR:]
    me = lax.axis_index("expert")
    cap, width = own.shape
    across = cuts[0].shape[1]
    acts = jnp.concatenate([hidden[lax.rem(me + j, sources)] for j in range(sources)], axis=0)
    cot = jnp.concatenate([own[...]] + [t[:, :width] for t in takes], axis=0)
    member = membership(own_code, takes, width)
    last = (((1,), (1,)), ((), ()))
    left = lax.dot_general(acts, acts, last, preferred_element_type=F32)
    right = lax.dot_general(cot, cot, last, preferred_element_type=F32)
    one_hot = member.astype(BF16)
    alike = lax.dot_general(one_hot, one_hot, last, preferred_element_type=F32)
    per_slot = jnp.sum(left * right * alike, axis=1, keepdims=True)
    squares[...] = jnp.sum(per_slot * member, axis=0, keepdims=True)
    for k in range(FAR):
        for j in range(1, sources):
            part = slice((j - 1) * cap, j * cap)
            outs[k][part, :width] = takes[j - 1][:, :width]
            outs[k][part, width : width + across] = cuts[k][j * cap : (j + 1) * cap]
            if j > 1:
                outs[k][part, width + across :] = jnp.zeros(
                    (cap, outs[k].shape[1] - width - across), BF16
                )
        outs[k][:cap, width + across : width + 2 * across] = cuts[k][:cap]
    outs[1][:cap, width + 2 * across : 2 * width + 2 * across] = own[...]
    outs[1][:cap, 2 * width + 2 * across :] = turned[...]


def membership(own_code, takes, width):
    code = jnp.concatenate(
        [own_code[...]] + [t[:, width:].astype(F32) for t in takes], axis=0
    )
    lane = iota(code.shape, 1).astype(F32)
    return jnp.where((code == lane) & (code > 0.0), 1.0, 0.0)


def weigh(sources, scale, own_code, *refs):
    takes = refs[: sources - 1]
    squares, out = refs[sources - 1 : -1], refs[-1]
    cap = own_code.shape[0]
    total = squares[0][...]
    for s in squares[1:]:
        total = total + s[...]
    clip = 1.0 / jnp.maximum(jnp.sqrt(total / scale), 1.0)
    member = membership(own_code, takes, takes[0].shape[1] - LANES)
    weight = jnp.sum(member * clip, axis=1, keepdims=True) / EXAMPLES
    diagonal = iota((cap, LANES), 0) == iota((cap, LANES), 1)
    for j in range(sources):
        here = jnp.where(diagonal, weight[j * cap : (j + 1) * cap], 0.0)
        out[j : j + 1] = jnp.sum(here, axis=0, keepdims=True)


def product(sources, rows, pad, *refs):
    straight, turned = refs[:2]
    rests, weights = refs[2 : 2 + FAR], refs[2 + FAR : 2 + 2 * FAR]
    keep, give, cots, units = refs[2 + 2 * FAR :]
    cap, width = straight.shape
    across = units.shape[1]
    first = width + 2 * across
    owns = [
        straight,
        rests[1].at[:cap, first : first + width],
        turned,
        rests[1].at[:cap, first + width :],
    ]
    slots = sources * cap
    diagonal = iota((cap, LANES), 0) == iota((cap, LANES), 1)
    for k in range(FAR):
        for j in range(sources):
            at = slice(k * slots + j * cap, k * slots + (j + 1) * cap)
            weight = jnp.where(diagonal, weights[k][j : j + 1], 0.0)
            weight = jnp.sum(weight, axis=1, keepdims=True)
            part = slice((j - 1) * cap, j * cap)
            cot = owns[k][...] if j == 0 else rests[k][part, :width]
            cots[at] = (weight * cot.astype(F32)).astype(BF16)
            if j == 0:
                units[at] = rests[k][:cap, width + across : width + 2 * across]
            else:
                units[at] = rests[k][part, width : width + across]
    half = keep.shape[0]
    pieces = width // LANES
    part = lax.dot_general(
        units[...], cots[...], (((0,), (0,)), ((), ())), preferred_element_type=F32
    )
    for p in range(2 * half):
        out = keep if p < half else give
        for j in range(pieces):
            out[p % half, pl.ds(j, rows, stride=pieces), :] = part[
                p * pad : p * pad + rows, j * LANES : (j + 1) * LANES
            ]


def call(body, outs, args, fetched=False, scratch=(), limit=32):
    vmem = pl.BlockSpec(memory_space=pltpu.VMEM)
    hbm = pl.BlockSpec(memory_space=pltpu.HBM)
    return pl.pallas_call(
        body,
        out_shape=tuple(outs),
        in_specs=[hbm if fetched else vmem] * len(args),
        out_specs=tuple([vmem] * len(outs)),
        scratch_shapes=list(scratch),
        compiler_params=pltpu.CompilerParams(vmem_limit_bytes=limit * 1024 * 1024),
        cost_estimate=pl.CostEstimate(flops=1, bytes_accessed=1, transcendentals=0),
    )(*args)


def shards(grad_out, routes, route_weight, example_ids, example_weight, hidden):
    sources = lax.axis_size("expert")
    n_dp = lax.axis_size("dp")
    near = n_dp // FAR
    tokens, width = grad_out.shape
    top = routes.shape[1]
    cap, ff = hidden.shape[3], hidden.shape[4]
    rows = ff // n_dp
    pad = -(-rows // 16) * 16
    while near * pad * 2 % LANES:
        pad += 16
    across = near * pad
    slots = sources * cap
    acts = hidden.reshape(sources, cap, ff)
    shape = jax.ShapeDtypeStruct

    def over_experts(array, k):
        return lax.ppermute(
            array, "expert", [(s, (s - k) % sources) for s in range(sources)]
        )

    def over_far(array, k):
        return lax.ppermute(array, "dp", [(i, i ^ (k * near)) for i in range(n_dp)])

    own, own_code, *gives = call(
        lambda *refs: build(sources, cap, *refs),
        [shape((cap, width), BF16), shape((cap, LANES), F32)]
        + [shape((cap, width + LANES), BF16)] * (sources - 1),
        (routes.T, route_weight.T, example_ids, example_weight, grad_out),
        fetched=True,
        limit=60,
        scratch=(
            pltpu.VMEM((top, tokens), jnp.int32),
            pltpu.VMEM((top, tokens), F32),
            pltpu.VMEM((1, tokens), jnp.int32),
            pltpu.SMEM((1, EXAMPLES), F32),
            pltpu.VMEM((tokens, width), BF16),
            pltpu.SemaphoreType.DMA((5,)),
        ),
    )
    takes = [over_experts(g, k + 1) for k, g in enumerate(gives)]
    turned = over_far(own, 2)

    cuts = call(
        lambda *refs: cut(sources, n_dp, pad, *refs),
        [shape((slots, across), BF16)] * FAR,
        (acts,),
    )
    squares, *rests = call(
        lambda *refs: meet(sources, *refs),
        [shape((1, LANES), F32)]
        + [
            shape((slots - cap, width + 2 * across + (2 * width if k == 1 else 0)), BF16)
            for k in range(FAR)
        ],
        (acts, own, own_code, turned, *takes, *cuts),
    )
    all_squares = [squares] + [over_experts(squares, k) for k in range(1, sources)]
    rests = [rests[0]] + [over_far(rests[k], k) for k in range(1, FAR)]
    (weight,) = call(
        lambda *refs: weigh(sources, ff * width, *refs),
        [shape((-(-sources // 8) * 8, LANES), F32)],
        (own_code, *takes, *all_squares),
    )
    weights = [weight] + [over_far(weight, k) for k in range(1, FAR)]

    keep, give = call(
        lambda *refs: product(sources, rows, pad, *refs),
        [shape((near // 2, rows * (width // LANES), LANES), F32)] * 2,
        (own, turned, *rests, *weights),
        scratch=(
            pltpu.VMEM((FAR * slots, width), BF16),
            pltpu.VMEM((FAR * slots, across), BF16),
        ),
    )
    bit = 1
    while True:
        part = keep + lax.ppermute(give, "dp", [(i, i ^ bit) for i in range(n_dp)])
        half = part.shape[0] // 2
        if half == 0:
            break
        keep, give, bit = part[:half], part[half:], bit * 2
    return part.reshape(rows, 1, width)


def solution(mesh):
    placed = (
        P(("dp", "expert"), None),
        P(("dp", "expert"), None),
        P(("dp", "expert"), None),
        P("dp", "expert"),
        P("dp", None),
        P("dp", "expert", None, None, None),
    )
    return jax.shard_map(
        shards, mesh=mesh, in_specs=placed, out_specs=P("dp", "expert", None), check_vma=False
    )
```

```python
import jax
import jax.numpy as jnp
from jax import lax
from jax.experimental import pallas as pl
from jax.experimental.pallas import tpu as pltpu
from jax.sharding import PartitionSpec as P

EXAMPLES = 8
FAR = 4
LANES = 128
BF16 = jnp.bfloat16
F32 = jnp.float32


def iota(shape, axis):
    return lax.broadcasted_iota(jnp.int32, shape, axis)


def reversed_bits(p, count):
    return int(format(p, "b").zfill(count)[::-1], 2) if count else 0


def build(sources, cap, n_dp, pad, routes_at, weights_at, ids_at, loss_at, grad_at, hidden_at, *refs):
    own, own_code, *gives = refs[: sources + 1]
    parcels = refs[sources + 1 : sources + 1 + FAR]
    routes, weights, ids, loss, grad, hidden, sems = refs[sources + 1 + FAR :]
    fetches = [
        pltpu.make_async_copy(source, target, sems.at[i])
        for i, (source, target) in enumerate(
            [
                (routes_at, routes),
                (ids_at, ids),
                (loss_at, loss),
                (weights_at, weights),
                (hidden_at, hidden),
                (grad_at, grad),
            ]
        )
    ]
    for fetch in fetches:
        fetch.start()
    me = lax.axis_index("expert")
    tokens, width = grad.shape
    before = (iota((tokens, tokens), 0) < iota((tokens, tokens), 1)).astype(F32).astype(BF16)
    slot = iota((cap, tokens), 0).astype(F32)
    fetches[0].wait()
    matches = [routes[...] == lax.rem(me + (sources - k), sources) for k in range(sources)]
    hits = [jnp.sum(jnp.where(m, 1.0, 0.0), axis=0, keepdims=True) for m in matches]
    blank = -(-sources // 8) * 8 - sources
    routed = jnp.concatenate(hits + [jnp.zeros((1, tokens), F32)] * blank, axis=0)
    ranking = jnp.dot(routed.astype(BF16), before, preferred_element_type=F32)
    for fetch in fetches[1:4]:
        fetch.wait()
    token_ids = ids[...]
    token_weight = jnp.zeros((1, tokens), F32)
    for x in range(EXAMPLES):
        token_weight = jnp.where(token_ids == x, loss[0, x], token_weight)
    token_code = (token_ids + 1).astype(F32)
    ready = []
    for k in range(sources):
        scale = jnp.sum(jnp.where(matches[k], weights[...], 0.0), axis=0, keepdims=True)
        scale = scale * token_weight
        placed = jnp.where(ranking[k : k + 1] == slot, hits[k], 0.0)
        slot_scale = jnp.sum(placed * scale, axis=1, keepdims=True)
        code = jnp.sum(placed * token_code, axis=1, keepdims=True)
        ready.append((placed.astype(BF16), slot_scale, code))
    fetches[4].wait()
    cut_hidden(sources, n_dp, pad, width, hidden, parcels)
    fetches[5].wait()
    for k in range(sources):
        placed, slot_scale, code = ready[k]
        rows = jnp.dot(placed, grad[...], preferred_element_type=F32)
        rows = (rows * slot_scale).astype(BF16)
        if k == 0:
            own[...] = rows
            own_code[...] = jnp.broadcast_to(code, (cap, LANES))
            parcels[1][:, :width] = rows
            parcels[2][:, :width] = rows
        else:
            gives[k - 1][:, :width] = rows
            gives[k - 1][:, width:] = jnp.broadcast_to(code, (cap, LANES)).astype(BF16)


def cut_hidden(sources, n_dp, pad, width, hidden, parcels):
    me, rank = lax.axis_index("expert"), lax.axis_index("dp")
    near = n_dp // FAR
    bits = near.bit_length() - 1
    cap, ff = hidden.shape[1:]
    rows = ff // n_dp
    mine, here = rank // near, lax.rem(rank, near)
    column = iota((1, near * pad), 1)
    wanted = jnp.full((1, near * pad), -ff, jnp.int32)
    for p in range(near):
        inside = (column >= p * pad) & (column < p * pad + rows)
        wanted = jnp.where(
            inside, (here ^ reversed_bits(p, bits)) * rows + column - p * pad, wanted
        )
    unit = iota((ff, near * pad), 0)
    acts = [hidden[lax.rem(me + j, sources)] for j in range(sources)]
    acts = jnp.concatenate(acts, axis=0)
    for k in range(FAR):
        pick = jnp.where(unit == wanted + (mine ^ k) * (near * rows), 1.0, 0.0).astype(BF16)
        units = jnp.dot(acts, pick, preferred_element_type=F32).astype(BF16)
        first = width if k in (1, 2) else 0
        for j in range(sources):
            at = slice(first + j * near * pad, first + (j + 1) * near * pad)
            parcels[k][:, at] = units[j * cap : (j + 1) * cap]


def norms(sources, hidden, own, own_code, *refs):
    takes, squares = refs[: sources - 1], refs[sources - 1]
    me = lax.axis_index("expert")
    width = own.shape[1]
    acts = jnp.concatenate([hidden[lax.rem(me + j, sources)] for j in range(sources)], axis=0)
    cot = jnp.concatenate([own[...]] + [t[:, :width] for t in takes], axis=0)
    member = membership(own_code, takes, width)
    last = (((1,), (1,)), ((), ()))
    left = lax.dot_general(acts, acts, last, preferred_element_type=F32)
    right = lax.dot_general(cot, cot, last, preferred_element_type=F32)
    one_hot = member.astype(BF16)
    alike = lax.dot_general(one_hot, one_hot, last, preferred_element_type=F32)
    per_slot = jnp.sum(left * right * alike, axis=1, keepdims=True)
    squares[...] = jnp.sum(per_slot * member, axis=0, keepdims=True)


def membership(own_code, takes, width):
    code = jnp.concatenate(
        [own_code[...]] + [t[:, width:].astype(F32) for t in takes], axis=0
    )
    lane = iota(code.shape, 1).astype(F32)
    return jnp.where((code == lane) & (code > 0.0), 1.0, 0.0)


def scale(sources, count, first, third, own_code, turned, *refs):
    takes, squares = refs[: sources - 1], refs[sources - 1 : 2 * sources - 1]
    rest, longer = refs[2 * sources - 1 :]
    cap = own_code.shape[0]
    width = takes[0].shape[1] - LANES
    total = squares[0][...]
    for s in squares[1:]:
        total = total + s[...]
    clip = 1.0 / jnp.maximum(jnp.sqrt(total / count), 1.0)
    member = membership(own_code, takes, width)
    weight = jnp.sum(member * clip, axis=1, keepdims=True) / EXAMPLES
    own_weight = jnp.broadcast_to(weight[:cap], (cap, LANES))
    high = own_weight.astype(BF16).astype(F32)
    middle = (own_weight - high).astype(BF16).astype(F32)
    low = own_weight - high - middle
    lane = iota((cap, LANES), 1)
    three = jnp.where(lane == 0, high, jnp.where(lane == 1, middle, low)).astype(BF16)
    for j in range(1, sources):
        part = slice((j - 1) * cap, j * cap)
        slot_weight = weight[j * cap : (j + 1) * cap]
        rows = (slot_weight * takes[j - 1][:, :width].astype(F32)).astype(BF16)
        for out in (rest, longer):
            out[part, :width] = rows
            out[part, width : width + LANES] = three
        longer[part, width + LANES :] = turned[:, :width]


def product(sources, rows, pad, *refs):
    own, cut, first, second, third, rest, longer, rest_second, rest_third = refs[:9]
    keep, give, cots, units = refs[9:]
    cap, width = own.shape
    across = units.shape[1]
    slots = sources * cap
    owns = [own, first.at[:, :width], second.at[:, :width], longer.at[:cap, width + LANES :]]
    cuts = [cut, first.at[:, width:], second.at[:, width:], third]
    rests = [rest, longer, rest_second, rest_third]
    for k in range(FAR):
        three = rests[k][:cap, width : width + LANES].astype(F32)
        weight = three[:, 0:1] + three[:, 1:2] + three[:, 2:3]
        at = k * slots
        cots[at : at + cap] = (weight * owns[k][...].astype(F32)).astype(BF16)
        cots[at + cap : at + slots] = rests[k][:, :width]
        for j in range(sources):
            units[at + j * cap : at + (j + 1) * cap] = cuts[k][:, j * across : (j + 1) * across]
    half = keep.shape[0]
    pieces = width // LANES
    part = lax.dot_general(
        units[...], cots[...], (((0,), (0,)), ((), ())), preferred_element_type=F32
    )
    for p in range(2 * half):
        out = keep if p < half else give
        for j in range(pieces):
            out[p % half, pl.ds(j, rows, stride=pieces), :] = part[
                p * pad : p * pad + rows, j * LANES : (j + 1) * LANES
            ]


def call(body, outs, args, fetched=(), scratch=(), limit=32):
    vmem = pl.BlockSpec(memory_space=pltpu.VMEM)
    anywhere = pl.BlockSpec(memory_space=pl.ANY)
    return pl.pallas_call(
        body,
        out_shape=tuple(outs),
        in_specs=[anywhere if i in fetched else vmem for i in range(len(args))],
        out_specs=tuple([vmem] * len(outs)),
        scratch_shapes=list(scratch),
        compiler_params=pltpu.CompilerParams(vmem_limit_bytes=limit * 1024 * 1024),
        cost_estimate=pl.CostEstimate(flops=1, bytes_accessed=1, transcendentals=0),
    )(*args)


def shards(grad_out, routes, route_weight, example_ids, example_weight, hidden):
    sources = lax.axis_size("expert")
    n_dp = lax.axis_size("dp")
    near = n_dp // FAR
    tokens, width = grad_out.shape
    top = routes.shape[1]
    cap, ff = hidden.shape[3], hidden.shape[4]
    rows = ff // n_dp
    pad = -(-rows // 16) * 16
    while near * pad * sources % LANES:
        pad += 16
    across = near * pad
    slots = sources * cap
    acts = hidden.reshape(sources, cap, ff)
    shape = jax.ShapeDtypeStruct

    def over_experts(array, k):
        return lax.ppermute(
            array, "expert", [(s, (s - k) % sources) for s in range(sources)]
        )

    def over_far(array, k):
        return lax.ppermute(array, "dp", [(i, i ^ (k * near)) for i in range(n_dp)])

    own, own_code, *made = call(
        lambda *refs: build(sources, cap, n_dp, pad, *refs),
        [shape((cap, width), BF16), shape((cap, LANES), F32)]
        + [shape((cap, width + LANES), BF16)] * (sources - 1)
        + [
            shape((cap, sources * across + (width if k in (1, 2) else 0)), BF16)
            for k in range(FAR)
        ],
        (routes.T, route_weight.T, example_ids, example_weight, grad_out, acts),
        fetched=range(6),
        limit=60,
        scratch=(
            pltpu.VMEM((top, tokens), jnp.int32),
            pltpu.VMEM((top, tokens), F32),
            pltpu.VMEM((1, tokens), jnp.int32),
            pltpu.SMEM((1, EXAMPLES), F32),
            pltpu.VMEM((tokens, width), BF16),
            pltpu.VMEM((sources, cap, ff), BF16),
            pltpu.SemaphoreType.DMA((6,)),
        ),
    )
    gives, (cut, *parcels) = made[: sources - 1], made[sources - 1 :]
    takes = [over_experts(g, k + 1) for k, g in enumerate(gives)]
    second = over_far(parcels[1], 2)
    first = over_far(parcels[0], 1)
    third = over_far(parcels[2], 3)

    (squares,) = call(
        lambda *refs: norms(sources, *refs),
        [shape((1, LANES), F32)],
        (acts, own, own_code, *takes),
    )
    all_squares = [squares] + [over_experts(squares, k) for k in range(1, sources)]
    rest, longer = call(
        lambda *refs: scale(sources, ff * width, *refs),
        [
            shape((slots - cap, width + LANES), BF16),
            shape((slots - cap, 2 * width + LANES), BF16),
        ],
        (first, third, own_code, second, *takes, *all_squares),
        fetched=(0, 1),
    )
    rests = [rest, over_far(longer, 1), over_far(rest, 2), over_far(rest, 3)]

    keep, give = call(
        lambda *refs: product(sources, rows, pad, *refs),
        [shape((near // 2, rows * (width // LANES), LANES), F32)] * 2,
        (own, cut, first, second, third, *rests),
        scratch=(
            pltpu.VMEM((FAR * slots, width), BF16),
            pltpu.VMEM((FAR * slots, across), BF16),
        ),
    )
    bit = 1
    while True:
        part = keep + lax.ppermute(give, "dp", [(i, i ^ bit) for i in range(n_dp)])
        half = part.shape[0] // 2
        if half == 0:
            break
        keep, give, bit = part[:half], part[half:], bit * 2
    return part.reshape(rows, 1, width)


def solution(mesh):
    placed = (
        P(("dp", "expert"), None),
        P(("dp", "expert"), None),
        P(("dp", "expert"), None),
        P("dp", "expert"),
        P("dp", None),
        P("dp", "expert", None, None, None),
    )
    return jax.shard_map(
        shards, mesh=mesh, in_specs=placed, out_specs=P("dp", "expert", None), check_vma=False
    )
```

```python
import jax
import jax.numpy as jnp
from jax import lax
from jax.experimental import pallas as pl
from jax.experimental.pallas import tpu as pltpu
from jax.sharding import PartitionSpec as P

EXAMPLES = 8
FAR = 4
LANES = 128
BF16 = jnp.bfloat16
F32 = jnp.float32


def iota(shape, axis):
    return lax.broadcasted_iota(jnp.int32, shape, axis)


def reversed_bits(p, count):
    return int(format(p, "b").zfill(count)[::-1], 2) if count else 0


def build(sources, cap, routes_at, weights_at, ids_at, loss_at, grad_at, own, own_code, *refs):
    gives = refs[: sources - 1]
    routes, weights, ids, loss, grad, sems = refs[sources - 1 :]
    fetches = [
        pltpu.make_async_copy(source, target, sems.at[i])
        for i, (source, target) in enumerate(
            [
                (routes_at, routes),
                (ids_at, ids),
                (loss_at, loss),
                (weights_at, weights),
                (grad_at, grad),
            ]
        )
    ]
    for fetch in fetches:
        fetch.start()
    me = lax.axis_index("expert")
    tokens, width = grad.shape
    before = (iota((tokens, tokens), 0) < iota((tokens, tokens), 1)).astype(F32).astype(BF16)
    slot = iota((cap, tokens), 0).astype(F32)
    fetches[0].wait()
    matches = [routes[...] == lax.rem(me + (sources - k), sources) for k in range(sources)]
    hits = [jnp.sum(jnp.where(m, 1.0, 0.0), axis=0, keepdims=True) for m in matches]
    blank = -(-sources // 8) * 8 - sources
    routed = jnp.concatenate(hits + [jnp.zeros((1, tokens), F32)] * blank, axis=0)
    ranking = jnp.dot(routed.astype(BF16), before, preferred_element_type=F32)
    for fetch in fetches[1:4]:
        fetch.wait()
    token_ids = ids[...]
    token_weight = jnp.zeros((1, tokens), F32)
    for x in range(EXAMPLES):
        token_weight = jnp.where(token_ids == x, loss[0, x], token_weight)
    token_code = (token_ids + 1).astype(F32)
    ready = []
    for k in range(sources):
        scale = jnp.sum(jnp.where(matches[k], weights[...], 0.0), axis=0, keepdims=True)
        scale = scale * token_weight
        placed = jnp.where(ranking[k : k + 1] == slot, hits[k], 0.0)
        slot_scale = jnp.sum(placed * scale, axis=1, keepdims=True)
        code = jnp.sum(placed * token_code, axis=1, keepdims=True)
        ready.append((placed.astype(BF16), slot_scale, code))
    fetches[4].wait()
    for k in range(sources):
        placed, slot_scale, code = ready[k]
        rows = jnp.dot(placed, grad[...], preferred_element_type=F32)
        rows = (rows * slot_scale).astype(BF16)
        if k == 0:
            own[...] = rows
            own_code[...] = jnp.broadcast_to(code, (cap, LANES))
        else:
            gives[k - 1][:, :width] = rows
            gives[k - 1][:, width:] = jnp.broadcast_to(code, (cap, LANES)).astype(BF16)


def early(sources, n_dp, pad, own_at, code_at, hidden_at, own, own_code, left, *refs):
    parcels, (hidden, sems) = refs[:FAR], refs[FAR:]
    fetches = [
        pltpu.make_async_copy(source, target, sems.at[i])
        for i, (source, target) in enumerate(
            [(hidden_at, hidden), (own_at, own), (code_at, own_code)]
        )
    ]
    for fetch in fetches:
        fetch.start()
    width = own.shape[1]
    me, rank = lax.axis_index("expert"), lax.axis_index("dp")
    near = n_dp // FAR
    bits = near.bit_length() - 1
    ff = hidden.shape[2]
    cap = hidden.shape[1]
    rows = ff // n_dp
    mine, here = rank // near, lax.rem(rank, near)
    column = iota((1, near * pad), 1)
    wanted = jnp.full((1, near * pad), -ff, jnp.int32)
    for p in range(near):
        inside = (column >= p * pad) & (column < p * pad + rows)
        wanted = jnp.where(
            inside, (here ^ reversed_bits(p, bits)) * rows + column - p * pad, wanted
        )
    unit = iota((ff, near * pad), 0)
    fetches[0].wait()
    acts = [hidden[lax.rem(me + j, sources)] for j in range(sources)]
    acts = jnp.concatenate(acts, axis=0)
    left[...] = lax.dot_general(
        acts, acts, (((1,), (1,)), ((), ())), preferred_element_type=F32
    )
    for k in range(FAR):
        pick = jnp.where(unit == wanted + (mine ^ k) * (near * rows), 1.0, 0.0).astype(BF16)
        units = jnp.dot(acts, pick, preferred_element_type=F32).astype(BF16)
        first = width if k in (1, 2) else 0
        for j in range(sources):
            at = slice(first + j * near * pad, first + (j + 1) * near * pad)
            parcels[k][:, at] = units[j * cap : (j + 1) * cap]
    fetches[1].wait()
    fetches[2].wait()
    for k in (1, 2):
        parcels[k][:, :width] = own[...]


def norms(sources, left, own, own_code, *refs):
    takes, squares = refs[: sources - 1], refs[sources - 1]
    width = own.shape[1]
    cot = jnp.concatenate([own[...]] + [t[:, :width] for t in takes], axis=0)
    member = membership(own_code, takes, width)
    last = (((1,), (1,)), ((), ()))
    right = lax.dot_general(cot, cot, last, preferred_element_type=F32)
    one_hot = member.astype(BF16)
    alike = lax.dot_general(one_hot, one_hot, last, preferred_element_type=F32)
    per_slot = jnp.sum(left[...] * right * alike, axis=1, keepdims=True)
    squares[...] = jnp.sum(per_slot * member, axis=0, keepdims=True)


def membership(own_code, takes, width):
    code = jnp.concatenate(
        [own_code[...]] + [t[:, width:].astype(F32) for t in takes], axis=0
    )
    lane = iota(code.shape, 1).astype(F32)
    return jnp.where((code == lane) & (code > 0.0), 1.0, 0.0)


def scale(sources, count, first, third, own_code, turned, *refs):
    takes, squares = refs[: sources - 1], refs[sources - 1 : 2 * sources - 1]
    rest, longer = refs[2 * sources - 1 :]
    cap = own_code.shape[0]
    width = takes[0].shape[1] - LANES
    total = squares[0][...]
    for s in squares[1:]:
        total = total + s[...]
    clip = 1.0 / jnp.maximum(jnp.sqrt(total / count), 1.0)
    member = membership(own_code, takes, width)
    weight = jnp.sum(member * clip, axis=1, keepdims=True) / EXAMPLES
    own_weight = jnp.broadcast_to(weight[:cap], (cap, LANES))
    high = own_weight.astype(BF16).astype(F32)
    middle = (own_weight - high).astype(BF16).astype(F32)
    low = own_weight - high - middle
    lane = iota((cap, LANES), 1)
    three = jnp.where(lane == 0, high, jnp.where(lane == 1, middle, low)).astype(BF16)
    for j in range(1, sources):
        part = slice((j - 1) * cap, j * cap)
        slot_weight = weight[j * cap : (j + 1) * cap]
        rows = (slot_weight * takes[j - 1][:, :width].astype(F32)).astype(BF16)
        for out in (rest, longer):
            out[part, :width] = rows
            out[part, width : width + LANES] = three
        longer[part, width + LANES :] = turned[:, :width]


def product(sources, rows, pad, *refs):
    own, cut, first, second, third, rest, longer, rest_second, rest_third = refs[:9]
    keep, give, cots, units = refs[9:]
    cap, width = own.shape
    across = units.shape[1]
    slots = sources * cap
    owns = [own, first.at[:, :width], second.at[:, :width], longer.at[:cap, width + LANES :]]
    cuts = [cut, first.at[:, width:], second.at[:, width:], third]
    rests = [rest, longer, rest_second, rest_third]
    for k in range(FAR):
        three = rests[k][:cap, width : width + LANES].astype(F32)
        weight = three[:, 0:1] + three[:, 1:2] + three[:, 2:3]
        at = k * slots
        cots[at : at + cap] = (weight * owns[k][...].astype(F32)).astype(BF16)
        cots[at + cap : at + slots] = rests[k][:, :width]
        for j in range(sources):
            units[at + j * cap : at + (j + 1) * cap] = cuts[k][:, j * across : (j + 1) * across]
    half = keep.shape[0]
    pieces = width // LANES
    part = lax.dot_general(
        units[...], cots[...], (((0,), (0,)), ((), ())), preferred_element_type=F32
    )
    for p in range(2 * half):
        out = keep if p < half else give
        for j in range(pieces):
            out[p % half, pl.ds(j, rows, stride=pieces), :] = part[
                p * pad : p * pad + rows, j * LANES : (j + 1) * LANES
            ]


def call(body, outs, args, fetched=(), scratch=(), limit=32, flops=1):
    vmem = pl.BlockSpec(memory_space=pltpu.VMEM)
    anywhere = pl.BlockSpec(memory_space=pl.ANY)
    return pl.pallas_call(
        body,
        out_shape=tuple(outs),
        in_specs=[anywhere if i in fetched else vmem for i in range(len(args))],
        out_specs=tuple([vmem] * len(outs)),
        scratch_shapes=list(scratch),
        compiler_params=pltpu.CompilerParams(vmem_limit_bytes=limit * 1024 * 1024),
        cost_estimate=pl.CostEstimate(flops=flops, bytes_accessed=1, transcendentals=0),
    )(*args)


def shards(grad_out, routes, route_weight, example_ids, example_weight, hidden):
    sources = lax.axis_size("expert")
    n_dp = lax.axis_size("dp")
    near = n_dp // FAR
    tokens, width = grad_out.shape
    top = routes.shape[1]
    cap, ff = hidden.shape[3], hidden.shape[4]
    rows = ff // n_dp
    pad = -(-rows // 16) * 16
    while near * pad * sources % LANES:
        pad += 16
    across = near * pad
    slots = sources * cap
    acts = hidden.reshape(sources, cap, ff)
    shape = jax.ShapeDtypeStruct

    def over_experts(array, k):
        return lax.ppermute(
            array, "expert", [(s, (s - k) % sources) for s in range(sources)]
        )

    def over_far(array, k):
        return lax.ppermute(array, "dp", [(i, i ^ (k * near)) for i in range(n_dp)])

    own_made, code_made, *gives = call(
        lambda *refs: build(sources, cap, *refs),
        [shape((cap, width), BF16), shape((cap, LANES), F32)]
        + [shape((cap, width + LANES), BF16)] * (sources - 1),
        (routes.T, route_weight.T, example_ids, example_weight, grad_out),
        fetched=range(5),
        limit=60,
        scratch=(
            pltpu.VMEM((top, tokens), jnp.int32),
            pltpu.VMEM((top, tokens), F32),
            pltpu.VMEM((1, tokens), jnp.int32),
            pltpu.SMEM((1, EXAMPLES), F32),
            pltpu.VMEM((tokens, width), BF16),
            pltpu.SemaphoreType.DMA((5,)),
        ),
    )
    takes = [over_experts(g, k + 1) for k, g in enumerate(gives)]
    own, own_code, left, cut, *parcels = call(
        lambda *refs: early(sources, n_dp, pad, *refs),
        [shape((cap, width), BF16), shape((cap, LANES), F32), shape((slots, slots), F32)]
        + [
            shape((cap, sources * across + (width if k in (1, 2) else 0)), BF16)
            for k in range(FAR)
        ],
        (own_made, code_made, acts),
        fetched=range(3),
        scratch=(pltpu.VMEM((sources, cap, ff), BF16), pltpu.SemaphoreType.DMA((3,))),
        flops=1 << 32,
    )
    second = over_far(parcels[1], 2)
    first = over_far(parcels[0], 1)
    third = over_far(parcels[2], 3)

    (squares,) = call(
        lambda *refs: norms(sources, *refs),
        [shape((1, LANES), F32)],
        (left, own, own_code, *takes),
        flops=1 << 32,
    )
    all_squares = [squares] + [over_experts(squares, k) for k in range(1, sources)]
    rest, longer = call(
        lambda *refs: scale(sources, ff * width, *refs),
        [
            shape((slots - cap, width + LANES), BF16),
            shape((slots - cap, 2 * width + LANES), BF16),
        ],
        (first, third, own_code, second, *takes, *all_squares),
        fetched=(0, 1),
    )
    rests = [rest, over_far(longer, 1), over_far(rest, 2), over_far(rest, 3)]

    keep, give = call(
        lambda *refs: product(sources, rows, pad, *refs),
        [shape((near // 2, rows * (width // LANES), LANES), F32)] * 2,
        (own, cut, first, second, third, *rests),
        scratch=(
            pltpu.VMEM((FAR * slots, width), BF16),
            pltpu.VMEM((FAR * slots, across), BF16),
        ),
    )
    bit = 1
    while True:
        part = keep + lax.ppermute(give, "dp", [(i, i ^ bit) for i in range(n_dp)])
        half = part.shape[0] // 2
        if half == 0:
            break
        keep, give, bit = part[:half], part[half:], bit * 2
    return part.reshape(rows, 1, width)


def solution(mesh):
    placed = (
        P(("dp", "expert"), None),
        P(("dp", "expert"), None),
        P(("dp", "expert"), None),
        P("dp", "expert"),
        P("dp", None),
        P("dp", "expert", None, None, None),
    )
    return jax.shard_map(
        shards, mesh=mesh, in_specs=placed, out_specs=P("dp", "expert", None), check_vma=False
    )
```

```python
import jax
import jax.numpy as jnp
from jax import lax
from jax.experimental import pallas as pl
from jax.experimental.pallas import tpu as pltpu
from jax.sharding import PartitionSpec as P

EXAMPLES = 8
MATES = 4
LANES = 128
BF16 = jnp.bfloat16
F32 = jnp.float32


def iota(shape, axis):
    return lax.broadcasted_iota(jnp.int32, shape, axis)


def build(sources, cap, n_dp, pad, routes_at, weights_at, ids_at, loss_at, grad_at, hidden_at, *refs):
    own, own_code, *gives = refs[: sources + 1]
    parcels = refs[sources + 1 : sources + 1 + MATES]
    routes, weights, ids, loss, grad, hidden, sems = refs[sources + 1 + MATES :]
    fetches = [
        pltpu.make_async_copy(source, target, sems.at[i])
        for i, (source, target) in enumerate(
            [
                (routes_at, routes),
                (ids_at, ids),
                (loss_at, loss),
                (weights_at, weights),
                (hidden_at, hidden),
                (grad_at, grad),
            ]
        )
    ]
    for fetch in fetches:
        fetch.start()
    me = lax.axis_index("expert")
    tokens, width = grad.shape
    before = (iota((tokens, tokens), 0) < iota((tokens, tokens), 1)).astype(F32).astype(BF16)
    slot = iota((cap, tokens), 0).astype(F32)
    fetches[0].wait()
    matches = [routes[...] == lax.rem(me + (sources - k), sources) for k in range(sources)]
    hits = [jnp.sum(jnp.where(m, 1.0, 0.0), axis=0, keepdims=True) for m in matches]
    blank = -(-sources // 8) * 8 - sources
    routed = jnp.concatenate(hits + [jnp.zeros((1, tokens), F32)] * blank, axis=0)
    ranking = jnp.dot(routed.astype(BF16), before, preferred_element_type=F32)
    for fetch in fetches[1:4]:
        fetch.wait()
    token_ids = ids[...]
    token_weight = jnp.zeros((1, tokens), F32)
    for x in range(EXAMPLES):
        token_weight = jnp.where(token_ids == x, loss[0, x], token_weight)
    token_code = (token_ids + 1).astype(F32)
    ready = []
    for k in range(sources):
        scale = jnp.sum(jnp.where(matches[k], weights[...], 0.0), axis=0, keepdims=True)
        scale = scale * token_weight
        placed = jnp.where(ranking[k : k + 1] == slot, hits[k], 0.0)
        slot_scale = jnp.sum(placed * scale, axis=1, keepdims=True)
        code = jnp.sum(placed * token_code, axis=1, keepdims=True)
        ready.append((placed.astype(BF16), slot_scale, code))
    fetches[4].wait()
    cut_hidden(sources, n_dp, pad, width, hidden, parcels)
    fetches[5].wait()
    for k in range(sources):
        placed, slot_scale, code = ready[k]
        rows = jnp.dot(placed, grad[...], preferred_element_type=F32)
        rows = (rows * slot_scale).astype(BF16)
        if k == 0:
            own[...] = rows
            own_code[...] = jnp.broadcast_to(code, (cap, LANES))
            for parcel in parcels[1:]:
                parcel[:, :width] = rows
        else:
            gives[k - 1][:, :width] = rows
            gives[k - 1][:, width:] = jnp.broadcast_to(code, (cap, LANES)).astype(BF16)


def cut_hidden(sources, n_dp, pad, width, hidden, parcels):
    me, rank = lax.axis_index("expert"), lax.axis_index("dp")
    spread = n_dp // MATES
    cap, ff = hidden.shape[1:]
    rows = ff // n_dp
    high, low = rank // MATES, lax.rem(rank, MATES)
    column = iota((1, spread * pad), 1)
    wanted = jnp.full((1, spread * pad), -2 * ff, jnp.int32)
    for p in range(spread):
        inside = (column >= p * pad) & (column < p * pad + rows)
        wanted = jnp.where(inside, (high ^ p) * (MATES * rows) + column - p * pad, wanted)
    unit = iota((ff, spread * pad), 0)
    acts = [hidden[lax.rem(me + j, sources)] for j in range(sources)]
    acts = jnp.concatenate(acts, axis=0)
    for k in range(MATES):
        pick = jnp.where(unit == wanted + (low ^ k) * rows, 1.0, 0.0).astype(BF16)
        units = jnp.dot(acts, pick, preferred_element_type=F32).astype(BF16)
        first = width if k else 0
        for j in range(sources):
            at = slice(first + j * spread * pad, first + (j + 1) * spread * pad)
            parcels[k][:, at] = units[j * cap : (j + 1) * cap]


def stage(sources, own_at, code_at, hidden_at, own, own_code, left, hidden, sems):
    fetches = [
        pltpu.make_async_copy(source, target, sems.at[i])
        for i, (source, target) in enumerate(
            [(hidden_at, hidden), (own_at, own), (code_at, own_code)]
        )
    ]
    for fetch in fetches:
        fetch.start()
    me = lax.axis_index("expert")
    fetches[0].wait()
    acts = jnp.concatenate([hidden[lax.rem(me + j, sources)] for j in range(sources)], axis=0)
    left[...] = lax.dot_general(
        acts, acts, (((1,), (1,)), ((), ())), preferred_element_type=F32
    )
    fetches[1].wait()
    fetches[2].wait()


def norms(sources, left, own, own_code, *refs):
    takes, squares = refs[: sources - 1], refs[sources - 1]
    width = own.shape[1]
    cot = jnp.concatenate([own[...]] + [t[:, :width] for t in takes], axis=0)
    member = membership(own_code, takes, width)
    last = (((1,), (1,)), ((), ()))
    right = lax.dot_general(cot, cot, last, preferred_element_type=F32)
    one_hot = member.astype(BF16)
    alike = lax.dot_general(one_hot, one_hot, last, preferred_element_type=F32)
    per_slot = jnp.sum(left[...] * right * alike, axis=1, keepdims=True)
    squares[...] = jnp.sum(per_slot * member, axis=0, keepdims=True)


def membership(own_code, takes, width):
    code = jnp.concatenate(
        [own_code[...]] + [t[:, width:].astype(F32) for t in takes], axis=0
    )
    lane = iota(code.shape, 1).astype(F32)
    return jnp.where((code == lane) & (code > 0.0), 1.0, 0.0)


def scale(sources, count, own_code, *refs):
    takes, squares, rest = refs[: sources - 1], refs[sources - 1 : -1], refs[-1]
    cap = own_code.shape[0]
    width = takes[0].shape[1] - LANES
    total = squares[0][...]
    for s in squares[1:]:
        total = total + s[...]
    clip = 1.0 / jnp.maximum(jnp.sqrt(total / count), 1.0)
    member = membership(own_code, takes, width)
    weight = jnp.sum(member * clip, axis=1, keepdims=True) / EXAMPLES
    own_weight = jnp.broadcast_to(weight[:cap], (cap, LANES))
    high = own_weight.astype(BF16).astype(F32)
    middle = (own_weight - high).astype(BF16).astype(F32)
    low = own_weight - high - middle
    lane = iota((cap, LANES), 1)
    three = jnp.where(lane == 0, high, jnp.where(lane == 1, middle, low)).astype(BF16)
    for j in range(1, sources):
        part = slice((j - 1) * cap, j * cap)
        slot_weight = weight[j * cap : (j + 1) * cap]
        rows = slot_weight * takes[j - 1][:, :width].astype(F32)
        rest[part, :width] = rows.astype(BF16)
        rest[part, width:] = three


def product(sources, rows, pad, *refs):
    own, cut, *parcels = refs[: MATES + 1]
    rests = refs[MATES + 1 : 2 * MATES + 1]
    keep, *leave, cots, units = refs[2 * MATES + 1 :]
    cap, width = own.shape
    across = units.shape[1]
    slots = sources * cap
    owns = [own] + [parcel.at[:, :width] for parcel in parcels]
    cuts = [cut] + [parcel.at[:, width:] for parcel in parcels]
    for k in range(MATES):
        three = rests[k][:cap, width:].astype(F32)
        weight = three[:, 0:1] + three[:, 1:2] + three[:, 2:3]
        at = k * slots
        cots[at : at + cap] = (weight * owns[k][...].astype(F32)).astype(BF16)
        cots[at + cap : at + slots] = rests[k][:, :width]
        for j in range(sources):
            units[at + j * cap : at + (j + 1) * cap] = cuts[k][:, j * across : (j + 1) * across]
    pieces = width // LANES
    part = lax.dot_general(
        units[...], cots[...], (((0,), (0,)), ((), ())), preferred_element_type=F32
    )
    for p, out in enumerate([keep] + leave):
        values = part[p * pad : p * pad + rows]
        if p:
            most = jnp.max(jnp.max(jnp.abs(values), axis=0, keepdims=True), axis=1, keepdims=True)
            exponent = jnp.ceil(jnp.log2(jnp.maximum(most, 2.0**-100)))
            values = values * jnp.exp2(-exponent)
            below = out.shape[0] - rows * pieces
            out[rows * pieces :] = jnp.broadcast_to(exponent, (below, LANES))
        for j in range(pieces):
            out[pl.ds(j, rows, stride=pieces), :] = values[:, j * LANES : (j + 1) * LANES]


def call(body, outs, args, fetched=(), scratch=(), limit=32, flops=1):
    vmem = pl.BlockSpec(memory_space=pltpu.VMEM)
    anywhere = pl.BlockSpec(memory_space=pl.ANY)
    return pl.pallas_call(
        body,
        out_shape=tuple(outs),
        in_specs=[anywhere if i in fetched else vmem for i in range(len(args))],
        out_specs=tuple([vmem] * len(outs)),
        scratch_shapes=list(scratch),
        compiler_params=pltpu.CompilerParams(vmem_limit_bytes=limit * 1024 * 1024),
        cost_estimate=pl.CostEstimate(flops=flops, bytes_accessed=1, transcendentals=0),
    )(*args)


def shards(grad_out, routes, route_weight, example_ids, example_weight, hidden):
    sources = lax.axis_size("expert")
    n_dp = lax.axis_size("dp")
    spread = n_dp // MATES
    tokens, width = grad_out.shape
    top = routes.shape[1]
    cap, ff = hidden.shape[3], hidden.shape[4]
    rows = ff // n_dp
    pad = -(-rows // 16) * 16
    while spread * pad * sources % LANES:
        pad += 16
    across = spread * pad
    slots = sources * cap
    acts = hidden.reshape(sources, cap, ff)
    shape = jax.ShapeDtypeStruct

    def over_experts(array, k):
        return lax.ppermute(
            array, "expert", [(s, (s - k) % sources) for s in range(sources)]
        )

    def over_dp(array, k):
        return lax.ppermute(array, "dp", [(i, i ^ k) for i in range(n_dp)])

    own_made, code_made, *made = call(
        lambda *refs: build(sources, cap, n_dp, pad, *refs),
        [shape((cap, width), BF16), shape((cap, LANES), F32)]
        + [shape((cap, width + LANES), BF16)] * (sources - 1)
        + [
            shape((cap, sources * across + (width if k else 0)), BF16) for k in range(MATES)
        ],
        (routes.T, route_weight.T, example_ids, example_weight, grad_out, acts),
        fetched=range(6),
        limit=60,
        scratch=(
            pltpu.VMEM((top, tokens), jnp.int32),
            pltpu.VMEM((top, tokens), F32),
            pltpu.VMEM((1, tokens), jnp.int32),
            pltpu.SMEM((1, EXAMPLES), F32),
            pltpu.VMEM((tokens, width), BF16),
            pltpu.VMEM((sources, cap, ff), BF16),
            pltpu.SemaphoreType.DMA((6,)),
        ),
    )
    gives, (cut, *parcels) = made[: sources - 1], made[sources - 1 :]
    takes = [over_experts(g, k + 1) for k, g in enumerate(gives)]
    parcels = [over_dp(parcel, k + 1) for k, parcel in enumerate(parcels)]
    own, own_code, left = call(
        lambda *refs: stage(sources, *refs),
        [shape((cap, width), BF16), shape((cap, LANES), F32), shape((slots, slots), F32)],
        (own_made, code_made, acts),
        fetched=range(3),
        scratch=(pltpu.VMEM((sources, cap, ff), BF16), pltpu.SemaphoreType.DMA((3,))),
        flops=1 << 32,
    )
    (squares,) = call(
        lambda *refs: norms(sources, *refs),
        [shape((1, LANES), F32)],
        (left, own, own_code, *takes),
        flops=1 << 32,
    )
    all_squares = [squares] + [over_experts(squares, k) for k in range(1, sources)]
    (rest,) = call(
        lambda *refs: scale(sources, ff * width, *refs),
        [shape((slots - cap, width + LANES), BF16)],
        (own_code, *takes, *all_squares),
    )
    rests = [rest] + [over_dp(rest, k) for k in range(1, MATES)]

    held = rows * (width // LANES)
    sent = -(-(held + 8) // 16) * 16
    part, *leave = call(
        lambda *refs: product(sources, rows, pad, *refs),
        [shape((held if p == 0 else sent, LANES), F32) for p in range(spread)],
        (own, cut, *parcels, *rests),
        scratch=(
            pltpu.VMEM((MATES * slots, width), BF16),
            pltpu.VMEM((MATES * slots, across), BF16),
        ),
    )
    for p in range(1, spread):
        got = over_dp(leave[p - 1].astype(jnp.float16), p * MATES).astype(F32)
        part = part + got[:held] * jnp.exp2(got[held : held + 1])
    return part.reshape(rows, 1, width)


def solution(mesh):
    placed = (
        P(("dp", "expert"), None),
        P(("dp", "expert"), None),
        P(("dp", "expert"), None),
        P("dp", "expert"),
        P("dp", None),
        P("dp", "expert", None, None, None),
    )
    return jax.shard_map(
        shards, mesh=mesh, in_specs=placed, out_specs=P("dp", "expert", None), check_vma=False
    )
```

```python
import jax
import jax.numpy as jnp
from jax import lax
from jax.experimental import pallas as pl
from jax.experimental.pallas import tpu as pltpu
from jax.sharding import PartitionSpec as P

EXAMPLES = 8
MATES = 4
LANES = 128
BF16 = jnp.bfloat16
F32 = jnp.float32


def iota(shape, axis):
    return lax.broadcasted_iota(jnp.int32, shape, axis)


def build(sources, cap, n_dp, pad, routes_at, weights_at, ids_at, loss_at, grad_at, hidden_at, *refs):
    blocks, parcels = refs[:sources], refs[sources : sources + MATES]
    routes, weights, ids, loss, grad, hidden, sems = refs[sources + MATES :]
    spare = grad_at.shape[1] + hidden_at.shape[2] // n_dp
    fetches = [
        pltpu.make_async_copy(source, target, sems.at[i])
        for i, (source, target) in enumerate(
            [
                (routes_at, routes),
                (ids_at, ids),
                (loss_at, loss),
                (weights_at, weights),
                (hidden_at, hidden),
                (grad_at, grad),
            ]
        )
    ]
    for fetch in fetches:
        fetch.start()
    me = lax.axis_index("expert")
    tokens, width = grad.shape
    before = (iota((tokens, tokens), 0) < iota((tokens, tokens), 1)).astype(F32).astype(BF16)
    slot = iota((cap, tokens), 0).astype(F32)
    fetches[0].wait()
    matches = [routes[...] == lax.rem(me + (sources - k), sources) for k in range(sources)]
    hits = [jnp.sum(jnp.where(m, 1.0, 0.0), axis=0, keepdims=True) for m in matches]
    blank = -(-sources // 8) * 8 - sources
    routed = jnp.concatenate(hits + [jnp.zeros((1, tokens), F32)] * blank, axis=0)
    ranking = jnp.dot(routed.astype(BF16), before, preferred_element_type=F32)
    for fetch in fetches[1:4]:
        fetch.wait()
    token_ids = ids[...]
    token_weight = jnp.zeros((1, tokens), F32)
    for x in range(EXAMPLES):
        token_weight = jnp.where(token_ids == x, loss[0, x], token_weight)
    token_code = (token_ids + 1).astype(F32)
    ready = []
    for k in range(sources):
        scale = jnp.sum(jnp.where(matches[k], weights[...], 0.0), axis=0, keepdims=True)
        scale = scale * token_weight
        placed = jnp.where(ranking[k : k + 1] == slot, hits[k], 0.0)
        slot_scale = jnp.sum(placed * scale, axis=1, keepdims=True)
        code = jnp.sum(placed * token_code, axis=1, keepdims=True)
        ready.append((placed.astype(BF16), slot_scale, code))
    fetches[4].wait()
    cut_hidden(sources, n_dp, pad, width, hidden, parcels)
    fetches[5].wait()
    for k in range(sources):
        placed, slot_scale, code = ready[k]
        rows = jnp.dot(placed, grad[...], preferred_element_type=F32)
        rows = (rows * slot_scale).astype(BF16)
        blocks[k][:, :width] = rows
        blocks[k][:, width:] = jnp.broadcast_to(code, (cap, LANES)).astype(BF16)
        if k == 0:
            parcels[2][:, :width] = rows
            parcels[2][:, spare : spare + 1] = code.astype(BF16)


def cut_hidden(sources, n_dp, pad, width, hidden, parcels):
    me, rank = lax.axis_index("expert"), lax.axis_index("dp")
    spread = n_dp // MATES
    cap, ff = hidden.shape[1:]
    rows = ff // n_dp
    high, low = rank // MATES, lax.rem(rank, MATES)
    column = iota((1, spread * pad), 1)
    wanted = jnp.full((1, spread * pad), -2 * ff, jnp.int32)
    for p in range(spread):
        inside = (column >= p * pad) & (column < p * pad + rows)
        wanted = jnp.where(inside, (high ^ p) * (MATES * rows) + column - p * pad, wanted)
    unit = iota((ff, spread * pad), 0)
    acts = [hidden[lax.rem(me + j, sources)] for j in range(sources)]
    acts = jnp.concatenate(acts, axis=0)
    for k in range(MATES):
        pick = jnp.where(unit == wanted + (low ^ k) * rows, 1.0, 0.0).astype(BF16)
        units = jnp.dot(acts, pick, preferred_element_type=F32).astype(BF16)
        first = width if k == 2 else 0
        for j in range(sources):
            at = slice(first + j * spread * pad, first + (j + 1) * spread * pad)
            parcels[k][:, at] = units[j * cap : (j + 1) * cap]


def stage(sources, block, hidden, own, left):
    me = lax.axis_index("expert")
    acts = jnp.concatenate([hidden[lax.rem(me + j, sources)] for j in range(sources)], axis=0)
    left[...] = lax.dot_general(
        acts, acts, (((1,), (1,)), ((), ())), preferred_element_type=F32
    )
    own[...] = block[...]


def chosen(codes):
    lane = iota(codes.shape, 1).astype(F32)
    return (codes == lane) & (codes > 0.0)


def norms(sources, left, own, *refs):
    takes, squares, rest = refs[: sources - 1], refs[-2], refs[-1]
    cap, width = own.shape[0], own.shape[1] - LANES
    blocks = jnp.concatenate([own[...]] + [t[...] for t in takes], axis=0)
    rest[...] = blocks[cap:]
    cot = blocks[:, :width]
    member = jnp.where(chosen(blocks[:, width:].astype(F32)), 1.0, 0.0)
    last = (((1,), (1,)), ((), ()))
    right = lax.dot_general(cot, cot, last, preferred_element_type=F32)
    one_hot = member.astype(BF16)
    alike = lax.dot_general(one_hot, one_hot, last, preferred_element_type=F32)
    per_slot = jnp.sum(left[...] * right * alike, axis=1, keepdims=True)
    squares[...] = jnp.sum(per_slot * member, axis=0, keepdims=True)


def pack(rows, own, rest, across, rest_across, clip, clip_across, out):
    cap, width = own.shape[0], own.shape[1] - LANES
    own_codes = own[:, width:].astype(F32)
    across_codes = across[:, width + rows : width + rows + 1].astype(F32)
    across_codes = jnp.broadcast_to(across_codes, (cap, LANES))
    at = 0
    for block, codes, factors in (
        (own, own_codes, clip),
        (rest, rest[:, width:].astype(F32), clip),
        (across, across_codes, clip_across),
        (rest_across, rest_across[:, width:].astype(F32), clip_across),
    ):
        weight = jnp.sum(jnp.where(chosen(codes), factors[...], 0.0), axis=1, keepdims=True)
        weight = weight / EXAMPLES
        scaled = (weight * block[:, :width].astype(F32)).astype(BF16)
        out[at : at + codes.shape[0]] = scaled
        at += codes.shape[0]


def multiply(cuts, cots, units):
    at, cap, across = 0, cuts[0].shape[0], units.shape[1]
    for cut in cuts:
        for j in range(cut.shape[1] // across):
            units[at : at + cap] = cut[:, j * across : (j + 1) * across]
            at += cap
    return lax.dot_general(
        units[...], cots[...], (((0,), (0,)), ((), ())), preferred_element_type=F32
    )


def near_product(cut, across, cots, out, units):
    out[...] = multiply([cut, across.at[:, cots.shape[1] :]], cots, units)


def product(rows, pad, start, cut, across, cots, keep, *refs):
    leave, units = refs[:-1], refs[-1]
    width = cots.shape[1]
    pieces = width // LANES
    part = start[...] + multiply([cut, across], cots, units)
    for p, out in enumerate([keep, *leave]):
        values = part[p * pad : p * pad + rows]
        if p:
            most = jnp.max(jnp.max(jnp.abs(values), axis=0, keepdims=True), axis=1, keepdims=True)
            exponent = jnp.ceil(jnp.log2(jnp.maximum(most, 2.0**-100)))
            values = values * jnp.exp2(-exponent)
            below = out.shape[0] - rows * pieces
            out[rows * pieces :] = jnp.broadcast_to(exponent, (below, LANES))
        for j in range(pieces):
            out[pl.ds(j, rows, stride=pieces), :] = values[:, j * LANES : (j + 1) * LANES]


def call(body, outs, args, fetched=(), scratch=(), limit=32, flops=1):
    vmem = pl.BlockSpec(memory_space=pltpu.VMEM)
    anywhere = pl.BlockSpec(memory_space=pl.ANY)
    return pl.pallas_call(
        body,
        out_shape=tuple(outs),
        in_specs=[anywhere if i in fetched else vmem for i in range(len(args))],
        out_specs=tuple([vmem] * len(outs)),
        scratch_shapes=list(scratch),
        compiler_params=pltpu.CompilerParams(vmem_limit_bytes=limit * 1024 * 1024),
        cost_estimate=pl.CostEstimate(flops=flops, bytes_accessed=1, transcendentals=0),
    )(*args)


def shards(grad_out, routes, route_weight, example_ids, example_weight, hidden):
    sources = lax.axis_size("expert")
    n_dp = lax.axis_size("dp")
    spread = n_dp // MATES
    tokens, width = grad_out.shape
    top = routes.shape[1]
    cap, ff = hidden.shape[3], hidden.shape[4]
    rows = ff // n_dp
    pad = -(-(rows + 1) // 16) * 16
    while spread * pad * sources % LANES:
        pad += 16
    across = spread * pad
    slots = sources * cap
    acts = hidden.reshape(sources, cap, ff)
    shape = jax.ShapeDtypeStruct

    def over_experts(array, k):
        return lax.ppermute(
            array, "expert", [(s, (s - k) % sources) for s in range(sources)]
        )

    def over_dp(array, k):
        return lax.ppermute(array, "dp", [(i, i ^ k) for i in range(n_dp)])

    made = call(
        lambda *refs: build(sources, cap, n_dp, pad, *refs),
        [shape((cap, width + LANES), BF16)] * sources
        + [
            shape((cap, sources * across + (width if k == 2 else 0)), BF16)
            for k in range(MATES)
        ],
        (routes.T, route_weight.T, example_ids, example_weight, grad_out, acts),
        fetched=range(6),
        limit=60,
        scratch=(
            pltpu.VMEM((top, tokens), jnp.int32),
            pltpu.VMEM((top, tokens), F32),
            pltpu.VMEM((1, tokens), jnp.int32),
            pltpu.SMEM((1, EXAMPLES), F32),
            pltpu.VMEM((tokens, width), BF16),
            pltpu.VMEM((sources, cap, ff), BF16),
            pltpu.SemaphoreType.DMA((6,)),
        ),
    )
    (block, *gives), (cut, *parcels) = made[:sources], made[sources:]
    takes = [over_experts(g, k + 1) for k, g in enumerate(gives)]
    parcels = [over_dp(parcel, k + 1) for k, parcel in enumerate(parcels)]
    own, left = call(
        lambda *refs: stage(sources, *refs),
        [shape((cap, width + LANES), BF16), shape((slots, slots), F32)],
        (block, acts),
        flops=1 << 32,
    )
    squares, rest = call(
        lambda *refs: norms(sources, *refs),
        [shape((1, LANES), F32), shape((slots - cap, width + LANES), BF16)],
        (left, own, *takes),
        flops=1 << 32,
    )
    total = squares
    for k in range(1, sources):
        total = total + over_experts(squares, k)
    rest_across = over_dp(rest, 2)
    clip = 1.0 / jnp.maximum(jnp.sqrt(total / (ff * width)), 1.0)
    clip_across = over_dp(clip, 2)
    (cots,) = call(
        lambda *refs: pack(rows, *refs),
        [shape((2 * slots, width), BF16)],
        (own, rest, parcels[1], rest_across, clip, clip_across),
    )
    other_cots = over_dp(cots, 1)
    (start,) = call(
        near_product,
        [shape((across, width), F32)],
        (cut, parcels[1], cots),
        scratch=(pltpu.VMEM((2 * slots, across), BF16),),
        flops=1 << 32,
    )

    held = rows * (width // LANES)
    sent = -(-(held + 8) // 16) * 16
    part, *leave = call(
        lambda *refs: product(rows, pad, *refs),
        [shape((held if p == 0 else sent, LANES), F32) for p in range(spread)],
        (start, parcels[0], parcels[2], other_cots),
        scratch=(pltpu.VMEM((2 * slots, across), BF16),),
    )
    for p in range(1, spread):
        got = over_dp(leave[p - 1].astype(jnp.float16), p * MATES).astype(F32)
        part = part + got[:held] * jnp.exp2(got[held : held + 1])
    return part.reshape(rows, 1, width)


def solution(mesh):
    placed = (
        P(("dp", "expert"), None),
        P(("dp", "expert"), None),
        P(("dp", "expert"), None),
        P("dp", "expert"),
        P("dp", None),
        P("dp", "expert", None, None, None),
    )
    return jax.shard_map(
        shards, mesh=mesh, in_specs=placed, out_specs=P("dp", "expert", None), check_vma=False
    )
```

```python
import jax
import jax.numpy as jnp
from jax import lax
from jax.experimental import pallas as pl
from jax.experimental.pallas import tpu as pltpu
from jax.sharding import PartitionSpec as P

EXAMPLES = 8
MATES = 4
LANES = 128
BF16 = jnp.bfloat16
F32 = jnp.float32


def iota(shape, axis):
    return lax.broadcasted_iota(jnp.int32, shape, axis)


def build(sources, cap, n_dp, pad, routes_at, weights_at, ids_at, loss_at, grad_at, hidden_at, *refs):
    blocks, parcels = refs[:sources], refs[sources : sources + MATES]
    routes, weights, ids, loss, grad, hidden, sems = refs[sources + MATES :]
    spare = grad_at.shape[1] + hidden_at.shape[2] // n_dp
    fetches = [
        pltpu.make_async_copy(source, target, sems.at[i])
        for i, (source, target) in enumerate(
            [
                (routes_at, routes),
                (ids_at, ids),
                (loss_at, loss),
                (weights_at, weights),
                (hidden_at, hidden),
                (grad_at, grad),
            ]
        )
    ]
    for fetch in fetches:
        fetch.start()
    me = lax.axis_index("expert")
    tokens, width = grad.shape
    before = (iota((tokens, tokens), 0) < iota((tokens, tokens), 1)).astype(F32).astype(BF16)
    slot = iota((cap, tokens), 0).astype(F32)
    fetches[0].wait()
    matches = [routes[...] == lax.rem(me + (sources - k), sources) for k in range(sources)]
    hits = [jnp.sum(jnp.where(m, 1.0, 0.0), axis=0, keepdims=True) for m in matches]
    blank = -(-sources // 8) * 8 - sources
    routed = jnp.concatenate(hits + [jnp.zeros((1, tokens), F32)] * blank, axis=0)
    ranking = jnp.dot(routed.astype(BF16), before, preferred_element_type=F32)
    for fetch in fetches[1:4]:
        fetch.wait()
    token_ids = ids[...]
    token_weight = jnp.zeros((1, tokens), F32)
    for x in range(EXAMPLES):
        token_weight = jnp.where(token_ids == x, loss[0, x], token_weight)
    token_code = (token_ids + 1).astype(F32)
    ready = []
    for k in range(sources):
        scale = jnp.sum(jnp.where(matches[k], weights[...], 0.0), axis=0, keepdims=True)
        scale = scale * token_weight
        placed = jnp.where(ranking[k : k + 1] == slot, hits[k], 0.0)
        slot_scale = jnp.sum(placed * scale, axis=1, keepdims=True)
        code = jnp.sum(placed * token_code, axis=1, keepdims=True)
        ready.append((placed.astype(BF16), slot_scale, code))
    fetches[4].wait()
    cut_hidden(sources, n_dp, pad, width, hidden, parcels)
    fetches[5].wait()
    for k in range(sources):
        placed, slot_scale, code = ready[k]
        rows = jnp.dot(placed, grad[...], preferred_element_type=F32)
        rows = (rows * slot_scale).astype(BF16)
        blocks[k][:, :width] = rows
        blocks[k][:, width:] = jnp.broadcast_to(code, (cap, LANES)).astype(BF16)
        if k == 0:
            parcels[2][:, :width] = rows
            parcels[2][:, spare : spare + 1] = code.astype(BF16)


def cut_hidden(sources, n_dp, pad, width, hidden, parcels):
    me, rank = lax.axis_index("expert"), lax.axis_index("dp")
    spread = n_dp // MATES
    cap, ff = hidden.shape[1:]
    rows = ff // n_dp
    high, low = rank // MATES, lax.rem(rank, MATES)
    column = iota((1, spread * pad), 1)
    wanted = jnp.full((1, spread * pad), -2 * ff, jnp.int32)
    for p in range(spread):
        inside = (column >= p * pad) & (column < p * pad + rows)
        wanted = jnp.where(inside, (high ^ p) * (MATES * rows) + column - p * pad, wanted)
    unit = iota((ff, spread * pad), 0)
    acts = [hidden[lax.rem(me + j, sources)] for j in range(sources)]
    acts = jnp.concatenate(acts, axis=0)
    for k in range(MATES):
        pick = jnp.where(unit == wanted + (low ^ k) * rows, 1.0, 0.0).astype(BF16)
        units = jnp.dot(acts, pick, preferred_element_type=F32).astype(BF16)
        first = width if k == 2 else 0
        for j in range(sources):
            at = slice(first + j * spread * pad, first + (j + 1) * spread * pad)
            parcels[k][:, at] = units[j * cap : (j + 1) * cap]


def stage(sources, block, hidden, own, left):
    me = lax.axis_index("expert")
    acts = jnp.concatenate([hidden[lax.rem(me + j, sources)] for j in range(sources)], axis=0)
    left[...] = lax.dot_general(
        acts, acts, (((1,), (1,)), ((), ())), preferred_element_type=F32
    )
    own[...] = block[...]


def chosen(codes):
    lane = iota(codes.shape, 1).astype(F32)
    return (codes == lane) & (codes > 0.0)


def norms(sources, left, own, *refs):
    takes, squares = refs[: sources - 1], refs[-1]
    width = own.shape[1] - LANES
    blocks = jnp.concatenate([own[...]] + [t[...] for t in takes], axis=0)
    cot = blocks[:, :width]
    member = jnp.where(chosen(blocks[:, width:].astype(F32)), 1.0, 0.0)
    last = (((1,), (1,)), ((), ()))
    right = lax.dot_general(cot, cot, last, preferred_element_type=F32)
    one_hot = member.astype(BF16)
    alike = lax.dot_general(one_hot, one_hot, last, preferred_element_type=F32)
    per_slot = jnp.sum(left[...] * right * alike, axis=1, keepdims=True)
    squares[...] = jnp.sum(per_slot * member, axis=0, keepdims=True)


def pass_on(across, *refs):
    takes, rest = refs[:-1], refs[-1]
    cap = takes[0].shape[0]
    for j, take in enumerate(takes):
        rest[j * cap : (j + 1) * cap] = take[...]


def pack(rows, own, rest, across, rest_across, clip, clip_across, out):
    cap, width = own.shape[0], own.shape[1] - LANES
    own_codes = own[:, width:].astype(F32)
    across_codes = across[:, width + rows : width + rows + 1].astype(F32)
    across_codes = jnp.broadcast_to(across_codes, (cap, LANES))
    at = 0
    for block, codes, factors in (
        (own, own_codes, clip),
        (rest, rest[:, width:].astype(F32), clip),
        (across, across_codes, clip_across),
        (rest_across, rest_across[:, width:].astype(F32), clip_across),
    ):
        weight = jnp.sum(jnp.where(chosen(codes), factors[...], 0.0), axis=1, keepdims=True)
        weight = weight / EXAMPLES
        scaled = (weight * block[:, :width].astype(F32)).astype(BF16)
        out[at : at + codes.shape[0]] = scaled
        at += codes.shape[0]


def multiply(cuts, cots, units):
    at, cap, across = 0, cuts[0].shape[0], units.shape[1]
    for cut in cuts:
        for j in range(cut.shape[1] // across):
            units[at : at + cap] = cut[:, j * across : (j + 1) * across]
            at += cap
    return lax.dot_general(
        units[...], cots[...], (((0,), (0,)), ((), ())), preferred_element_type=F32
    )


def near_product(cut, across, cots, out, units):
    out[...] = multiply([cut, across.at[:, cots.shape[1] :]], cots, units)


def product(rows, pad, start, cut, across, cots, keep, *refs):
    leave, units = refs[:-1], refs[-1]
    width = cots.shape[1]
    pieces = width // LANES
    part = start[...] + multiply([cut, across], cots, units)
    for p, out in enumerate([keep, *leave]):
        values = part[p * pad : p * pad + rows]
        if p:
            most = jnp.max(jnp.max(jnp.abs(values), axis=0, keepdims=True), axis=1, keepdims=True)
            exponent = jnp.ceil(jnp.log2(jnp.maximum(most, 2.0**-100)))
            values = values * jnp.exp2(-exponent)
            below = out.shape[0] - rows * pieces
            out[rows * pieces :] = jnp.broadcast_to(exponent, (below, LANES))
        for j in range(pieces):
            out[pl.ds(j, rows, stride=pieces), :] = values[:, j * LANES : (j + 1) * LANES]


def call(body, outs, args, fetched=(), scratch=(), limit=32, flops=1):
    vmem = pl.BlockSpec(memory_space=pltpu.VMEM)
    anywhere = pl.BlockSpec(memory_space=pl.ANY)
    return pl.pallas_call(
        body,
        out_shape=tuple(outs),
        in_specs=[anywhere if i in fetched else vmem for i in range(len(args))],
        out_specs=tuple([vmem] * len(outs)),
        scratch_shapes=list(scratch),
        compiler_params=pltpu.CompilerParams(vmem_limit_bytes=limit * 1024 * 1024),
        cost_estimate=pl.CostEstimate(flops=flops, bytes_accessed=1, transcendentals=0),
    )(*args)


def shards(grad_out, routes, route_weight, example_ids, example_weight, hidden):
    sources = lax.axis_size("expert")
    n_dp = lax.axis_size("dp")
    spread = n_dp // MATES
    tokens, width = grad_out.shape
    top = routes.shape[1]
    cap, ff = hidden.shape[3], hidden.shape[4]
    rows = ff // n_dp
    pad = -(-(rows + 1) // 16) * 16
    while spread * pad * sources % LANES:
        pad += 16
    across = spread * pad
    slots = sources * cap
    acts = hidden.reshape(sources, cap, ff)
    shape = jax.ShapeDtypeStruct

    def over_experts(array, k):
        return lax.ppermute(
            array, "expert", [(s, (s - k) % sources) for s in range(sources)]
        )

    def over_dp(array, k):
        return lax.ppermute(array, "dp", [(i, i ^ k) for i in range(n_dp)])

    made = call(
        lambda *refs: build(sources, cap, n_dp, pad, *refs),
        [shape((cap, width + LANES), BF16)] * sources
        + [
            shape((cap, sources * across + (width if k == 2 else 0)), BF16)
            for k in range(MATES)
        ],
        (routes.T, route_weight.T, example_ids, example_weight, grad_out, acts),
        fetched=range(6),
        limit=60,
        scratch=(
            pltpu.VMEM((top, tokens), jnp.int32),
            pltpu.VMEM((top, tokens), F32),
            pltpu.VMEM((1, tokens), jnp.int32),
            pltpu.SMEM((1, EXAMPLES), F32),
            pltpu.VMEM((tokens, width), BF16),
            pltpu.VMEM((sources, cap, ff), BF16),
            pltpu.SemaphoreType.DMA((6,)),
        ),
    )
    (block, *gives), (cut, *parcels) = made[:sources], made[sources:]
    takes = [over_experts(g, k + 1) for k, g in enumerate(gives)]
    parcels = [over_dp(parcel, k + 1) for k, parcel in enumerate(parcels)]
    own, left = call(
        lambda *refs: stage(sources, *refs),
        [shape((cap, width + LANES), BF16), shape((slots, slots), F32)],
        (block, acts),
        flops=1 << 32,
    )
    (rest,) = call(
        pass_on,
        [shape((slots - cap, width + LANES), BF16)],
        (parcels[1], *takes),
        fetched=(0,),
    )
    (squares,) = call(
        lambda *refs: norms(sources, *refs),
        [shape((1, LANES), F32)],
        (left, own, *takes),
        flops=1 << 32,
    )
    total = squares
    for k in range(1, sources):
        total = total + over_experts(squares, k)
    rest_across = over_dp(rest, 2)
    clip = 1.0 / jnp.maximum(jnp.sqrt(total / (ff * width)), 1.0)
    clip_across = over_dp(clip, 2)
    (cots,) = call(
        lambda *refs: pack(rows, *refs),
        [shape((2 * slots, width), BF16)],
        (own, rest, parcels[1], rest_across, clip, clip_across),
    )
    other_cots = over_dp(cots, 1)
    (start,) = call(
        near_product,
        [shape((across, width), F32)],
        (cut, parcels[1], cots),
        scratch=(pltpu.VMEM((2 * slots, across), BF16),),
        flops=1 << 32,
    )

    held = rows * (width // LANES)
    sent = -(-(held + 8) // 16) * 16
    part, *leave = call(
        lambda *refs: product(rows, pad, *refs),
        [shape((held if p == 0 else sent, LANES), F32) for p in range(spread)],
        (start, parcels[0], parcels[2], other_cots),
        scratch=(pltpu.VMEM((2 * slots, across), BF16),),
    )
    for p in range(1, spread):
        got = over_dp(leave[p - 1].astype(jnp.float16), p * MATES).astype(F32)
        part = part + got[:held] * jnp.exp2(got[held : held + 1])
    return part.reshape(rows, 1, width)


def solution(mesh):
    placed = (
        P(("dp", "expert"), None),
        P(("dp", "expert"), None),
        P(("dp", "expert"), None),
        P("dp", "expert"),
        P("dp", None),
        P("dp", "expert", None, None, None),
    )
    return jax.shard_map(
        shards, mesh=mesh, in_specs=placed, out_specs=P("dp", "expert", None), check_vma=False
    )
```

```python
import jax
import jax.numpy as jnp
from jax import lax
from jax.experimental import pallas as pl
from jax.experimental.pallas import tpu as pltpu
from jax.sharding import PartitionSpec as P

EXAMPLES = 8
MATES = 4
LANES = 128
BF16 = jnp.bfloat16
F32 = jnp.float32


def iota(shape, axis):
    return lax.broadcasted_iota(jnp.int32, shape, axis)


def build(sources, cap, routes_at, weights_at, ids_at, loss_at, grad_at, *refs):
    blocks = refs[:sources]
    routes, weights, ids, loss, grad, sems = refs[sources:]
    fetches = [
        pltpu.make_async_copy(source, target, sems.at[i])
        for i, (source, target) in enumerate(
            [
                (routes_at, routes),
                (ids_at, ids),
                (loss_at, loss),
                (weights_at, weights),
                (grad_at, grad),
            ]
        )
    ]
    for fetch in fetches:
        fetch.start()
    me = lax.axis_index("expert")
    tokens, width = grad.shape
    before = (iota((tokens, tokens), 0) < iota((tokens, tokens), 1)).astype(F32).astype(BF16)
    slot = iota((cap, tokens), 0).astype(F32)
    fetches[0].wait()
    matches = [routes[...] == lax.rem(me + (sources - k), sources) for k in range(sources)]
    hits = [jnp.sum(jnp.where(m, 1.0, 0.0), axis=0, keepdims=True) for m in matches]
    blank = -(-sources // 8) * 8 - sources
    routed = jnp.concatenate(hits + [jnp.zeros((1, tokens), F32)] * blank, axis=0)
    ranking = jnp.dot(routed.astype(BF16), before, preferred_element_type=F32)
    for fetch in fetches[1:4]:
        fetch.wait()
    token_ids = ids[...]
    token_weight = jnp.zeros((1, tokens), F32)
    for x in range(EXAMPLES):
        token_weight = jnp.where(token_ids == x, loss[0, x], token_weight)
    token_code = (token_ids + 1).astype(F32)
    ready = []
    for k in range(sources):
        scale = jnp.sum(jnp.where(matches[k], weights[...], 0.0), axis=0, keepdims=True)
        scale = scale * token_weight
        placed = jnp.where(ranking[k : k + 1] == slot, hits[k], 0.0)
        slot_scale = jnp.sum(placed * scale, axis=1, keepdims=True)
        code = jnp.sum(placed * token_code, axis=1, keepdims=True)
        ready.append((placed.astype(BF16), slot_scale, code))
    fetches[4].wait()
    for k in range(sources):
        placed, slot_scale, code = ready[k]
        rows = jnp.dot(placed, grad[...], preferred_element_type=F32)
        rows = (rows * slot_scale).astype(BF16)
        blocks[k][:, :width] = rows
        blocks[k][:, width:] = jnp.broadcast_to(code, (cap, LANES)).astype(BF16)


def stage(sources, n_dp, pad, block, hidden, own, left, *cuts):
    own[...] = block[...]
    me, rank = lax.axis_index("expert"), lax.axis_index("dp")
    spread = n_dp // MATES
    cap, ff = hidden.shape[1:]
    rows = ff // n_dp
    high, low = rank // MATES, lax.rem(rank, MATES)
    column = iota((1, spread * pad), 1)
    wanted = jnp.full((1, spread * pad), -2 * ff, jnp.int32)
    for p in range(spread):
        inside = (column >= p * pad) & (column < p * pad + rows)
        wanted = jnp.where(inside, (high ^ p) * (MATES * rows) + column - p * pad, wanted)
    unit = iota((ff, spread * pad), 0)
    acts = [hidden[lax.rem(me + j, sources)] for j in range(sources)]
    acts = jnp.concatenate(acts, axis=0)
    left[...] = lax.dot_general(
        acts, acts, (((1,), (1,)), ((), ())), preferred_element_type=F32
    )
    for k in range(MATES):
        pick = jnp.where(unit == wanted + (low ^ k) * rows, 1.0, 0.0).astype(BF16)
        units = jnp.dot(acts, pick, preferred_element_type=F32).astype(BF16)
        for j in range(sources):
            at = slice(j * spread * pad, (j + 1) * spread * pad)
            cuts[k][:, at] = units[j * cap : (j + 1) * cap]


def chosen(codes):
    codes = jnp.broadcast_to(codes.astype(F32), (codes.shape[0], LANES))
    lane = iota(codes.shape, 1).astype(F32)
    return (codes == lane) & (codes > 0.0)


def norms(sources, left, own, *refs):
    takes, squares = refs[: sources - 1], refs[-1]
    width = own.shape[1] - LANES
    blocks = jnp.concatenate([own[...]] + [t[...] for t in takes], axis=0)
    cot = blocks[:, :width]
    member = jnp.where(chosen(blocks[:, width : width + 1]), 1.0, 0.0)
    last = (((1,), (1,)), ((), ()))
    right = lax.dot_general(cot, cot, last, preferred_element_type=F32)
    one_hot = member.astype(BF16)
    alike = lax.dot_general(one_hot, one_hot, last, preferred_element_type=F32)
    per_slot = jnp.sum(left[...] * right * alike, axis=1, keepdims=True)
    squares[...] = jnp.sum(per_slot * member, axis=0, keepdims=True)


def pass_on(across, squares, cut, *refs):
    takes, rest = refs[:-1], refs[-1]
    cap, wide = takes[0].shape
    half = LANES // 2
    for j, take in enumerate(takes):
        part = slice(j * cap, (j + 1) * cap)
        rest[part, :wide] = take[...]
        if j:
            rest[part, wide:] = jnp.zeros((cap, rest.shape[1] - wide), BF16)
    rest[:cap, wide:] = cut[...]
    value = jnp.broadcast_to(squares[...], (cap, LANES))
    high = value.astype(BF16).astype(F32)
    middle = (value - high).astype(BF16).astype(F32)
    low = value - high - middle
    row = iota((cap, LANES), 0)
    three = jnp.where(row == 0, high, jnp.where(row == 1, middle, low)).astype(BF16)
    rest[:cap, wide - half : wide] = three[:, :half]


def pack(sources, count, own, rest, across, rest_across, *refs):
    near, far, out = refs[:sources], refs[sources:-1], refs[-1]
    width = own.shape[1] - LANES
    half = LANES // 2
    three = rest_across[0:8, width + half : width + LANES].astype(F32)
    three = three[0:1] + three[1:2] + three[2:3]
    totals = [near[0][...], jnp.concatenate([three, jnp.zeros_like(three)], axis=1)]
    for k in range(1, sources):
        totals = [totals[0] + near[k][...], totals[1] + far[k - 1][...]]
    clips = [1.0 / jnp.maximum(jnp.sqrt(total / count), 1.0) for total in totals]
    at = 0
    for block, clip in ((own, clips[0]), (rest, clips[0]), (across, clips[1]), (rest_across, clips[1])):
        mine = chosen(block[:, width : width + 1])
        weight = jnp.sum(jnp.where(mine, clip, 0.0), axis=1, keepdims=True) / EXAMPLES
        scaled = (weight * block[:, :width].astype(F32)).astype(BF16)
        out[at : at + mine.shape[0]] = scaled
        at += mine.shape[0]


def multiply(cuts, cots, units):
    at, cap, across = 0, cuts[0].shape[0], units.shape[1]
    for cut in cuts:
        for j in range(cut.shape[1] // across):
            units[at : at + cap] = cut[:, j * across : (j + 1) * across]
            at += cap
    return lax.dot_general(
        units[...], cots[...], (((0,), (0,)), ((), ())), preferred_element_type=F32
    )


def near_product(cut, rest_across, cots, out, units):
    first = cots.shape[1] + LANES
    cap = cut.shape[0]
    across = rest_across.at[:cap, first : first + cut.shape[1]]
    out[...] = multiply([cut, across], cots, units)


def product(rows, pad, start, cut, across, cots, keep, *refs):
    leave, units = refs[:-1], refs[-1]
    width = cots.shape[1]
    pieces = width // LANES
    part = start[...] + multiply([cut, across], cots, units)
    for p, out in enumerate([keep, *leave]):
        values = part[p * pad : p * pad + rows]
        if p:
            most = jnp.max(jnp.max(jnp.abs(values), axis=0, keepdims=True), axis=1, keepdims=True)
            exponent = jnp.ceil(jnp.log2(jnp.maximum(most, 2.0**-100)))
            values = values * jnp.exp2(-exponent)
            below = out.shape[0] - rows * pieces
            out[rows * pieces :] = jnp.broadcast_to(exponent, (below, LANES))
        for j in range(pieces):
            out[pl.ds(j, rows, stride=pieces), :] = values[:, j * LANES : (j + 1) * LANES]


def call(body, outs, args, fetched=(), scratch=(), limit=32, flops=1):
    vmem = pl.BlockSpec(memory_space=pltpu.VMEM)
    anywhere = pl.BlockSpec(memory_space=pl.ANY)
    return pl.pallas_call(
        body,
        out_shape=tuple(outs),
        in_specs=[anywhere if i in fetched else vmem for i in range(len(args))],
        out_specs=tuple([vmem] * len(outs)),
        scratch_shapes=list(scratch),
        compiler_params=pltpu.CompilerParams(vmem_limit_bytes=limit * 1024 * 1024),
        cost_estimate=pl.CostEstimate(flops=flops, bytes_accessed=1, transcendentals=0),
    )(*args)


def shards(grad_out, routes, route_weight, example_ids, example_weight, hidden):
    sources = lax.axis_size("expert")
    n_dp = lax.axis_size("dp")
    spread = n_dp // MATES
    tokens, width = grad_out.shape
    top = routes.shape[1]
    cap, ff = hidden.shape[3], hidden.shape[4]
    rows = ff // n_dp
    pad = -(-(rows + 1) // 16) * 16
    while spread * pad * sources % LANES:
        pad += 16
    across = spread * pad
    slots = sources * cap
    acts = hidden.reshape(sources, cap, ff)
    shape = jax.ShapeDtypeStruct

    def over_experts(array, k):
        return lax.ppermute(
            array, "expert", [(s, (s - k) % sources) for s in range(sources)]
        )

    def over_dp(array, k):
        return lax.ppermute(array, "dp", [(i, i ^ k) for i in range(n_dp)])

    def over_both(array, k):
        where = [(i, e) for i in range(n_dp) for e in range(sources)]
        pairs = [
            (i * sources + e, (i ^ 2) * sources + (e - k) % sources) for i, e in where
        ]
        return lax.ppermute(array, ("dp", "expert"), pairs)

    block, *gives = call(
        lambda *refs: build(sources, cap, *refs),
        [shape((cap, width + LANES), BF16)] * sources,
        (routes.T, route_weight.T, example_ids, example_weight, grad_out),
        fetched=range(5),
        limit=60,
        scratch=(
            pltpu.VMEM((top, tokens), jnp.int32),
            pltpu.VMEM((top, tokens), F32),
            pltpu.VMEM((1, tokens), jnp.int32),
            pltpu.SMEM((1, EXAMPLES), F32),
            pltpu.VMEM((tokens, width), BF16),
            pltpu.SemaphoreType.DMA((5,)),
        ),
    )
    takes = [over_experts(g, k + 1) for k, g in enumerate(gives)]
    block_across = over_dp(block, 2)
    own, left, *cuts = call(
        lambda *refs: stage(sources, n_dp, pad, *refs),
        [shape((cap, width + LANES), BF16), shape((slots, slots), F32)]
        + [shape((cap, sources * across), BF16)] * MATES,
        (block, acts),
        flops=1 << 32,
    )
    (squares,) = call(
        lambda *refs: norms(sources, *refs),
        [shape((1, LANES), F32)],
        (left, own, *takes),
        flops=1 << 32,
    )
    (rest,) = call(
        pass_on,
        [shape((slots - cap, width + LANES + sources * across), BF16)],
        (block_across, squares, cuts[2], *takes),
        fetched=(0,),
    )
    rest_across = over_dp(rest, 2)
    near_squares = [squares] + [over_experts(squares, k) for k in range(1, sources)]
    far_squares = [over_both(squares, k) for k in range(1, sources)]
    (cots,) = call(
        lambda *refs: pack(sources, ff * width, *refs),
        [shape((2 * slots, width), BF16)],
        (own, rest, block_across, rest_across, *near_squares, *far_squares),
    )
    other_cots = over_dp(cots, 1)
    (start,) = call(
        near_product,
        [shape((across, width), F32)],
        (cuts[0], rest_across, cots),
        scratch=(pltpu.VMEM((2 * slots, across), BF16),),
        flops=1 << 32,
    )

    held = rows * (width // LANES)
    sent = held + 8
    part, *leave = call(
        lambda *refs: product(rows, pad, *refs),
        [shape((held if p == 0 else sent, LANES), F32) for p in range(spread)],
        (start, over_dp(cuts[1], 1), over_dp(cuts[3], 3), other_cots),
        scratch=(pltpu.VMEM((2 * slots, across), BF16),),
    )
    for p in range(1, spread):
        got = over_dp(leave[p - 1].astype(jnp.float16), p * MATES).astype(F32)
        part = part + got[:held] * jnp.exp2(got[held : held + 1])
    return part.reshape(rows, 1, width)


def solution(mesh):
    placed = (
        P(("dp", "expert"), None),
        P(("dp", "expert"), None),
        P(("dp", "expert"), None),
        P("dp", "expert"),
        P("dp", None),
        P("dp", "expert", None, None, None),
    )
    return jax.shard_map(
        shards, mesh=mesh, in_specs=placed, out_specs=P("dp", "expert", None), check_vma=False
    )
```

```python
import jax
import jax.numpy as jnp
from jax import lax
from jax.experimental import pallas as pl
from jax.experimental.pallas import tpu as pltpu
from jax.sharding import PartitionSpec as P

EXAMPLES = 8
MATES = 4
LANES = 128
BF16 = jnp.bfloat16
F32 = jnp.float32


def iota(shape, axis):
    return lax.broadcasted_iota(jnp.int32, shape, axis)


def build(sources, cap, n_dp, pad, routes_at, weights_at, ids_at, loss_at, grad_at, hidden_at, *refs):
    blocks = refs[:sources]
    routes, weights, ids, loss, grad, hidden, sems = refs[sources:]
    fetches = [
        pltpu.make_async_copy(source, target, sems.at[i])
        for i, (source, target) in enumerate(
            [
                (routes_at, routes),
                (ids_at, ids),
                (loss_at, loss),
                (weights_at, weights),
                (hidden_at, hidden),
                (grad_at, grad),
            ]
        )
    ]
    for fetch in fetches:
        fetch.start()
    me = lax.axis_index("expert")
    tokens, width = grad.shape
    before = (iota((tokens, tokens), 0) < iota((tokens, tokens), 1)).astype(F32).astype(BF16)
    slot = iota((cap, tokens), 0).astype(F32)
    fetches[0].wait()
    matches = [routes[...] == lax.rem(me + (sources - k), sources) for k in range(sources)]
    hits = [jnp.sum(jnp.where(m, 1.0, 0.0), axis=0, keepdims=True) for m in matches]
    blank = -(-sources // 8) * 8 - sources
    routed = jnp.concatenate(hits + [jnp.zeros((1, tokens), F32)] * blank, axis=0)
    ranking = jnp.dot(routed.astype(BF16), before, preferred_element_type=F32)
    for fetch in fetches[1:4]:
        fetch.wait()
    token_ids = ids[...]
    token_weight = jnp.zeros((1, tokens), F32)
    for x in range(EXAMPLES):
        token_weight = jnp.where(token_ids == x, loss[0, x], token_weight)
    token_code = (token_ids + 1).astype(F32)
    ready = []
    for k in range(sources):
        scale = jnp.sum(jnp.where(matches[k], weights[...], 0.0), axis=0, keepdims=True)
        scale = scale * token_weight
        placed = jnp.where(ranking[k : k + 1] == slot, hits[k], 0.0)
        slot_scale = jnp.sum(placed * scale, axis=1, keepdims=True)
        code = jnp.sum(placed * token_code, axis=1, keepdims=True)
        ready.append((placed.astype(BF16), slot_scale, code))
    fetches[4].wait()
    at = width + LANES
    for units in cuts_of(sources, n_dp, pad, hidden, (2, 3)):
        for j in range(sources):
            blocks[0][:, at : at + units.shape[1]] = units[j * cap : (j + 1) * cap]
            at += units.shape[1]
    fetches[5].wait()
    for k in range(sources):
        placed, slot_scale, code = ready[k]
        rows = jnp.dot(placed, grad[...], preferred_element_type=F32)
        rows = (rows * slot_scale).astype(BF16)
        blocks[k][:, :width] = rows
        blocks[k][:, width : width + LANES] = jnp.broadcast_to(code, (cap, LANES)).astype(BF16)


def cuts_of(sources, n_dp, pad, hidden, mates):
    me, rank = lax.axis_index("expert"), lax.axis_index("dp")
    spread = n_dp // MATES
    cap, ff = hidden.shape[1:]
    rows = ff // n_dp
    high, low = rank // MATES, lax.rem(rank, MATES)
    column = iota((1, spread * pad), 1)
    wanted = jnp.full((1, spread * pad), -2 * ff, jnp.int32)
    for p in range(spread):
        inside = (column >= p * pad) & (column < p * pad + rows)
        wanted = jnp.where(inside, (high ^ p) * (MATES * rows) + column - p * pad, wanted)
    unit = iota((ff, spread * pad), 0)
    acts = [hidden[lax.rem(me + j, sources)] for j in range(sources)]
    acts = jnp.concatenate(acts, axis=0)
    units = []
    for k in mates:
        pick = jnp.where(unit == wanted + (low ^ k) * rows, 1.0, 0.0).astype(BF16)
        units.append(jnp.dot(acts, pick, preferred_element_type=F32).astype(BF16))
    return units


def stage(sources, n_dp, pad, block, hidden, own, left, cut, sibling_cut):
    own[...] = block[:, : own.shape[1]]
    me = lax.axis_index("expert")
    acts = jnp.concatenate([hidden[lax.rem(me + j, sources)] for j in range(sources)], axis=0)
    left[...] = lax.dot_general(
        acts, acts, (((1,), (1,)), ((), ())), preferred_element_type=F32
    )
    cut[...], sibling_cut[...] = cuts_of(sources, n_dp, pad, hidden, (0, 1))


def chosen(codes):
    codes = jnp.broadcast_to(codes.astype(F32), (codes.shape[0], LANES))
    lane = iota(codes.shape, 1).astype(F32)
    return (codes == lane) & (codes > 0.0)


def norms(sources, left, own, *refs):
    takes, squares = refs[: sources - 1], refs[-1]
    width = own.shape[1] - LANES
    blocks = jnp.concatenate([own[...]] + [t[...] for t in takes], axis=0)
    cot = blocks[:, :width]
    member = jnp.where(chosen(blocks[:, width : width + 1]), 1.0, 0.0)
    last = (((1,), (1,)), ((), ()))
    right = lax.dot_general(cot, cot, last, preferred_element_type=F32)
    one_hot = member.astype(BF16)
    alike = lax.dot_general(one_hot, one_hot, last, preferred_element_type=F32)
    per_slot = jnp.sum(left[...] * right * alike, axis=1, keepdims=True)
    squares[...] = jnp.sum(per_slot * member, axis=0, keepdims=True)


def after(across, squares, out):
    out[...] = squares[...]


def pass_on(squares, *refs):
    takes, rest = refs[:-1], refs[-1]
    cap, wide = takes[0].shape
    half = LANES // 2
    for j, take in enumerate(takes):
        part = slice(j * cap, (j + 1) * cap)
        rest[part] = take[...]
    value = jnp.broadcast_to(squares[...], (cap, LANES))
    high = value.astype(BF16).astype(F32)
    middle = (value - high).astype(BF16).astype(F32)
    low = value - high - middle
    row = iota((cap, LANES), 0)
    three = jnp.where(row == 0, high, jnp.where(row == 1, middle, low)).astype(BF16)
    rest[:cap, wide - half : wide] = three[:, :half]


def pack(sources, count, own, rest, across, rest_across, sibling_cut, *refs):
    near, far, out = refs[:sources], refs[sources:-1], refs[-1]
    width = own.shape[1] - LANES
    half = LANES // 2
    three = rest_across[0:8, width + half : width + LANES].astype(F32)
    three = three[0:1] + three[1:2] + three[2:3]
    totals = [near[0][...], jnp.concatenate([three, jnp.zeros_like(three)], axis=1)]
    for k in range(1, sources):
        totals = [totals[0] + near[k][...], totals[1] + far[k - 1][...]]
    clips = [1.0 / jnp.maximum(jnp.sqrt(total / count), 1.0) for total in totals]
    at = 0
    for block, clip in ((own, clips[0]), (rest, clips[0]), (across, clips[1]), (rest_across, clips[1])):
        mine = chosen(block[:, width : width + 1])
        weight = jnp.sum(jnp.where(mine, clip, 0.0), axis=1, keepdims=True) / EXAMPLES
        scaled = (weight * block[:, :width].astype(F32)).astype(BF16)
        out[at : at + mine.shape[0], :width] = scaled
        at += mine.shape[0]
    slots, lanes = sibling_cut.shape
    cap = own.shape[0]
    out[:slots, width:] = sibling_cut[...]
    for j in range(sources):
        first = width + LANES + (sources + j) * lanes
        out[slots + j * cap : slots + (j + 1) * cap, width:] = across[:, first : first + lanes]


def multiply(units, cots):
    return lax.dot_general(
        units, cots, (((0,), (0,)), ((), ())), preferred_element_type=F32
    )


def near_product(sources, cut, across, cots, out):
    lanes = cut.shape[1]
    width = cots.shape[1] - lanes
    first = width + LANES
    units = [cut[...]] + [
        across[:, first + j * lanes : first + (j + 1) * lanes] for j in range(sources)
    ]
    out[...] = multiply(jnp.concatenate(units, axis=0), cots[:, :width])


def product(rows, pad, start, cots, keep, *leave):
    width = start.shape[1]
    pieces = width // LANES
    part = start[...] + multiply(cots[:, width:], cots[:, :width])
    for p, out in enumerate([keep, *leave]):
        values = part[p * pad : p * pad + rows]
        if p:
            most = jnp.max(jnp.max(jnp.abs(values), axis=0, keepdims=True), axis=1, keepdims=True)
            exponent = jnp.ceil(jnp.log2(jnp.maximum(most, 2.0**-100)))
            values = values * jnp.exp2(-exponent)
            below = out.shape[0] - rows * pieces
            out[rows * pieces :] = jnp.broadcast_to(exponent, (below, LANES))
        for j in range(pieces):
            out[pl.ds(j, rows, stride=pieces), :] = values[:, j * LANES : (j + 1) * LANES]


def call(body, outs, args, fetched=(), scratch=(), limit=32, flops=1):
    vmem = pl.BlockSpec(memory_space=pltpu.VMEM)
    anywhere = pl.BlockSpec(memory_space=pl.ANY)
    return pl.pallas_call(
        body,
        out_shape=tuple(outs),
        in_specs=[anywhere if i in fetched else vmem for i in range(len(args))],
        out_specs=tuple([vmem] * len(outs)),
        scratch_shapes=list(scratch),
        compiler_params=pltpu.CompilerParams(vmem_limit_bytes=limit * 1024 * 1024),
        cost_estimate=pl.CostEstimate(flops=flops, bytes_accessed=1, transcendentals=0),
    )(*args)


def shards(grad_out, routes, route_weight, example_ids, example_weight, hidden):
    sources = lax.axis_size("expert")
    n_dp = lax.axis_size("dp")
    spread = n_dp // MATES
    tokens, width = grad_out.shape
    top = routes.shape[1]
    cap, ff = hidden.shape[3], hidden.shape[4]
    rows = ff // n_dp
    pad = -(-(rows + 1) // 16) * 16
    while spread * pad * sources % LANES:
        pad += 16
    across = spread * pad
    slots = sources * cap
    acts = hidden.reshape(sources, cap, ff)
    shape = jax.ShapeDtypeStruct

    def over_experts(array, k):
        return lax.ppermute(
            array, "expert", [(s, (s - k) % sources) for s in range(sources)]
        )

    def over_dp(array, k):
        return lax.ppermute(array, "dp", [(i, i ^ k) for i in range(n_dp)])

    def over_both(array, k):
        where = [(i, e) for i in range(n_dp) for e in range(sources)]
        pairs = [
            (i * sources + e, (i ^ 2) * sources + (e - k) % sources) for i, e in where
        ]
        return lax.ppermute(array, ("dp", "expert"), pairs)

    block, *gives = call(
        lambda *refs: build(sources, cap, n_dp, pad, *refs),
        [shape((cap, width + LANES + 2 * sources * across), BF16)]
        + [shape((cap, width + LANES), BF16)] * (sources - 1),
        (routes.T, route_weight.T, example_ids, example_weight, grad_out, acts),
        fetched=range(6),
        limit=60,
        scratch=(
            pltpu.VMEM((top, tokens), jnp.int32),
            pltpu.VMEM((top, tokens), F32),
            pltpu.VMEM((1, tokens), jnp.int32),
            pltpu.SMEM((1, EXAMPLES), F32),
            pltpu.VMEM((tokens, width), BF16),
            pltpu.VMEM((sources, cap, ff), BF16),
            pltpu.SemaphoreType.DMA((6,)),
        ),
    )
    takes = [over_experts(g, k + 1) for k, g in enumerate(gives)]
    block_across = over_dp(block, 2)
    own, left, cut, sibling_cut = call(
        lambda *refs: stage(sources, n_dp, pad, *refs),
        [shape((cap, width + LANES), BF16), shape((slots, slots), F32)]
        + [shape((slots, across), BF16)] * 2,
        (block, acts),
        flops=1 << 32,
    )
    (squares,) = call(
        lambda *refs: norms(sources, *refs),
        [shape((1, LANES), F32)],
        (left, own, *takes),
        flops=1 << 32,
    )
    (rest,) = call(
        pass_on,
        [shape((slots - cap, width + LANES), BF16)],
        (squares, *takes),
    )
    (late_squares,) = call(
        after, [shape((1, LANES), F32)], (block_across, squares), fetched=(0,)
    )
    rest_across = over_dp(rest, 2)
    near_squares = [squares] + [over_experts(squares, k) for k in range(1, sources)]
    far_squares = [over_both(late_squares, k) for k in range(1, sources)]
    (cots,) = call(
        lambda *refs: pack(sources, ff * width, *refs),
        [shape((2 * slots, width + across), BF16)],
        (own, rest, block_across, rest_across, sibling_cut, *near_squares, *far_squares),
    )
    other_cots = over_dp(cots, 1)
    (start,) = call(
        lambda *refs: near_product(sources, *refs),
        [shape((across, width), F32)],
        (cut, block_across, cots),
        flops=1 << 32,
    )

    held = rows * (width // LANES)
    sent = held + 8
    part, *leave = call(
        lambda *refs: product(rows, pad, *refs),
        [shape((held if p == 0 else sent, LANES), F32) for p in range(spread)],
        (start, other_cots),
    )
    for p in range(1, spread):
        got = over_dp(leave[p - 1].astype(jnp.float16), p * MATES).astype(F32)
        part = part + got[:held] * jnp.exp2(got[held : held + 1])
    return part.reshape(rows, 1, width)


def solution(mesh):
    placed = (
        P(("dp", "expert"), None),
        P(("dp", "expert"), None),
        P(("dp", "expert"), None),
        P("dp", "expert"),
        P("dp", None),
        P("dp", "expert", None, None, None),
    )
    return jax.shard_map(
        shards, mesh=mesh, in_specs=placed, out_specs=P("dp", "expert", None), check_vma=False
    )
```

```python
import jax
import jax.numpy as jnp
from jax import lax
from jax.experimental import pallas as pl
from jax.experimental.pallas import tpu as pltpu
from jax.sharding import PartitionSpec as P

EXAMPLES = 8
MATES = 4
LANES = 128
BF16 = jnp.bfloat16
F32 = jnp.float32


def iota(shape, axis):
    return lax.broadcasted_iota(jnp.int32, shape, axis)


def build(sources, cap, routes_at, weights_at, ids_at, loss_at, grad_at, *refs):
    alone, blocks = refs[0], refs[1 : sources + 1]
    routes, weights, ids, loss, grad, sems = refs[sources + 1 :]
    fetches = [
        pltpu.make_async_copy(source, target, sems.at[i])
        for i, (source, target) in enumerate(
            [
                (routes_at, routes),
                (ids_at, ids),
                (loss_at, loss),
                (weights_at, weights),
                (grad_at, grad),
            ]
        )
    ]
    for fetch in fetches:
        fetch.start()
    me = lax.axis_index("expert")
    tokens, width = grad.shape
    before = (iota((tokens, tokens), 0) < iota((tokens, tokens), 1)).astype(F32).astype(BF16)
    slot = iota((cap, tokens), 0).astype(F32)
    fetches[0].wait()
    matches = [routes[...] == lax.rem(me + (sources - k), sources) for k in range(sources)]
    hits = [jnp.sum(jnp.where(m, 1.0, 0.0), axis=0, keepdims=True) for m in matches]
    blank = -(-sources // 8) * 8 - sources
    routed = jnp.concatenate(hits + [jnp.zeros((1, tokens), F32)] * blank, axis=0)
    ranking = jnp.dot(routed.astype(BF16), before, preferred_element_type=F32)
    for fetch in fetches[1:4]:
        fetch.wait()
    token_ids = ids[...]
    token_weight = jnp.zeros((1, tokens), F32)
    for x in range(EXAMPLES):
        token_weight = jnp.where(token_ids == x, loss[0, x], token_weight)
    token_code = (token_ids + 1).astype(F32)
    ready = []
    for k in range(sources):
        scale = jnp.sum(jnp.where(matches[k], weights[...], 0.0), axis=0, keepdims=True)
        scale = scale * token_weight
        placed = jnp.where(ranking[k : k + 1] == slot, hits[k], 0.0)
        slot_scale = jnp.sum(placed * scale, axis=1, keepdims=True)
        code = jnp.sum(placed * token_code, axis=1, keepdims=True)
        ready.append((placed.astype(BF16), slot_scale, code))
    fetches[4].wait()
    for k in range(sources):
        placed, slot_scale, code = ready[k]
        rows = jnp.dot(placed, grad[...], preferred_element_type=F32)
        rows = (rows * slot_scale).astype(BF16)
        blocks[k][:, :width] = rows
        if k == 0:
            alone[...] = rows
        blocks[k][:, width:] = jnp.broadcast_to(code, (cap, LANES)).astype(BF16)


def stage(sources, n_dp, pad, block, hidden, own, left, *cuts):
    own[...] = block[...]
    me, rank = lax.axis_index("expert"), lax.axis_index("dp")
    spread = n_dp // MATES
    cap, ff = hidden.shape[1:]
    rows = ff // n_dp
    high, low = rank // MATES, lax.rem(rank, MATES)
    column = iota((1, spread * pad), 1)
    wanted = jnp.full((1, spread * pad), -2 * ff, jnp.int32)
    for p in range(spread):
        inside = (column >= p * pad) & (column < p * pad + rows)
        wanted = jnp.where(inside, (high ^ p) * (MATES * rows) + column - p * pad, wanted)
    unit = iota((ff, spread * pad), 0)
    acts = [hidden[lax.rem(me + j, sources)] for j in range(sources)]
    acts = jnp.concatenate(acts, axis=0)
    left[...] = lax.dot_general(
        acts, acts, (((1,), (1,)), ((), ())), preferred_element_type=F32
    )
    for k in range(MATES):
        pick = jnp.where(unit == wanted + (low ^ k) * rows, 1.0, 0.0).astype(BF16)
        units = jnp.dot(acts, pick, preferred_element_type=F32).astype(BF16)
        for j in range(sources):
            at = slice(j * spread * pad, (j + 1) * spread * pad)
            cuts[k][:, at] = units[j * cap : (j + 1) * cap]


def chosen(codes):
    codes = jnp.broadcast_to(codes.astype(F32), (codes.shape[0], LANES))
    lane = iota(codes.shape, 1).astype(F32)
    return (codes == lane) & (codes > 0.0)


def norms(sources, left, own, *refs):
    takes, squares = refs[: sources - 1], refs[-1]
    width = own.shape[1] - LANES
    blocks = jnp.concatenate([own[...]] + [t[...] for t in takes], axis=0)
    cot = blocks[:, :width]
    member = jnp.where(chosen(blocks[:, width : width + 1]), 1.0, 0.0)
    last = (((1,), (1,)), ((), ()))
    right = lax.dot_general(cot, cot, last, preferred_element_type=F32)
    one_hot = member.astype(BF16)
    alike = lax.dot_general(one_hot, one_hot, last, preferred_element_type=F32)
    per_slot = jnp.sum(left[...] * right * alike, axis=1, keepdims=True)
    squares[...] = jnp.sum(per_slot * member, axis=0, keepdims=True)


def diagonal(cap):
    return iota((cap, LANES), 0) == iota((cap, LANES), 1)


def pass_on(rows, pad, across, own, squares, cut, *refs):
    takes, rest = refs[:-1], refs[-1]
    cap, width = own.shape[0], own.shape[1] - LANES
    value = jnp.where(diagonal(cap), squares[...], 0.0)
    value = jnp.sum(value, axis=1, keepdims=True)
    high = value.astype(BF16).astype(F32)
    middle = (value - high).astype(BF16).astype(F32)
    lane = iota(cut.shape, 1)
    tail = cut[...].astype(F32)
    for at, column in (
        (pad + rows, own[:, width : width + 1].astype(F32)),
        (rows + 1, high),
        (rows + 2, middle),
        (rows + 3, value - high - middle),
    ):
        tail = jnp.where(lane == at, column, tail)
    for j, take in enumerate(takes):
        part = slice(j * cap, (j + 1) * cap)
        rest[part, :width] = take[:, :width]
        code = take[:, width : width + 1].astype(F32)
        rest[part, width:] = jnp.where(lane == rows, code, 0.0 if j else tail).astype(BF16)


def pack(sources, count, rows, pad, own, rest, across, rest_across, *refs):
    near, far, out = refs[:sources], refs[sources:-1], refs[-1]
    cap, width = own.shape[0], own.shape[1] - LANES
    first = width + rows
    three = rest_across[:cap, first + 1 : first + 4].astype(F32)
    three = three[:, 0:1] + three[:, 1:2] + three[:, 2:3]
    three = jnp.where(diagonal(cap), three, 0.0)
    totals = [near[0][...], jnp.sum(three, axis=0, keepdims=True)]
    for k in range(1, sources):
        totals = [totals[0] + near[k][...], totals[1] + far[k - 1][...]]
    clips = [1.0 / jnp.maximum(jnp.sqrt(total / count), 1.0) for total in totals]
    at = 0
    for block, codes, clip in (
        (own, own[:, width : width + 1], clips[0]),
        (rest, rest[:, first : first + 1], clips[0]),
        (across, rest_across[:cap, first + pad : first + pad + 1], clips[1]),
        (rest_across, rest_across[:, first : first + 1], clips[1]),
    ):
        mine = chosen(codes)
        weight = jnp.sum(jnp.where(mine, clip, 0.0), axis=1, keepdims=True) / EXAMPLES
        scaled = (weight * block[:, :width].astype(F32)).astype(BF16)
        out[at : at + mine.shape[0]] = scaled
        at += mine.shape[0]


def multiply(cuts, cots, units):
    at, cap, across = 0, cuts[0].shape[0], units.shape[1]
    for cut in cuts:
        for j in range(cut.shape[1] // across):
            units[at : at + cap] = cut[:, j * across : (j + 1) * across]
            at += cap
    return lax.dot_general(
        units[...], cots[...], (((0,), (0,)), ((), ())), preferred_element_type=F32
    )


def near_product(cut, rest_across, cots, out, units):
    across = rest_across.at[: cut.shape[0], cots.shape[1] :]
    out[...] = multiply([cut, across], cots, units)


def product(rows, pad, start, cut, across, cots, keep, *refs):
    leave, units = refs[:-1], refs[-1]
    width = cots.shape[1]
    pieces = width // LANES
    part = start[...] + multiply([cut, across], cots, units)
    for p, out in enumerate([keep, *leave]):
        values = part[p * pad : p * pad + rows]
        if p:
            most = jnp.max(jnp.max(jnp.abs(values), axis=0, keepdims=True), axis=1, keepdims=True)
            exponent = jnp.ceil(jnp.log2(jnp.maximum(most, 2.0**-100)))
            values = values * jnp.exp2(-exponent)
            below = out.shape[0] - rows * pieces
            out[rows * pieces :] = jnp.broadcast_to(exponent, (below, LANES))
        for j in range(pieces):
            out[pl.ds(j, rows, stride=pieces), :] = values[:, j * LANES : (j + 1) * LANES]


def call(body, outs, args, fetched=(), scratch=(), limit=32, flops=1):
    vmem = pl.BlockSpec(memory_space=pltpu.VMEM)
    anywhere = pl.BlockSpec(memory_space=pl.ANY)
    return pl.pallas_call(
        body,
        out_shape=tuple(outs),
        in_specs=[anywhere if i in fetched else vmem for i in range(len(args))],
        out_specs=tuple([vmem] * len(outs)),
        scratch_shapes=list(scratch),
        compiler_params=pltpu.CompilerParams(vmem_limit_bytes=limit * 1024 * 1024),
        cost_estimate=pl.CostEstimate(flops=flops, bytes_accessed=1, transcendentals=0),
    )(*args)


def shards(grad_out, routes, route_weight, example_ids, example_weight, hidden):
    sources = lax.axis_size("expert")
    n_dp = lax.axis_size("dp")
    spread = n_dp // MATES
    tokens, width = grad_out.shape
    top = routes.shape[1]
    cap, ff = hidden.shape[3], hidden.shape[4]
    rows = ff // n_dp
    pad = -(-(rows + 4) // 16) * 16
    while spread * pad * sources % LANES:
        pad += 16
    across = spread * pad
    slots = sources * cap
    acts = hidden.reshape(sources, cap, ff)
    shape = jax.ShapeDtypeStruct

    def over_experts(array, k):
        return lax.ppermute(
            array, "expert", [(s, (s - k) % sources) for s in range(sources)]
        )

    def over_dp(array, k):
        return lax.ppermute(array, "dp", [(i, i ^ k) for i in range(n_dp)])

    def over_both(array, k):
        where = [(i, e) for i in range(n_dp) for e in range(sources)]
        pairs = [
            (i * sources + e, (i ^ 2) * sources + (e - k) % sources) for i, e in where
        ]
        return lax.ppermute(array, ("dp", "expert"), pairs)

    alone, block, *gives = call(
        lambda *refs: build(sources, cap, *refs),
        [shape((cap, width), BF16)] + [shape((cap, width + LANES), BF16)] * sources,
        (routes.T, route_weight.T, example_ids, example_weight, grad_out),
        fetched=range(5),
        limit=60,
        scratch=(
            pltpu.VMEM((top, tokens), jnp.int32),
            pltpu.VMEM((top, tokens), F32),
            pltpu.VMEM((1, tokens), jnp.int32),
            pltpu.SMEM((1, EXAMPLES), F32),
            pltpu.VMEM((tokens, width), BF16),
            pltpu.SemaphoreType.DMA((5,)),
        ),
    )
    takes = [over_experts(g, k + 1) for k, g in enumerate(gives)]
    block_across = over_dp(alone, 2)
    own, left, *cuts = call(
        lambda *refs: stage(sources, n_dp, pad, *refs),
        [shape((cap, width + LANES), BF16), shape((slots, slots), F32)]
        + [shape((cap, sources * across), BF16)] * MATES,
        (block, acts),
        flops=1,
    )
    (squares,) = call(
        lambda *refs: norms(sources, *refs),
        [shape((1, LANES), F32)],
        (left, own, *takes),
        flops=1 << 32,
    )
    (rest,) = call(
        lambda *refs: pass_on(rows, pad, *refs),
        [shape((slots - cap, width + sources * across), BF16)],
        (block_across, own, squares, cuts[2], *takes),
        fetched=(0,),
    )
    rest_across = over_dp(rest, 2)
    near_squares = [squares] + [over_experts(squares, k) for k in range(1, sources)]
    far_squares = [over_both(squares, k) for k in range(1, sources)]
    (cots,) = call(
        lambda *refs: pack(sources, ff * width, rows, pad, *refs),
        [shape((2 * slots, width), BF16)],
        (own, rest, block_across, rest_across, *near_squares, *far_squares),
    )
    other_cots = over_dp(cots, 1)
    (start,) = call(
        near_product,
        [shape((across, width), F32)],
        (cuts[0], rest_across, cots),
        scratch=(pltpu.VMEM((2 * slots, across), BF16),),
        flops=1 << 32,
    )

    held = rows * (width // LANES)
    sent = held + 8
    part, *leave = call(
        lambda *refs: product(rows, pad, *refs),
        [shape((held if p == 0 else sent, LANES), F32) for p in range(spread)],
        (start, over_dp(cuts[1], 1), over_dp(cuts[3], 3), other_cots),
        scratch=(pltpu.VMEM((2 * slots, across), BF16),),
    )
    for p in range(1, spread):
        got = over_dp(leave[p - 1].astype(jnp.float16), p * MATES).astype(F32)
        part = part + got[:held] * jnp.exp2(got[held : held + 1])
    return part.reshape(rows, 1, width)


def solution(mesh):
    placed = (
        P(("dp", "expert"), None),
        P(("dp", "expert"), None),
        P(("dp", "expert"), None),
        P("dp", "expert"),
        P("dp", None),
        P("dp", "expert", None, None, None),
    )
    return jax.shard_map(
        shards, mesh=mesh, in_specs=placed, out_specs=P("dp", "expert", None), check_vma=False
    )
```

```python
import jax
import jax.numpy as jnp
from jax import lax
from jax.experimental import pallas as pl
from jax.experimental.pallas import tpu as pltpu
from jax.sharding import PartitionSpec as P

EXAMPLES = 8
MATES = 4
LANES = 128
BF16 = jnp.bfloat16
F32 = jnp.float32


def iota(shape, axis):
    return lax.broadcasted_iota(jnp.int32, shape, axis)


def build(sources, cap, routes_at, weights_at, ids_at, loss_at, grad_at, *refs):
    blocks = refs[:sources]
    routes, weights, ids, loss, grad, sems = refs[sources:]
    fetches = [
        pltpu.make_async_copy(source, target, sems.at[i])
        for i, (source, target) in enumerate(
            [
                (routes_at, routes),
                (ids_at, ids),
                (loss_at, loss),
                (weights_at, weights),
                (grad_at, grad),
            ]
        )
    ]
    for fetch in fetches:
        fetch.start()
    me = lax.axis_index("expert")
    tokens, width = grad.shape
    before = (iota((tokens, tokens), 0) < iota((tokens, tokens), 1)).astype(F32).astype(BF16)
    slot = iota((cap, tokens), 0).astype(F32)
    fetches[0].wait()
    matches = [routes[...] == lax.rem(me + (sources - k), sources) for k in range(sources)]
    hits = [jnp.sum(jnp.where(m, 1.0, 0.0), axis=0, keepdims=True) for m in matches]
    blank = -(-sources // 8) * 8 - sources
    routed = jnp.concatenate(hits + [jnp.zeros((1, tokens), F32)] * blank, axis=0)
    ranking = jnp.dot(routed.astype(BF16), before, preferred_element_type=F32)
    for fetch in fetches[1:4]:
        fetch.wait()
    token_ids = ids[...]
    token_weight = jnp.zeros((1, tokens), F32)
    for x in range(EXAMPLES):
        token_weight = jnp.where(token_ids == x, loss[0, x], token_weight)
    token_code = (token_ids + 1).astype(F32)
    ready = []
    for k in range(sources):
        scale = jnp.sum(jnp.where(matches[k], weights[...], 0.0), axis=0, keepdims=True)
        scale = scale * token_weight
        placed = jnp.where(ranking[k : k + 1] == slot, hits[k], 0.0)
        slot_scale = jnp.sum(placed * scale, axis=1, keepdims=True)
        code = jnp.sum(placed * token_code, axis=1, keepdims=True)
        ready.append((placed.astype(BF16), slot_scale, code))
    fetches[4].wait()
    for k in range(sources):
        placed, slot_scale, code = ready[k]
        rows = jnp.dot(placed, grad[...], preferred_element_type=F32)
        rows = (rows * slot_scale).astype(BF16)
        blocks[k][:, :width] = rows
        blocks[k][:, width:] = jnp.broadcast_to(code, (cap, LANES)).astype(BF16)


def stage(sources, n_dp, pad, block, hidden, own, left, *cuts):
    own[...] = block[...]
    me, rank = lax.axis_index("expert"), lax.axis_index("dp")
    spread = n_dp // MATES
    cap, ff = hidden.shape[1:]
    rows = ff // n_dp
    high, low = rank // MATES, lax.rem(rank, MATES)
    column = iota((1, spread * pad), 1)
    wanted = jnp.full((1, spread * pad), -2 * ff, jnp.int32)
    for p in range(spread):
        inside = (column >= p * pad) & (column < p * pad + rows)
        wanted = jnp.where(inside, (high ^ p) * (MATES * rows) + column - p * pad, wanted)
    unit = iota((ff, spread * pad), 0)
    acts = [hidden[lax.rem(me + j, sources)] for j in range(sources)]
    acts = jnp.concatenate(acts, axis=0)
    left[...] = lax.dot_general(
        acts, acts, (((1,), (1,)), ((), ())), preferred_element_type=F32
    )
    for k in range(MATES):
        pick = jnp.where(unit == wanted + (low ^ k) * rows, 1.0, 0.0).astype(BF16)
        units = jnp.dot(acts, pick, preferred_element_type=F32).astype(BF16)
        for j in range(sources):
            at = slice(j * spread * pad, (j + 1) * spread * pad)
            cuts[k][:, at] = units[j * cap : (j + 1) * cap]


def chosen(codes):
    codes = jnp.broadcast_to(codes.astype(F32), (codes.shape[0], LANES))
    lane = iota(codes.shape, 1).astype(F32)
    return (codes == lane) & (codes > 0.0)


def norms(sources, left, own, *refs):
    takes, squares = refs[: sources - 1], refs[-1]
    width = own.shape[1] - LANES
    blocks = jnp.concatenate([own[...]] + [t[...] for t in takes], axis=0)
    cot = blocks[:, :width]
    member = jnp.where(chosen(blocks[:, width : width + 1]), 1.0, 0.0)
    last = (((1,), (1,)), ((), ()))
    right = lax.dot_general(cot, cot, last, preferred_element_type=F32)
    one_hot = member.astype(BF16)
    alike = lax.dot_general(one_hot, one_hot, last, preferred_element_type=F32)
    per_slot = jnp.sum(left[...] * right * alike, axis=1, keepdims=True)
    squares[...] = jnp.sum(per_slot * member, axis=0, keepdims=True)


def pass_on(across, squares, cut, *refs):
    takes, rest = refs[:-1], refs[-1]
    cap, wide = takes[0].shape
    half = LANES // 2
    for j, take in enumerate(takes):
        part = slice(j * cap, (j + 1) * cap)
        rest[part, :wide] = take[...]
        if j:
            rest[part, wide:] = jnp.zeros((cap, rest.shape[1] - wide), BF16)
    rest[:cap, wide:] = cut[...]
    value = jnp.broadcast_to(squares[...], (cap, LANES))
    high = value.astype(BF16).astype(F32)
    middle = (value - high).astype(BF16).astype(F32)
    low = value - high - middle
    row = iota((cap, LANES), 0)
    three = jnp.where(row == 0, high, jnp.where(row == 1, middle, low)).astype(BF16)
    rest[:cap, wide - half : wide] = three[:, :half]


def pack(sources, count, own, rest, across, rest_across, *refs):
    near, far, out = refs[:sources], refs[sources:-1], refs[-1]
    width = own.shape[1] - LANES
    half = LANES // 2
    three = rest_across[0:8, width + half : width + LANES].astype(F32)
    three = three[0:1] + three[1:2] + three[2:3]
    totals = [near[0][...], jnp.concatenate([three, jnp.zeros_like(three)], axis=1)]
    for k in range(1, sources):
        totals = [totals[0] + near[k][...], totals[1] + far[k - 1][...]]
    clips = [1.0 / jnp.maximum(jnp.sqrt(total / count), 1.0) for total in totals]
    at = 0
    for block, clip in ((own, clips[0]), (rest, clips[0]), (across, clips[1]), (rest_across, clips[1])):
        mine = chosen(block[:, width : width + 1])
        weight = jnp.sum(jnp.where(mine, clip, 0.0), axis=1, keepdims=True) / EXAMPLES
        scaled = (weight * block[:, :width].astype(F32)).astype(BF16)
        out[at : at + mine.shape[0]] = scaled
        at += mine.shape[0]


def multiply(cuts, cots, units):
    at, cap, across = 0, cuts[0].shape[0], units.shape[1]
    for cut in cuts:
        for j in range(cut.shape[1] // across):
            units[at : at + cap] = cut[:, j * across : (j + 1) * across]
            at += cap
    return lax.dot_general(
        units[...], cots[...], (((0,), (0,)), ((), ())), preferred_element_type=F32
    )


def near_product(cut, rest_across, cots, out, units):
    first = cots.shape[1] + LANES
    cap = cut.shape[0]
    across = rest_across.at[:cap, first : first + cut.shape[1]]
    out[...] = multiply([cut, across], cots, units)


def product(rows, pad, start, cut, across, cots, keep, *refs):
    leave, units = refs[:-1], refs[-1]
    width = cots.shape[1]
    pieces = width // LANES
    part = start[...] + multiply([cut, across], cots, units)
    leave = list(leave)
    for p in range(part.shape[0] // pad):
        values = part[p * pad : p * pad + rows]
        if p:
            most = jnp.max(jnp.max(jnp.abs(values), axis=0, keepdims=True), axis=1, keepdims=True)
            exponent = jnp.ceil(jnp.log2(jnp.maximum(most, 2.0**-100)))
            values = values * jnp.exp2(-exponent)
        done = 0
        for out in [keep] if p == 0 else [leave.pop(0) for _ in range(1 if p == 1 else 2)]:
            held = out.shape[0] if p == 0 else out.shape[0] - 8
            count = held // pieces
            for j in range(pieces):
                out[pl.ds(j, count, stride=pieces), :] = values[
                    done : done + count, j * LANES : (j + 1) * LANES
                ]
            if p:
                out[held:] = jnp.broadcast_to(exponent, (8, LANES))
            done += count


def call(body, outs, args, fetched=(), scratch=(), limit=32, flops=1):
    vmem = pl.BlockSpec(memory_space=pltpu.VMEM)
    anywhere = pl.BlockSpec(memory_space=pl.ANY)
    return pl.pallas_call(
        body,
        out_shape=tuple(outs),
        in_specs=[anywhere if i in fetched else vmem for i in range(len(args))],
        out_specs=tuple([vmem] * len(outs)),
        scratch_shapes=list(scratch),
        compiler_params=pltpu.CompilerParams(vmem_limit_bytes=limit * 1024 * 1024),
        cost_estimate=pl.CostEstimate(flops=flops, bytes_accessed=1, transcendentals=0),
    )(*args)


def shards(grad_out, routes, route_weight, example_ids, example_weight, hidden):
    sources = lax.axis_size("expert")
    n_dp = lax.axis_size("dp")
    spread = n_dp // MATES
    tokens, width = grad_out.shape
    top = routes.shape[1]
    cap, ff = hidden.shape[3], hidden.shape[4]
    rows = ff // n_dp
    pad = -(-(rows + 1) // 16) * 16
    while spread * pad * sources % LANES:
        pad += 16
    across = spread * pad
    slots = sources * cap
    acts = hidden.reshape(sources, cap, ff)
    shape = jax.ShapeDtypeStruct

    def over_experts(array, k):
        return lax.ppermute(
            array, "expert", [(s, (s - k) % sources) for s in range(sources)]
        )

    def over_dp(array, k):
        return lax.ppermute(array, "dp", [(i, i ^ k) for i in range(n_dp)])

    def over_both(array, k):
        where = [(i, e) for i in range(n_dp) for e in range(sources)]
        pairs = [
            (i * sources + e, (i ^ 2) * sources + (e - k) % sources) for i, e in where
        ]
        return lax.ppermute(array, ("dp", "expert"), pairs)

    block, *gives = call(
        lambda *refs: build(sources, cap, *refs),
        [shape((cap, width + LANES), BF16)] * sources,
        (routes.T, route_weight.T, example_ids, example_weight, grad_out),
        fetched=range(5),
        limit=60,
        scratch=(
            pltpu.VMEM((top, tokens), jnp.int32),
            pltpu.VMEM((top, tokens), F32),
            pltpu.VMEM((1, tokens), jnp.int32),
            pltpu.SMEM((1, EXAMPLES), F32),
            pltpu.VMEM((tokens, width), BF16),
            pltpu.SemaphoreType.DMA((5,)),
        ),
    )
    takes = [over_experts(g, k + 1) for k, g in enumerate(gives)]
    block_across = over_dp(block, 2)
    own, left, *cuts = call(
        lambda *refs: stage(sources, n_dp, pad, *refs),
        [shape((cap, width + LANES), BF16), shape((slots, slots), F32)]
        + [shape((cap, sources * across), BF16)] * MATES,
        (block, acts),
        flops=1 << 32,
    )
    (squares,) = call(
        lambda *refs: norms(sources, *refs),
        [shape((1, LANES), F32)],
        (left, own, *takes),
        flops=1 << 32,
    )
    (rest,) = call(
        pass_on,
        [shape((slots - cap, width + LANES + sources * across), BF16)],
        (block_across, squares, cuts[2], *takes),
        fetched=(0,),
    )
    rest_across = over_dp(rest, 2)
    near_squares = [squares] + [over_experts(squares, k) for k in range(1, sources)]
    far_squares = [over_both(squares, k) for k in range(1, sources)]
    (cots,) = call(
        lambda *refs: pack(sources, ff * width, *refs),
        [shape((2 * slots, width), BF16)],
        (own, rest, block_across, rest_across, *near_squares, *far_squares),
    )
    other_cots = over_dp(cots, 1)
    (start,) = call(
        near_product,
        [shape((across, width), F32)],
        (cuts[0], rest_across, cots),
        scratch=(pltpu.VMEM((2 * slots, across), BF16),),
        flops=1 << 32,
    )

    held = rows * (width // LANES)
    pieces = width // LANES
    upper = rows // 2 * pieces
    lower = held - upper
    sizes = [held, held + 8] + [upper + 8, lower + 8] * (spread - 2)
    part, *leave = call(
        lambda *refs: product(rows, pad, *refs),
        [shape((size, LANES), F32) for size in sizes],
        (start, over_dp(cuts[1], 1), over_dp(cuts[3], 3), other_cots),
        scratch=(pltpu.VMEM((2 * slots, across), BF16),),
    )
    uppers, lowers = [None, None] + leave[1::2], [None, None] + leave[2::2]

    def over_spread(array, p):
        return over_dp(array.astype(jnp.float16), p * MATES).astype(F32)

    def value(array):
        return array[:-8] * jnp.exp2(array[-8:-7])

    sums = {}
    for p in range(2, spread, 2):
        got = over_spread(lowers[p + 1], 1)
        top = jnp.maximum(got[-8:-7], lowers[p][-8:-7])
        added = got[:-8] * jnp.exp2(got[-8:-7] - top)
        added = added + lowers[p][:-8] * jnp.exp2(lowers[p][-8:-7] - top)
        sums[p] = jnp.concatenate([added, jnp.broadcast_to(top, (8, LANES))], axis=0)
    come = sum(value(over_spread(uppers[p], p)) for p in range(spread - 1, 1, -1))
    come_lower = sum(value(over_spread(sums[p], p)) for p in sums)
    come = jnp.concatenate([come, come_lower], axis=0)
    part = part + value(over_spread(leave[0], 1)) + come
    return part.reshape(rows, 1, width)


def solution(mesh):
    placed = (
        P(("dp", "expert"), None),
        P(("dp", "expert"), None),
        P(("dp", "expert"), None),
        P("dp", "expert"),
        P("dp", None),
        P("dp", "expert", None, None, None),
    )
    return jax.shard_map(
        shards, mesh=mesh, in_specs=placed, out_specs=P("dp", "expert", None), check_vma=False
    )
```

```python
import jax
import jax.numpy as jnp
from jax import lax
from jax.experimental import pallas as pl
from jax.experimental.pallas import tpu as pltpu
from jax.sharding import PartitionSpec as P

EXAMPLES = 8
MATES = 4
LANES = 128
BF16 = jnp.bfloat16
F32 = jnp.float32


def iota(shape, axis):
    return lax.broadcasted_iota(jnp.int32, shape, axis)


def build(sources, cap, routes_at, weights_at, ids_at, loss_at, grad_at, *refs):
    blocks = refs[:sources]
    routes, weights, ids, loss, grad, sems = refs[sources:]
    fetches = [
        pltpu.make_async_copy(source, target, sems.at[i])
        for i, (source, target) in enumerate(
            [
                (routes_at, routes),
                (ids_at, ids),
                (loss_at, loss),
                (weights_at, weights),
                (grad_at, grad),
            ]
        )
    ]
    for fetch in fetches:
        fetch.start()
    me = lax.axis_index("expert")
    tokens, width = grad.shape
    before = (iota((tokens, tokens), 0) < iota((tokens, tokens), 1)).astype(F32).astype(BF16)
    slot = iota((cap, tokens), 0).astype(F32)
    fetches[0].wait()
    matches = [routes[...] == lax.rem(me + (sources - k), sources) for k in range(sources)]
    hits = [jnp.sum(jnp.where(m, 1.0, 0.0), axis=0, keepdims=True) for m in matches]
    blank = -(-sources // 8) * 8 - sources
    routed = jnp.concatenate(hits + [jnp.zeros((1, tokens), F32)] * blank, axis=0)
    ranking = jnp.dot(routed.astype(BF16), before, preferred_element_type=F32)
    for fetch in fetches[1:4]:
        fetch.wait()
    token_ids = ids[...]
    token_weight = jnp.zeros((1, tokens), F32)
    for x in range(EXAMPLES):
        token_weight = jnp.where(token_ids == x, loss[0, x], token_weight)
    token_code = (token_ids + 1).astype(F32)
    ready = []
    for k in range(sources):
        scale = jnp.sum(jnp.where(matches[k], weights[...], 0.0), axis=0, keepdims=True)
        scale = scale * token_weight
        placed = jnp.where(ranking[k : k + 1] == slot, hits[k], 0.0)
        slot_scale = jnp.sum(placed * scale, axis=1, keepdims=True)
        code = jnp.sum(placed * token_code, axis=1, keepdims=True)
        ready.append((placed.astype(BF16), slot_scale, code))
    fetches[4].wait()
    for k in range(sources):
        placed, slot_scale, code = ready[k]
        rows = jnp.dot(placed, grad[...], preferred_element_type=F32)
        rows = (rows * slot_scale).astype(BF16)
        blocks[k][:, :width] = rows
        blocks[k][:, width:] = jnp.broadcast_to(code, (cap, LANES)).astype(BF16)


def stage(sources, n_dp, pad, block, hidden, own, left, *cuts):
    own[...] = block[...]
    me, rank = lax.axis_index("expert"), lax.axis_index("dp")
    spread = n_dp // MATES
    cap, ff = hidden.shape[1:]
    rows = ff // n_dp
    high, low = rank // MATES, lax.rem(rank, MATES)
    column = iota((1, spread * pad), 1)
    wanted = jnp.full((1, spread * pad), -2 * ff, jnp.int32)
    for p in range(spread):
        inside = (column >= p * pad) & (column < p * pad + rows)
        wanted = jnp.where(inside, (high ^ p) * (MATES * rows) + column - p * pad, wanted)
    unit = iota((ff, spread * pad), 0)
    acts = [hidden[lax.rem(me + j, sources)] for j in range(sources)]
    acts = jnp.concatenate(acts, axis=0)
    left[...] = lax.dot_general(
        acts, acts, (((1,), (1,)), ((), ())), preferred_element_type=F32
    )
    for k in range(MATES):
        pick = jnp.where(unit == wanted + (low ^ k) * rows, 1.0, 0.0).astype(BF16)
        units = jnp.dot(acts, pick, preferred_element_type=F32).astype(BF16)
        for j in range(sources):
            at = slice(j * spread * pad, (j + 1) * spread * pad)
            cuts[k][:, at] = units[j * cap : (j + 1) * cap]


def chosen(codes):
    codes = jnp.broadcast_to(codes.astype(F32), (codes.shape[0], LANES))
    lane = iota(codes.shape, 1).astype(F32)
    return (codes == lane) & (codes > 0.0)


def norms(sources, left, own, *refs):
    takes, squares = refs[: sources - 1], refs[-1]
    width = own.shape[1] - LANES
    blocks = jnp.concatenate([own[...]] + [t[...] for t in takes], axis=0)
    cot = blocks[:, :width]
    member = jnp.where(chosen(blocks[:, width : width + 1]), 1.0, 0.0)
    last = (((1,), (1,)), ((), ()))
    right = lax.dot_general(cot, cot, last, preferred_element_type=F32)
    one_hot = member.astype(BF16)
    alike = lax.dot_general(one_hot, one_hot, last, preferred_element_type=F32)
    per_slot = jnp.sum(left[...] * right * alike, axis=1, keepdims=True)
    squares[...] = jnp.sum(per_slot * member, axis=0, keepdims=True)


def pass_on(across, squares, cut, *refs):
    takes, rest = refs[:-1], refs[-1]
    cap, wide = takes[0].shape
    half = LANES // 2
    for j, take in enumerate(takes):
        part = slice(j * cap, (j + 1) * cap)
        rest[part, :wide] = take[...]
        if j:
            rest[part, wide:] = jnp.zeros((cap, rest.shape[1] - wide), BF16)
    rest[:cap, wide:] = cut[...]
    value = jnp.broadcast_to(squares[...], (cap, LANES))
    high = value.astype(BF16).astype(F32)
    middle = (value - high).astype(BF16).astype(F32)
    low = value - high - middle
    row = iota((cap, LANES), 0)
    three = jnp.where(row == 0, high, jnp.where(row == 1, middle, low)).astype(BF16)
    rest[:cap, wide - half : wide] = three[:, :half]


def pack(sources, count, own, rest, across, rest_across, *refs):
    near, far, out = refs[:sources], refs[sources:-1], refs[-1]
    width = own.shape[1] - LANES
    half = LANES // 2
    three = rest_across[0:8, width + half : width + LANES].astype(F32)
    three = three[0:1] + three[1:2] + three[2:3]
    totals = [near[0][...], jnp.concatenate([three, jnp.zeros_like(three)], axis=1)]
    for k in range(1, sources):
        totals = [totals[0] + near[k][...], totals[1] + far[k - 1][...]]
    clips = [1.0 / jnp.maximum(jnp.sqrt(total / count), 1.0) for total in totals]
    at = 0
    for block, clip in ((own, clips[0]), (rest, clips[0]), (across, clips[1]), (rest_across, clips[1])):
        mine = chosen(block[:, width : width + 1])
        weight = jnp.sum(jnp.where(mine, clip, 0.0), axis=1, keepdims=True) / EXAMPLES
        scaled = (weight * block[:, :width].astype(F32)).astype(BF16)
        out[at : at + mine.shape[0]] = scaled
        at += mine.shape[0]


def multiply(cuts, cots, units):
    at, cap, across = 0, cuts[0].shape[0], units.shape[1]
    for cut in cuts:
        for j in range(cut.shape[1] // across):
            units[at : at + cap] = cut[:, j * across : (j + 1) * across]
            at += cap
    return lax.dot_general(
        units[...], cots[...], (((0,), (0,)), ((), ())), preferred_element_type=F32
    )


def near_product(cut, rest_across, cots, out, units):
    first = cots.shape[1] + LANES
    cap = cut.shape[0]
    across = rest_across.at[:cap, first : first + cut.shape[1]]
    out[...] = multiply([cut, across], cots, units)


def store(out, first, values, exponent=None):
    pieces = values.shape[1] // LANES
    for j in range(pieces):
        out[pl.ds(first + j, values.shape[0], stride=pieces), :] = values[
            :, j * LANES : (j + 1) * LANES
        ]
    if exponent is not None:
        end = first + values.shape[0] * pieces
        out[end : end + 8] = jnp.broadcast_to(exponent, (8, LANES))


def product(rows, pad, start, cut, across, cots, keep, joint, *refs):
    leave, units = list(refs[:-1]), refs[-1]
    pieces = start.shape[1] // LANES
    upper = rows // 2
    part = start[...] + multiply([cut, across], cots, units)
    store(keep, 0, part[:rows])
    at = 0
    for p in range(1, part.shape[0] // pad):
        values = part[p * pad : p * pad + rows]
        most = jnp.max(jnp.max(jnp.abs(values), axis=0, keepdims=True), axis=1, keepdims=True)
        exponent = jnp.ceil(jnp.log2(jnp.maximum(most, 2.0**-100)))
        values = values * jnp.exp2(-exponent)
        if p > 1:
            store(leave.pop(0), 0, values[:upper], exponent)
            values = values[upper:]
        if p % 2:
            store(joint, at, values, exponent)
            at += values.shape[0] * pieces + 8
        else:
            store(leave.pop(0), 0, values, exponent)


def call(body, outs, args, fetched=(), scratch=(), limit=32, flops=1):
    vmem = pl.BlockSpec(memory_space=pltpu.VMEM)
    anywhere = pl.BlockSpec(memory_space=pl.ANY)
    return pl.pallas_call(
        body,
        out_shape=tuple(outs),
        in_specs=[anywhere if i in fetched else vmem for i in range(len(args))],
        out_specs=tuple([vmem] * len(outs)),
        scratch_shapes=list(scratch),
        compiler_params=pltpu.CompilerParams(vmem_limit_bytes=limit * 1024 * 1024),
        cost_estimate=pl.CostEstimate(flops=flops, bytes_accessed=1, transcendentals=0),
    )(*args)


def shards(grad_out, routes, route_weight, example_ids, example_weight, hidden):
    sources = lax.axis_size("expert")
    n_dp = lax.axis_size("dp")
    spread = n_dp // MATES
    tokens, width = grad_out.shape
    top = routes.shape[1]
    cap, ff = hidden.shape[3], hidden.shape[4]
    rows = ff // n_dp
    pad = -(-(rows + 1) // 16) * 16
    while spread * pad * sources % LANES:
        pad += 16
    across = spread * pad
    slots = sources * cap
    acts = hidden.reshape(sources, cap, ff)
    shape = jax.ShapeDtypeStruct

    def over_experts(array, k):
        return lax.ppermute(
            array, "expert", [(s, (s - k) % sources) for s in range(sources)]
        )

    def over_dp(array, k):
        return lax.ppermute(array, "dp", [(i, i ^ k) for i in range(n_dp)])

    def over_both(array, k):
        where = [(i, e) for i in range(n_dp) for e in range(sources)]
        pairs = [
            (i * sources + e, (i ^ 2) * sources + (e - k) % sources) for i, e in where
        ]
        return lax.ppermute(array, ("dp", "expert"), pairs)

    block, *gives = call(
        lambda *refs: build(sources, cap, *refs),
        [shape((cap, width + LANES), BF16)] * sources,
        (routes.T, route_weight.T, example_ids, example_weight, grad_out),
        fetched=range(5),
        limit=60,
        scratch=(
            pltpu.VMEM((top, tokens), jnp.int32),
            pltpu.VMEM((top, tokens), F32),
            pltpu.VMEM((1, tokens), jnp.int32),
            pltpu.SMEM((1, EXAMPLES), F32),
            pltpu.VMEM((tokens, width), BF16),
            pltpu.SemaphoreType.DMA((5,)),
        ),
    )
    takes = [over_experts(g, k + 1) for k, g in enumerate(gives)]
    block_across = over_dp(block, 2)
    own, left, *cuts = call(
        lambda *refs: stage(sources, n_dp, pad, *refs),
        [shape((cap, width + LANES), BF16), shape((slots, slots), F32)]
        + [shape((cap, sources * across), BF16)] * MATES,
        (block, acts),
        flops=1 << 32,
    )
    (squares,) = call(
        lambda *refs: norms(sources, *refs),
        [shape((1, LANES), F32)],
        (left, own, *takes),
        flops=1 << 32,
    )
    (rest,) = call(
        pass_on,
        [shape((slots - cap, width + LANES + sources * across), BF16)],
        (block_across, squares, cuts[2], *takes),
        fetched=(0,),
    )
    rest_across = over_dp(rest, 2)
    near_squares = [squares] + [over_experts(squares, k) for k in range(1, sources)]
    far_squares = [over_both(squares, k) for k in range(1, sources)]
    (cots,) = call(
        lambda *refs: pack(sources, ff * width, *refs),
        [shape((2 * slots, width), BF16)],
        (own, rest, block_across, rest_across, *near_squares, *far_squares),
    )
    other_cots = over_dp(cots, 1)
    (start,) = call(
        near_product,
        [shape((across, width), F32)],
        (cuts[0], rest_across, cots),
        scratch=(pltpu.VMEM((2 * slots, across), BF16),),
        flops=1 << 32,
    )

    held = rows * (width // LANES)
    pieces = width // LANES
    upper = rows // 2 * pieces
    lower = held - upper
    pairs = spread // 2 - 1
    sizes = [held, held + 8 + pairs * (lower + 8)] + [upper + 8, lower + 8, upper + 8] * pairs
    part, joint, *leave = call(
        lambda *refs: product(rows, pad, *refs),
        [shape((size, LANES), F32) for size in sizes],
        (start, over_dp(cuts[1], 1), over_dp(cuts[3], 3), other_cots),
        scratch=(pltpu.VMEM((2 * slots, across), BF16),),
    )
    uppers = {p: leave[p // 2 * 3 - 3 + p % 2 * 2] for p in range(2, spread)}
    lowers = {p: leave[p // 2 * 3 - 2] for p in range(2, spread, 2)}

    def over_spread(array, p):
        return over_dp(array.astype(jnp.float16), p * MATES)

    def value(array):
        return array[:-8] * jnp.exp2(array[-8:-7])

    near = over_spread(joint, 1).astype(F32)
    sums = {}
    for p in range(2, spread, 2):
        got = near[held + 8 :][(p // 2 - 1) * (lower + 8) : p // 2 * (lower + 8)]
        top = jnp.maximum(got[-8:-7], lowers[p][-8:-7])
        added = got[:-8] * jnp.exp2(got[-8:-7] - top)
        added = added + lowers[p][:-8] * jnp.exp2(lowers[p][-8:-7] - top)
        sums[p] = jnp.concatenate([added, jnp.broadcast_to(top, (8, LANES))], axis=0)
    come = [over_spread(sums[p], p) for p in sums]
    come += [over_spread(uppers[p], p) for p in range(spread - 1, 1, -1)]
    halves = [value(array.astype(F32)) for array in lax.optimization_barrier(come)]
    lower_sum, upper_sum = sum(halves[: len(sums)]), sum(halves[len(sums) :])
    part = part + value(near[: held + 8]) + jnp.concatenate([upper_sum, lower_sum], axis=0)
    return part.reshape(rows, 1, width)


def solution(mesh):
    placed = (
        P(("dp", "expert"), None),
        P(("dp", "expert"), None),
        P(("dp", "expert"), None),
        P("dp", "expert"),
        P("dp", None),
        P("dp", "expert", None, None, None),
    )
    return jax.shard_map(
        shards, mesh=mesh, in_specs=placed, out_specs=P("dp", "expert", None), check_vma=False
    )
```

```python
import jax
import jax.numpy as jnp
from jax import lax
from jax.experimental import pallas as pl
from jax.experimental.pallas import tpu as pltpu
from jax.sharding import PartitionSpec as P

EXAMPLES = 8
MATES = 4
LANES = 128
BF16 = jnp.bfloat16
F32 = jnp.float32


def iota(shape, axis):
    return lax.broadcasted_iota(jnp.int32, shape, axis)


def build(sources, cap, routes_at, weights_at, ids_at, loss_at, grad_at, *refs):
    blocks = refs[:sources]
    routes, weights, ids, loss, grad, sems = refs[sources:]
    fetches = [
        pltpu.make_async_copy(source, target, sems.at[i])
        for i, (source, target) in enumerate(
            [
                (routes_at, routes),
                (ids_at, ids),
                (loss_at, loss),
                (weights_at, weights),
                (grad_at, grad),
            ]
        )
    ]
    for fetch in fetches:
        fetch.start()
    me = lax.axis_index("expert")
    tokens, width = grad.shape
    before = (iota((tokens, tokens), 0) < iota((tokens, tokens), 1)).astype(F32).astype(BF16)
    slot = iota((cap, tokens), 0).astype(F32)
    fetches[0].wait()
    matches = [routes[...] == lax.rem(me + (sources - k), sources) for k in range(sources)]
    hits = [jnp.sum(jnp.where(m, 1.0, 0.0), axis=0, keepdims=True) for m in matches]
    blank = -(-sources // 8) * 8 - sources
    routed = jnp.concatenate(hits + [jnp.zeros((1, tokens), F32)] * blank, axis=0)
    ranking = jnp.dot(routed.astype(BF16), before, preferred_element_type=F32)
    for fetch in fetches[1:4]:
        fetch.wait()
    token_ids = ids[...]
    token_weight = jnp.zeros((1, tokens), F32)
    for x in range(EXAMPLES):
        token_weight = jnp.where(token_ids == x, loss[0, x], token_weight)
    token_code = (token_ids + 1).astype(F32)
    ready = []
    for k in range(sources):
        scale = jnp.sum(jnp.where(matches[k], weights[...], 0.0), axis=0, keepdims=True)
        scale = scale * token_weight
        placed = jnp.where(ranking[k : k + 1] == slot, hits[k], 0.0)
        slot_scale = jnp.sum(placed * scale, axis=1, keepdims=True)
        code = jnp.sum(placed * token_code, axis=1, keepdims=True)
        ready.append((placed.astype(BF16), slot_scale, code))
    fetches[4].wait()
    for k in range(sources):
        placed, slot_scale, code = ready[k]
        rows = jnp.dot(placed, grad[...], preferred_element_type=F32)
        rows = (rows * slot_scale).astype(BF16)
        blocks[k][:, :width] = rows
        blocks[k][:, width:] = jnp.broadcast_to(code, (cap, LANES)).astype(BF16)


def stage(sources, n_dp, pad, block, hidden, own, left, *cuts):
    own[...] = block[...]
    me, rank = lax.axis_index("expert"), lax.axis_index("dp")
    spread = n_dp // MATES
    cap, ff = hidden.shape[1:]
    rows = ff // n_dp
    high, low = rank // MATES, lax.rem(rank, MATES)
    column = iota((1, spread * pad), 1)
    wanted = jnp.full((1, spread * pad), -2 * ff, jnp.int32)
    for p in range(spread):
        inside = (column >= p * pad) & (column < p * pad + rows)
        wanted = jnp.where(inside, (high ^ p) * (MATES * rows) + column - p * pad, wanted)
    unit = iota((ff, spread * pad), 0)
    acts = [hidden[lax.rem(me + j, sources)] for j in range(sources)]
    acts = jnp.concatenate(acts, axis=0)
    left[...] = lax.dot_general(
        acts, acts, (((1,), (1,)), ((), ())), preferred_element_type=F32
    )
    for k in range(MATES):
        pick = jnp.where(unit == wanted + (low ^ k) * rows, 1.0, 0.0).astype(BF16)
        units = jnp.dot(acts, pick, preferred_element_type=F32).astype(BF16)
        for j in range(sources):
            at = slice(j * spread * pad, (j + 1) * spread * pad)
            cuts[k][:, at] = units[j * cap : (j + 1) * cap]


def chosen(codes):
    codes = jnp.broadcast_to(codes.astype(F32), (codes.shape[0], LANES))
    lane = iota(codes.shape, 1).astype(F32)
    return (codes == lane) & (codes > 0.0)


def norms(sources, left, own, *refs):
    takes, squares = refs[: sources - 1], refs[-1]
    width = own.shape[1] - LANES
    blocks = jnp.concatenate([own[...]] + [t[...] for t in takes], axis=0)
    cot = blocks[:, :width]
    member = jnp.where(chosen(blocks[:, width : width + 1]), 1.0, 0.0)
    last = (((1,), (1,)), ((), ()))
    right = lax.dot_general(cot, cot, last, preferred_element_type=F32)
    one_hot = member.astype(BF16)
    alike = lax.dot_general(one_hot, one_hot, last, preferred_element_type=F32)
    per_slot = jnp.sum(left[...] * right * alike, axis=1, keepdims=True)
    squares[...] = jnp.sum(per_slot * member, axis=0, keepdims=True)


def pass_on(across, squares, cut, *refs):
    takes, rest = refs[:-1], refs[-1]
    cap, wide = takes[0].shape
    half = LANES // 2
    for j, take in enumerate(takes):
        part = slice(j * cap, (j + 1) * cap)
        rest[part, :wide] = take[...]
        if j:
            rest[part, wide:] = jnp.zeros((cap, rest.shape[1] - wide), BF16)
    rest[:cap, wide:] = cut[...]
    value = jnp.broadcast_to(squares[...], (cap, LANES))
    high = value.astype(BF16).astype(F32)
    middle = (value - high).astype(BF16).astype(F32)
    low = value - high - middle
    row = iota((cap, LANES), 0)
    three = jnp.where(row == 0, high, jnp.where(row == 1, middle, low)).astype(BF16)
    rest[:cap, wide - half : wide] = three[:, :half]


def pack(sources, count, own, rest, across, rest_across, *refs):
    near, far, out = refs[:sources], refs[sources:-1], refs[-1]
    width = own.shape[1] - LANES
    half = LANES // 2
    three = rest_across[0:8, width + half : width + LANES].astype(F32)
    three = three[0:1] + three[1:2] + three[2:3]
    totals = [near[0][...], jnp.concatenate([three, jnp.zeros_like(three)], axis=1)]
    for k in range(1, sources):
        totals = [totals[0] + near[k][...], totals[1] + far[k - 1][...]]
    clips = [1.0 / jnp.maximum(jnp.sqrt(total / count), 1.0) for total in totals]
    at = 0
    for block, clip in ((own, clips[0]), (rest, clips[0]), (across, clips[1]), (rest_across, clips[1])):
        mine = chosen(block[:, width : width + 1])
        weight = jnp.sum(jnp.where(mine, clip, 0.0), axis=1, keepdims=True) / EXAMPLES
        scaled = (weight * block[:, :width].astype(F32)).astype(BF16)
        out[at : at + mine.shape[0]] = scaled
        at += mine.shape[0]


def multiply(cuts, cots, units):
    at, cap, across = 0, cuts[0].shape[0], units.shape[1]
    for cut in cuts:
        for j in range(cut.shape[1] // across):
            units[at : at + cap] = cut[:, j * across : (j + 1) * across]
            at += cap
    return lax.dot_general(
        units[...], cots[...], (((0,), (0,)), ((), ())), preferred_element_type=F32
    )


def near_product(cut, rest_across, cots, out, units):
    first = cots.shape[1] + LANES
    cap = cut.shape[0]
    across = rest_across.at[:cap, first : first + cut.shape[1]]
    out[...] = multiply([cut, across], cots, units)


def product(rows, pad, start, cut, across, cots, keep, *refs):
    leave, units = refs[:-1], refs[-1]
    width = cots.shape[1]
    pieces = width // LANES
    part = start[...] + multiply([cut, across], cots, units)
    leave = list(leave)
    for p in range(part.shape[0] // pad):
        values = part[p * pad : p * pad + rows]
        if p:
            most = jnp.max(jnp.max(jnp.abs(values), axis=0, keepdims=True), axis=1, keepdims=True)
            exponent = jnp.ceil(jnp.log2(jnp.maximum(most, 2.0**-100)))
            values = values * jnp.exp2(-exponent)
        done = 0
        for out in [keep] if p == 0 else [leave.pop(0) for _ in range(1 if p == 1 else 2)]:
            held = out.shape[0] if p == 0 else out.shape[0] - 8
            count = held // pieces
            for j in range(pieces):
                out[pl.ds(j, count, stride=pieces), :] = values[
                    done : done + count, j * LANES : (j + 1) * LANES
                ]
            if p:
                out[held:] = jnp.broadcast_to(exponent, (8, LANES))
            done += count


def call(body, outs, args, fetched=(), scratch=(), limit=32, flops=1):
    vmem = pl.BlockSpec(memory_space=pltpu.VMEM)
    anywhere = pl.BlockSpec(memory_space=pl.ANY)
    return pl.pallas_call(
        body,
        out_shape=tuple(outs),
        in_specs=[anywhere if i in fetched else vmem for i in range(len(args))],
        out_specs=tuple([vmem] * len(outs)),
        scratch_shapes=list(scratch),
        compiler_params=pltpu.CompilerParams(vmem_limit_bytes=limit * 1024 * 1024),
        cost_estimate=pl.CostEstimate(flops=flops, bytes_accessed=1, transcendentals=0),
    )(*args)


def shards(grad_out, routes, route_weight, example_ids, example_weight, hidden):
    sources = lax.axis_size("expert")
    n_dp = lax.axis_size("dp")
    spread = n_dp // MATES
    tokens, width = grad_out.shape
    top = routes.shape[1]
    cap, ff = hidden.shape[3], hidden.shape[4]
    rows = ff // n_dp
    pad = -(-(rows + 1) // 16) * 16
    while spread * pad * sources % LANES:
        pad += 16
    across = spread * pad
    slots = sources * cap
    acts = hidden.reshape(sources, cap, ff)
    shape = jax.ShapeDtypeStruct

    def over_experts(array, k):
        return lax.ppermute(
            array, "expert", [(s, (s - k) % sources) for s in range(sources)]
        )

    def over_dp(array, k):
        return lax.ppermute(array, "dp", [(i, i ^ k) for i in range(n_dp)])

    def over_both(array, k):
        where = [(i, e) for i in range(n_dp) for e in range(sources)]
        pairs = [
            (i * sources + e, (i ^ 2) * sources + (e - k) % sources) for i, e in where
        ]
        return lax.ppermute(array, ("dp", "expert"), pairs)

    block, *gives = call(
        lambda *refs: build(sources, cap, *refs),
        [shape((cap, width + LANES), BF16)] * sources,
        (routes.T, route_weight.T, example_ids, example_weight, grad_out),
        fetched=range(5),
        limit=60,
        scratch=(
            pltpu.VMEM((top, tokens), jnp.int32),
            pltpu.VMEM((top, tokens), F32),
            pltpu.VMEM((1, tokens), jnp.int32),
            pltpu.SMEM((1, EXAMPLES), F32),
            pltpu.VMEM((tokens, width), BF16),
            pltpu.SemaphoreType.DMA((5,)),
        ),
    )
    takes = [over_experts(g, k + 1) for k, g in enumerate(gives)]
    block_across = over_dp(block, 2)
    own, left, *cuts = call(
        lambda *refs: stage(sources, n_dp, pad, *refs),
        [shape((cap, width + LANES), BF16), shape((slots, slots), F32)]
        + [shape((cap, sources * across), BF16)] * MATES,
        (block, acts),
        flops=1 << 32,
    )
    (squares,) = call(
        lambda *refs: norms(sources, *refs),
        [shape((1, LANES), F32)],
        (left, own, *takes),
        flops=1 << 32,
    )
    (rest,) = call(
        pass_on,
        [shape((slots - cap, width + LANES + sources * across), BF16)],
        (block_across, squares, cuts[2], *takes),
        fetched=(0,),
    )
    rest_across = over_dp(rest, 2)
    near_squares = [squares] + [over_experts(squares, k) for k in range(1, sources)]
    far_squares = [over_both(squares, k) for k in range(1, sources)]
    (cots,) = call(
        lambda *refs: pack(sources, ff * width, *refs),
        [shape((2 * slots, width), BF16)],
        (own, rest, block_across, rest_across, *near_squares, *far_squares),
    )
    other_cots = over_dp(cots, 1)
    (start,) = call(
        near_product,
        [shape((across, width), F32)],
        (cuts[0], rest_across, cots),
        scratch=(pltpu.VMEM((2 * slots, across), BF16),),
        flops=1 << 32,
    )

    held = rows * (width // LANES)
    pieces = width // LANES
    upper = (rows - rows // 3) * pieces
    lower = held - upper
    sizes = [held, held + 8] + [upper + 8, lower + 8] * (spread - 2)
    part, *leave = call(
        lambda *refs: product(rows, pad, *refs),
        [shape((size, LANES), F32) for size in sizes],
        (start, over_dp(cuts[1], 1), over_dp(cuts[3], 3), other_cots),
        scratch=(pltpu.VMEM((2 * slots, across), BF16),),
    )
    uppers, lowers = [None, None] + leave[1::2], [None, None] + leave[2::2]

    def over_spread(array, p):
        return over_dp(array.astype(jnp.float16), p * MATES).astype(F32)

    def value(array):
        return array[:-8] * jnp.exp2(array[-8:-7])

    sums = {}
    for p in range(2, spread, 2):
        got = over_spread(lowers[p + 1], 1)
        top = jnp.maximum(got[-8:-7], lowers[p][-8:-7])
        added = got[:-8] * jnp.exp2(got[-8:-7] - top)
        added = added + lowers[p][:-8] * jnp.exp2(lowers[p][-8:-7] - top)
        sums[p] = jnp.concatenate([added, jnp.broadcast_to(top, (8, LANES))], axis=0)
    come = sum(value(over_spread(uppers[p], p)) for p in range(spread - 1, 1, -1))
    come_lower = sum(value(over_spread(sums[p], p)) for p in sums)
    come = jnp.concatenate([come, come_lower], axis=0)
    part = part + value(over_spread(leave[0], 1)) + come
    return part.reshape(rows, 1, width)


def solution(mesh):
    placed = (
        P(("dp", "expert"), None),
        P(("dp", "expert"), None),
        P(("dp", "expert"), None),
        P("dp", "expert"),
        P("dp", None),
        P("dp", "expert", None, None, None),
    )
    return jax.shard_map(
        shards, mesh=mesh, in_specs=placed, out_specs=P("dp", "expert", None), check_vma=False
    )
```

```python
import jax
import jax.numpy as jnp
from jax import lax
from jax.experimental import pallas as pl
from jax.experimental.pallas import tpu as pltpu
from jax.sharding import PartitionSpec as P

EXAMPLES = 8
MATES = 4
LANES = 128
BF16 = jnp.bfloat16
F32 = jnp.float32


def iota(shape, axis):
    return lax.broadcasted_iota(jnp.int32, shape, axis)


def build(sources, cap, routes_at, weights_at, ids_at, loss_at, grad_at, *refs):
    alone, blocks = refs[0], refs[1 : sources + 1]
    routes, weights, ids, loss, grad, sems = refs[sources + 1 :]
    fetches = [
        pltpu.make_async_copy(source, target, sems.at[i])
        for i, (source, target) in enumerate(
            [
                (routes_at, routes),
                (ids_at, ids),
                (loss_at, loss),
                (weights_at, weights),
                (grad_at, grad),
            ]
        )
    ]
    for fetch in fetches:
        fetch.start()
    me = lax.axis_index("expert")
    tokens, width = grad.shape
    before = (iota((tokens, tokens), 0) < iota((tokens, tokens), 1)).astype(F32).astype(BF16)
    slot = iota((cap, tokens), 0).astype(F32)
    fetches[0].wait()
    matches = [routes[...] == lax.rem(me + (sources - k), sources) for k in range(sources)]
    hits = [jnp.sum(jnp.where(m, 1.0, 0.0), axis=0, keepdims=True) for m in matches]
    blank = -(-sources // 8) * 8 - sources
    routed = jnp.concatenate(hits + [jnp.zeros((1, tokens), F32)] * blank, axis=0)
    ranking = jnp.dot(routed.astype(BF16), before, preferred_element_type=F32)
    for fetch in fetches[1:4]:
        fetch.wait()
    token_ids = ids[...]
    token_weight = jnp.zeros((1, tokens), F32)
    for x in range(EXAMPLES):
        token_weight = jnp.where(token_ids == x, loss[0, x], token_weight)
    token_code = (token_ids + 1).astype(F32)
    ready = []
    for k in range(sources):
        scale = jnp.sum(jnp.where(matches[k], weights[...], 0.0), axis=0, keepdims=True)
        scale = scale * token_weight
        placed = jnp.where(ranking[k : k + 1] == slot, hits[k], 0.0)
        slot_scale = jnp.sum(placed * scale, axis=1, keepdims=True)
        code = jnp.sum(placed * token_code, axis=1, keepdims=True)
        ready.append((placed.astype(BF16), slot_scale, code))
    fetches[4].wait()
    for k in range(sources):
        placed, slot_scale, code = ready[k]
        rows = jnp.dot(placed, grad[...], preferred_element_type=F32)
        rows = (rows * slot_scale).astype(BF16)
        blocks[k][:, :width] = rows
        if k == 0:
            alone[...] = rows
        blocks[k][:, width:] = jnp.broadcast_to(code, (cap, LANES)).astype(BF16)


def stage(sources, n_dp, pad, block, hidden, own, left, *cuts):
    own[...] = block[...]
    me, rank = lax.axis_index("expert"), lax.axis_index("dp")
    spread = n_dp // MATES
    cap, ff = hidden.shape[1:]
    rows = ff // n_dp
    high, low = rank // MATES, lax.rem(rank, MATES)
    column = iota((1, spread * pad), 1)
    wanted = jnp.full((1, spread * pad), -2 * ff, jnp.int32)
    for p in range(spread):
        inside = (column >= p * pad) & (column < p * pad + rows)
        wanted = jnp.where(inside, (high ^ p) * (MATES * rows) + column - p * pad, wanted)
    unit = iota((ff, spread * pad), 0)
    acts = [hidden[lax.rem(me + j, sources)] for j in range(sources)]
    acts = jnp.concatenate(acts, axis=0)
    left[...] = lax.dot_general(
        acts, acts, (((1,), (1,)), ((), ())), preferred_element_type=F32
    )
    for k in range(MATES):
        pick = jnp.where(unit == wanted + (low ^ k) * rows, 1.0, 0.0).astype(BF16)
        units = jnp.dot(acts, pick, preferred_element_type=F32).astype(BF16)
        for j in range(sources):
            at = slice(j * spread * pad, (j + 1) * spread * pad)
            cuts[k][:, at] = units[j * cap : (j + 1) * cap]


def chosen(codes):
    codes = jnp.broadcast_to(codes.astype(F32), (codes.shape[0], LANES))
    lane = iota(codes.shape, 1).astype(F32)
    return (codes == lane) & (codes > 0.0)


def norms(sources, left, own, *refs):
    takes, squares = refs[: sources - 1], refs[-1]
    width = own.shape[1] - LANES
    blocks = jnp.concatenate([own[...]] + [t[...] for t in takes], axis=0)
    cot = blocks[:, :width]
    member = jnp.where(chosen(blocks[:, width : width + 1]), 1.0, 0.0)
    last = (((1,), (1,)), ((), ()))
    right = lax.dot_general(cot, cot, last, preferred_element_type=F32)
    one_hot = member.astype(BF16)
    alike = lax.dot_general(one_hot, one_hot, last, preferred_element_type=F32)
    per_slot = jnp.sum(left[...] * right * alike, axis=1, keepdims=True)
    squares[...] = jnp.sum(per_slot * member, axis=0, keepdims=True)


def diagonal(cap):
    return iota((cap, LANES), 0) == iota((cap, LANES), 1)


def pass_on(rows, pad, across, own, squares, cut, *refs):
    takes, rest = refs[:-1], refs[-1]
    cap, width = own.shape[0], own.shape[1] - LANES
    value = jnp.where(diagonal(cap), squares[...], 0.0)
    value = jnp.sum(value, axis=1, keepdims=True)
    high = value.astype(BF16).astype(F32)
    middle = (value - high).astype(BF16).astype(F32)
    lane = iota(cut.shape, 1)
    tail = cut[...].astype(F32)
    for at, column in (
        (pad + rows, own[:, width : width + 1].astype(F32)),
        (rows + 1, high),
        (rows + 2, middle),
        (rows + 3, value - high - middle),
    ):
        tail = jnp.where(lane == at, column, tail)
    for j, take in enumerate(takes):
        part = slice(j * cap, (j + 1) * cap)
        rest[part, :width] = take[:, :width]
        code = take[:, width : width + 1].astype(F32)
        rest[part, width:] = jnp.where(lane == rows, code, 0.0 if j else tail).astype(BF16)


def pack(sources, count, rows, pad, own, rest, across, rest_across, *refs):
    near, far, out = refs[:sources], refs[sources:-1], refs[-1]
    cap, width = own.shape[0], own.shape[1] - LANES
    first = width + rows
    three = rest_across[:cap, first + 1 : first + 4].astype(F32)
    three = three[:, 0:1] + three[:, 1:2] + three[:, 2:3]
    three = jnp.where(diagonal(cap), three, 0.0)
    totals = [near[0][...], jnp.sum(three, axis=0, keepdims=True)]
    for k in range(1, sources):
        totals = [totals[0] + near[k][...], totals[1] + far[k - 1][...]]
    clips = [1.0 / jnp.maximum(jnp.sqrt(total / count), 1.0) for total in totals]
    at = 0
    for block, codes, clip in (
        (own, own[:, width : width + 1], clips[0]),
        (rest, rest[:, first : first + 1], clips[0]),
        (across, rest_across[:cap, first + pad : first + pad + 1], clips[1]),
        (rest_across, rest_across[:, first : first + 1], clips[1]),
    ):
        mine = chosen(codes)
        weight = jnp.sum(jnp.where(mine, clip, 0.0), axis=1, keepdims=True) / EXAMPLES
        scaled = (weight * block[:, :width].astype(F32)).astype(BF16)
        out[at : at + mine.shape[0]] = scaled
        at += mine.shape[0]


def multiply(cuts, cots, units):
    at, cap, across = 0, cuts[0].shape[0], units.shape[1]
    for cut in cuts:
        for j in range(cut.shape[1] // across):
            units[at : at + cap] = cut[:, j * across : (j + 1) * across]
            at += cap
    return lax.dot_general(
        units[...], cots[...], (((0,), (0,)), ((), ())), preferred_element_type=F32
    )


def near_product(cut, rest_across, cots, out, units):
    across = rest_across.at[: cut.shape[0], cots.shape[1] :]
    out[...] = multiply([cut, across], cots, units)


def product(rows, pad, start, cut, across, cots, keep, *refs):
    leave, units = refs[:-1], refs[-1]
    width = cots.shape[1]
    pieces = width // LANES
    part = start[...] + multiply([cut, across], cots, units)
    leave = list(leave)
    for p in range(part.shape[0] // pad):
        values = part[p * pad : p * pad + rows]
        if p:
            most = jnp.max(jnp.max(jnp.abs(values), axis=0, keepdims=True), axis=1, keepdims=True)
            exponent = jnp.ceil(jnp.log2(jnp.maximum(most, 2.0**-100)))
            values = values * jnp.exp2(-exponent)
        done = 0
        for out in [keep] if p == 0 else [leave.pop(0) for _ in range(1 if p == 1 else 2)]:
            held = out.shape[0] if p == 0 else out.shape[0] - 8
            count = held // pieces
            for j in range(pieces):
                out[pl.ds(j, count, stride=pieces), :] = values[
                    done : done + count, j * LANES : (j + 1) * LANES
                ]
            if p:
                out[held:] = jnp.broadcast_to(exponent, (8, LANES))
            done += count


def call(body, outs, args, fetched=(), scratch=(), limit=32, flops=1):
    vmem = pl.BlockSpec(memory_space=pltpu.VMEM)
    anywhere = pl.BlockSpec(memory_space=pl.ANY)
    return pl.pallas_call(
        body,
        out_shape=tuple(outs),
        in_specs=[anywhere if i in fetched else vmem for i in range(len(args))],
        out_specs=tuple([vmem] * len(outs)),
        scratch_shapes=list(scratch),
        compiler_params=pltpu.CompilerParams(vmem_limit_bytes=limit * 1024 * 1024),
        cost_estimate=pl.CostEstimate(flops=flops, bytes_accessed=1, transcendentals=0),
    )(*args)


def shards(grad_out, routes, route_weight, example_ids, example_weight, hidden):
    sources = lax.axis_size("expert")
    n_dp = lax.axis_size("dp")
    spread = n_dp // MATES
    tokens, width = grad_out.shape
    top = routes.shape[1]
    cap, ff = hidden.shape[3], hidden.shape[4]
    rows = ff // n_dp
    pad = -(-(rows + 4) // 16) * 16
    while spread * pad * sources % LANES:
        pad += 16
    across = spread * pad
    slots = sources * cap
    acts = hidden.reshape(sources, cap, ff)
    shape = jax.ShapeDtypeStruct

    def over_experts(array, k):
        return lax.ppermute(
            array, "expert", [(s, (s - k) % sources) for s in range(sources)]
        )

    def over_dp(array, k):
        return lax.ppermute(array, "dp", [(i, i ^ k) for i in range(n_dp)])

    def over_both(array, k):
        where = [(i, e) for i in range(n_dp) for e in range(sources)]
        pairs = [
            (i * sources + e, (i ^ 2) * sources + (e - k) % sources) for i, e in where
        ]
        return lax.ppermute(array, ("dp", "expert"), pairs)

    alone, block, *gives = call(
        lambda *refs: build(sources, cap, *refs),
        [shape((cap, width), BF16)] + [shape((cap, width + LANES), BF16)] * sources,
        (routes.T, route_weight.T, example_ids, example_weight, grad_out),
        fetched=range(5),
        limit=60,
        scratch=(
            pltpu.VMEM((top, tokens), jnp.int32),
            pltpu.VMEM((top, tokens), F32),
            pltpu.VMEM((1, tokens), jnp.int32),
            pltpu.SMEM((1, EXAMPLES), F32),
            pltpu.VMEM((tokens, width), BF16),
            pltpu.SemaphoreType.DMA((5,)),
        ),
    )
    takes = [over_experts(g, k + 1) for k, g in enumerate(gives)]
    block_across = over_dp(alone, 2)
    own, left, *cuts = call(
        lambda *refs: stage(sources, n_dp, pad, *refs),
        [shape((cap, width + LANES), BF16), shape((slots, slots), F32)]
        + [shape((cap, sources * across), BF16)] * MATES,
        (block, acts),
        flops=1,
    )
    (squares,) = call(
        lambda *refs: norms(sources, *refs),
        [shape((1, LANES), F32)],
        (left, own, *takes),
        flops=1 << 32,
    )
    (rest,) = call(
        lambda *refs: pass_on(rows, pad, *refs),
        [shape((slots - cap, width + sources * across), BF16)],
        (block_across, own, squares, cuts[2], *takes),
        fetched=(0,),
    )
    rest_across = over_dp(rest, 2)
    near_squares = [squares] + [over_experts(squares, k) for k in range(1, sources)]
    far_squares = [over_both(squares, k) for k in range(1, sources)]
    (cots,) = call(
        lambda *refs: pack(sources, ff * width, rows, pad, *refs),
        [shape((2 * slots, width), BF16)],
        (own, rest, block_across, rest_across, *near_squares, *far_squares),
    )
    other_cots = over_dp(cots, 1)
    (start,) = call(
        near_product,
        [shape((across, width), F32)],
        (cuts[0], rest_across, cots),
        scratch=(pltpu.VMEM((2 * slots, across), BF16),),
        flops=1 << 32,
    )

    held = rows * (width // LANES)
    pieces = width // LANES
    upper = rows // 2 * pieces
    lower = held - upper
    sizes = [held, held + 8] + [upper + 8, lower + 8] * (spread - 2)
    part, *leave = call(
        lambda *refs: product(rows, pad, *refs),
        [shape((size, LANES), F32) for size in sizes],
        (start, over_dp(cuts[1], 1), over_dp(cuts[3], 3), other_cots),
        scratch=(pltpu.VMEM((2 * slots, across), BF16),),
    )
    uppers, lowers = [None, None] + leave[1::2], [None, None] + leave[2::2]

    def over_spread(array, p):
        return over_dp(array.astype(jnp.float16), p * MATES).astype(F32)

    def value(array):
        return array[:-8] * jnp.exp2(array[-8:-7])

    sums = {}
    for p in range(2, spread, 2):
        got = over_spread(lowers[p + 1], 1)
        top = jnp.maximum(got[-8:-7], lowers[p][-8:-7])
        added = got[:-8] * jnp.exp2(got[-8:-7] - top)
        added = added + lowers[p][:-8] * jnp.exp2(lowers[p][-8:-7] - top)
        sums[p] = jnp.concatenate([added, jnp.broadcast_to(top, (8, LANES))], axis=0)
    come = sum(value(over_spread(uppers[p], p)) for p in range(spread - 1, 1, -1))
    come_lower = sum(value(over_spread(sums[p], p)) for p in sums)
    come = jnp.concatenate([come, come_lower], axis=0)
    part = part + value(over_spread(leave[0], 1)) + come
    return part.reshape(rows, 1, width)


def solution(mesh):
    placed = (
        P(("dp", "expert"), None),
        P(("dp", "expert"), None),
        P(("dp", "expert"), None),
        P("dp", "expert"),
        P("dp", None),
        P("dp", "expert", None, None, None),
    )
    return jax.shard_map(
        shards, mesh=mesh, in_specs=placed, out_specs=P("dp", "expert", None), check_vma=False
    )
```

```python
import jax
import jax.numpy as jnp
from jax import lax
from jax.experimental import pallas as pl
from jax.experimental.pallas import tpu as pltpu
from jax.sharding import PartitionSpec as P

EXAMPLES = 8
MATES = 4
LANES = 128
BF16 = jnp.bfloat16
F32 = jnp.float32


def iota(shape, axis):
    return lax.broadcasted_iota(jnp.int32, shape, axis)


def build(sources, cap, routes_at, weights_at, ids_at, loss_at, grad_at, *refs):
    blocks = refs[:sources]
    routes, weights, ids, loss, grad, sems = refs[sources:]
    fetches = [
        pltpu.make_async_copy(source, target, sems.at[i])
        for i, (source, target) in enumerate(
            [
                (routes_at, routes),
                (ids_at, ids),
                (loss_at, loss),
                (weights_at, weights),
                (grad_at, grad),
            ]
        )
    ]
    for fetch in fetches:
        fetch.start()
    me = lax.axis_index("expert")
    tokens, width = grad.shape
    before = (iota((tokens, tokens), 0) < iota((tokens, tokens), 1)).astype(F32).astype(BF16)
    slot = iota((cap, tokens), 0).astype(F32)
    fetches[0].wait()
    matches = [routes[...] == lax.rem(me + (sources - k), sources) for k in range(sources)]
    hits = [jnp.sum(jnp.where(m, 1.0, 0.0), axis=0, keepdims=True) for m in matches]
    blank = -(-sources // 8) * 8 - sources
    routed = jnp.concatenate(hits + [jnp.zeros((1, tokens), F32)] * blank, axis=0)
    ranking = jnp.dot(routed.astype(BF16), before, preferred_element_type=F32)
    for fetch in fetches[1:4]:
        fetch.wait()
    token_ids = ids[...]
    token_weight = jnp.zeros((1, tokens), F32)
    for x in range(EXAMPLES):
        token_weight = jnp.where(token_ids == x, loss[0, x], token_weight)
    token_code = (token_ids + 1).astype(F32)
    ready = []
    for k in range(sources):
        scale = jnp.sum(jnp.where(matches[k], weights[...], 0.0), axis=0, keepdims=True)
        scale = scale * token_weight
        placed = jnp.where(ranking[k : k + 1] == slot, hits[k], 0.0)
        slot_scale = jnp.sum(placed * scale, axis=1, keepdims=True)
        code = jnp.sum(placed * token_code, axis=1, keepdims=True)
        ready.append((placed.astype(BF16), slot_scale, code))
    fetches[4].wait()
    for k in range(sources):
        placed, slot_scale, code = ready[k]
        rows = jnp.dot(placed, grad[...], preferred_element_type=F32)
        rows = (rows * slot_scale).astype(BF16)
        blocks[k][:, :width] = rows
        blocks[k][:, width:] = jnp.broadcast_to(code, (cap, LANES)).astype(BF16)


def stage(sources, n_dp, pad, block, hidden, own, left, *cuts):
    own[...] = block[...]
    me, rank = lax.axis_index("expert"), lax.axis_index("dp")
    spread = n_dp // MATES
    cap, ff = hidden.shape[1:]
    rows = ff // n_dp
    high, low = rank // MATES, lax.rem(rank, MATES)
    column = iota((1, spread * pad), 1)
    wanted = jnp.full((1, spread * pad), -2 * ff, jnp.int32)
    for p in range(spread):
        inside = (column >= p * pad) & (column < p * pad + rows)
        wanted = jnp.where(inside, (high ^ p) * (MATES * rows) + column - p * pad, wanted)
    unit = iota((ff, spread * pad), 0)
    acts = [hidden[lax.rem(me + j, sources)] for j in range(sources)]
    acts = jnp.concatenate(acts, axis=0)
    left[...] = lax.dot_general(
        acts, acts, (((1,), (1,)), ((), ())), preferred_element_type=F32
    )
    for k in range(MATES):
        pick = jnp.where(unit == wanted + (low ^ k) * rows, 1.0, 0.0).astype(BF16)
        units = jnp.dot(acts, pick, preferred_element_type=F32).astype(BF16)
        for j in range(sources):
            at = slice(j * spread * pad, (j + 1) * spread * pad)
            cuts[k][:, at] = units[j * cap : (j + 1) * cap]


def chosen(codes):
    codes = jnp.broadcast_to(codes.astype(F32), (codes.shape[0], LANES))
    lane = iota(codes.shape, 1).astype(F32)
    return (codes == lane) & (codes > 0.0)


def norms(sources, left, own, *refs):
    takes, squares = refs[: sources - 1], refs[-1]
    width = own.shape[1] - LANES
    blocks = jnp.concatenate([own[...]] + [t[...] for t in takes], axis=0)
    cot = blocks[:, :width]
    member = jnp.where(chosen(blocks[:, width : width + 1]), 1.0, 0.0)
    last = (((1,), (1,)), ((), ()))
    right = lax.dot_general(cot, cot, last, preferred_element_type=F32)
    one_hot = member.astype(BF16)
    alike = lax.dot_general(one_hot, one_hot, last, preferred_element_type=F32)
    per_slot = jnp.sum(left[...] * right * alike, axis=1, keepdims=True)
    squares[...] = jnp.sum(per_slot * member, axis=0, keepdims=True)


def pass_on(across, squares, cut, *refs):
    takes, rest = refs[:-1], refs[-1]
    cap, wide = takes[0].shape
    half = LANES // 2
    for j, take in enumerate(takes):
        part = slice(j * cap, (j + 1) * cap)
        rest[part, :wide] = take[...]
        if j:
            rest[part, wide:] = jnp.zeros((cap, rest.shape[1] - wide), BF16)
    rest[:cap, wide:] = cut[...]
    value = jnp.broadcast_to(squares[...], (cap, LANES))
    high = value.astype(BF16).astype(F32)
    middle = (value - high).astype(BF16).astype(F32)
    low = value - high - middle
    row = iota((cap, LANES), 0)
    three = jnp.where(row == 0, high, jnp.where(row == 1, middle, low)).astype(BF16)
    rest[:cap, wide - half : wide] = three[:, :half]


def pack(sources, count, own, rest, across, rest_across, *refs):
    near, far, out = refs[:sources], refs[sources:-1], refs[-1]
    width = own.shape[1] - LANES
    half = LANES // 2
    three = rest_across[0:8, width + half : width + LANES].astype(F32)
    three = three[0:1] + three[1:2] + three[2:3]
    totals = [near[0][...], jnp.concatenate([three, jnp.zeros_like(three)], axis=1)]
    for k in range(1, sources):
        totals = [totals[0] + near[k][...], totals[1] + far[k - 1][...]]
    clips = [1.0 / jnp.maximum(jnp.sqrt(total / count), 1.0) for total in totals]
    at = 0
    for block, clip in ((own, clips[0]), (rest, clips[0]), (across, clips[1]), (rest_across, clips[1])):
        mine = chosen(block[:, width : width + 1])
        weight = jnp.sum(jnp.where(mine, clip, 0.0), axis=1, keepdims=True) / EXAMPLES
        scaled = (weight * block[:, :width].astype(F32)).astype(BF16)
        out[at : at + mine.shape[0]] = scaled
        at += mine.shape[0]


def multiply(cuts, cots, units):
    at, cap, across = 0, cuts[0].shape[0], units.shape[1]
    for cut in cuts:
        for j in range(cut.shape[1] // across):
            units[at : at + cap] = cut[:, j * across : (j + 1) * across]
            at += cap
    return lax.dot_general(
        units[...], cots[...], (((0,), (0,)), ((), ())), preferred_element_type=F32
    )


def near_product(cut, rest_across, cots, out, units):
    first = cots.shape[1] + LANES
    cap = cut.shape[0]
    across = rest_across.at[:cap, first : first + cut.shape[1]]
    out[...] = multiply([cut, across], cots, units)


def product(rows, pad, start, cut, across, cots, keep, *refs):
    leave, units = refs[:-1], refs[-1]
    width = cots.shape[1]
    pieces = width // LANES
    part = start[...] + multiply([cut, across], cots, units)
    leave = list(leave)
    for p in range(part.shape[0] // pad):
        values = part[p * pad : p * pad + rows]
        if p:
            most = jnp.max(jnp.max(jnp.abs(values), axis=0, keepdims=True), axis=1, keepdims=True)
            exponent = jnp.ceil(jnp.log2(jnp.maximum(most, 2.0**-100)))
            values = values * jnp.exp2(-exponent)
        done = 0
        for out in [keep] if p == 0 else [leave.pop(0) for _ in range(1 if p == 1 else 2)]:
            held = out.shape[0] if p == 0 else out.shape[0] - 8
            count = held // pieces
            for j in range(pieces):
                out[pl.ds(j, count, stride=pieces), :] = values[
                    done : done + count, j * LANES : (j + 1) * LANES
                ]
            if p:
                out[held:] = jnp.broadcast_to(exponent, (8, LANES))
            done += count


def call(body, outs, args, fetched=(), scratch=(), limit=32, flops=1):
    vmem = pl.BlockSpec(memory_space=pltpu.VMEM)
    anywhere = pl.BlockSpec(memory_space=pl.ANY)
    return pl.pallas_call(
        body,
        out_shape=tuple(outs),
        in_specs=[anywhere if i in fetched else vmem for i in range(len(args))],
        out_specs=tuple([vmem] * len(outs)),
        scratch_shapes=list(scratch),
        compiler_params=pltpu.CompilerParams(vmem_limit_bytes=limit * 1024 * 1024),
        cost_estimate=pl.CostEstimate(flops=flops, bytes_accessed=1, transcendentals=0),
    )(*args)


def shards(grad_out, routes, route_weight, example_ids, example_weight, hidden):
    sources = lax.axis_size("expert")
    n_dp = lax.axis_size("dp")
    spread = n_dp // MATES
    tokens, width = grad_out.shape
    top = routes.shape[1]
    cap, ff = hidden.shape[3], hidden.shape[4]
    rows = ff // n_dp
    pad = -(-(rows + 1) // 16) * 16
    while spread * pad * sources % LANES:
        pad += 16
    across = spread * pad
    slots = sources * cap
    acts = hidden.reshape(sources, cap, ff)
    shape = jax.ShapeDtypeStruct

    def over_experts(array, k):
        return lax.ppermute(
            array, "expert", [(s, (s - k) % sources) for s in range(sources)]
        )

    def over_dp(array, k):
        return lax.ppermute(array, "dp", [(i, i ^ k) for i in range(n_dp)])

    def over_both(array, k):
        where = [(i, e) for i in range(n_dp) for e in range(sources)]
        pairs = [
            (i * sources + e, (i ^ 2) * sources + (e - k) % sources) for i, e in where
        ]
        return lax.ppermute(array, ("dp", "expert"), pairs)

    block, *gives = call(
        lambda *refs: build(sources, cap, *refs),
        [shape((cap, width + LANES), BF16)] * sources,
        (routes.T, route_weight.T, example_ids, example_weight, grad_out),
        fetched=range(5),
        limit=60,
        scratch=(
            pltpu.VMEM((top, tokens), jnp.int32),
            pltpu.VMEM((top, tokens), F32),
            pltpu.VMEM((1, tokens), jnp.int32),
            pltpu.SMEM((1, EXAMPLES), F32),
            pltpu.VMEM((tokens, width), BF16),
            pltpu.SemaphoreType.DMA((5,)),
        ),
    )
    takes = [over_experts(g, k + 1) for k, g in enumerate(gives)]
    block_across = over_dp(block, 2)
    own, left, *cuts = call(
        lambda *refs: stage(sources, n_dp, pad, *refs),
        [shape((cap, width + LANES), BF16), shape((slots, slots), F32)]
        + [shape((cap, sources * across), BF16)] * MATES,
        (block, acts),
        flops=1 << 32,
    )
    (squares,) = call(
        lambda *refs: norms(sources, *refs),
        [shape((1, LANES), F32)],
        (left, own, *takes),
        flops=1 << 32,
    )
    (rest,) = call(
        pass_on,
        [shape((slots - cap, width + LANES + sources * across), BF16)],
        (block_across, squares, cuts[2], *takes),
        fetched=(0,),
    )
    rest_across = over_dp(rest, 2)
    near_squares = [squares] + [over_experts(squares, k) for k in range(1, sources)]
    far_squares = [over_both(squares, k) for k in range(1, sources)]
    (cots,) = call(
        lambda *refs: pack(sources, ff * width, *refs),
        [shape((2 * slots, width), BF16)],
        (own, rest, block_across, rest_across, *near_squares, *far_squares),
    )
    other_cots = over_dp(cots, 1)
    (start,) = call(
        near_product,
        [shape((across, width), F32)],
        (cuts[0], rest_across, cots),
        scratch=(pltpu.VMEM((2 * slots, across), BF16),),
        flops=1 << 32,
    )

    held = rows * (width // LANES)
    pieces = width // LANES
    upper = rows // 2 * pieces
    lower = held - upper
    sizes = [held, held + 8] + [upper + 8, lower + 8] * (spread - 2)
    part, *leave = call(
        lambda *refs: product(rows, pad, *refs),
        [shape((size, LANES), F32) for size in sizes],
        (start, over_dp(cuts[1], 1), over_dp(cuts[3], 3), other_cots),
        scratch=(pltpu.VMEM((2 * slots, across), BF16),),
    )
    uppers, lowers = [None, None] + leave[1::2], [None, None] + leave[2::2]

    def over_spread(array, p):
        return over_dp(array.astype(jnp.float16), p * MATES)

    def value(array):
        return array[:-8] * jnp.exp2(array[-8:-7])

    sums = {}
    for p in range(2, spread, 2):
        got = over_spread(lowers[p + 1], 1).astype(F32)
        top = jnp.maximum(got[-8:-7], lowers[p][-8:-7])
        added = got[:-8] * jnp.exp2(got[-8:-7] - top)
        added = added + lowers[p][:-8] * jnp.exp2(lowers[p][-8:-7] - top)
        sums[p] = jnp.concatenate([added, jnp.broadcast_to(top, (8, LANES))], axis=0)
    far = list(range(spread - 1, 1, -1))
    come = [over_spread(leave[0], 1)] + [over_spread(sums[p], p) for p in sums]
    come += [over_spread(uppers[p], p) for p in far]
    whole, *halves = [value(array.astype(F32)) for array in lax.optimization_barrier(come)]
    lower_sum, upper_sum = sum(halves[: len(sums)]), sum(halves[len(sums) :])
    part = part + whole + jnp.concatenate([upper_sum, lower_sum], axis=0)
    return part.reshape(rows, 1, width)


def solution(mesh):
    placed = (
        P(("dp", "expert"), None),
        P(("dp", "expert"), None),
        P(("dp", "expert"), None),
        P("dp", "expert"),
        P("dp", None),
        P("dp", "expert", None, None, None),
    )
    return jax.shard_map(
        shards, mesh=mesh, in_specs=placed, out_specs=P("dp", "expert", None), check_vma=False
    )
```
